128 devices in a mesh: grp: 4 (over x), dev: 32 (over z, y, core).
Axes of the slice: x: 4, y: 4, z: 4, core: 2. Of those that a mesh axis runs over, the one named last changes fastest.
Arguments:
- populations: float32 [19, 128, 8, 4096], P(None, 'grp', None, 'dev'), as said below
- fill: float32 [128, 8, 4096], P('grp', None, 'dev'), may hold values from 0 to 1, as said below
- flags: int32 [128, 8, 4096], P('grp', None, 'dev'), may hold values from 0 to 2, as said below
- specific_energy_grid: float32 [128, 8, 4096], P(('grp', 'dev')), may hold values from 0 to 2.5
Outputs:
- populations_out: float32 [19, 128, 8, 4096], P(None, 'grp', None, 'dev')
- fill_out: float32 [128, 8, 4096], P('grp', None, 'dev')
- enthalpy_out: float32 [128, 8, 4096], P(('grp', 'dev'))
The draws below stay inside these ranges and needn't reach their ends.
Inputs may be any that keep to these rules, and one draw needn't show every extreme that they name: flags is 0 on gas, 1 on interface, 2 on liquid cells. fill is exactly 0 on gas cells, exactly 1 on liquid cells, and between 0.02 and 0.98 on interface cells. `populations`: every population is positive, within 0.5 and 1.5 times its lattice weight.
All inputs are finite; a program needn't handle non-finite values.
Results may differ from the reference program's by a relative error of at most 0.0003.
Values sent between devices are 32-bit elements; how exact they have to be, the bound alone decides.
A program may use at most 128 MiB of HBM per device.

```python
import jax
import jax.numpy as jnp
from jax import lax

NX = 128
NY = 8
NZ = 4096


def flag_field(key):
    key_jitter = jax.random.fold_in(key, 101)
    key_thick = jax.random.fold_in(key, 102)
    key_drops = jax.random.fold_in(key, 103)
    period_x = max(NX // 2, 2)
    period_y = max(NY // 2, 2)
    index_x = jnp.arange(NX, dtype=jnp.int32)
    index_y = jnp.arange(NY, dtype=jnp.int32)
    wave_x = jnp.abs(2 * (index_x % period_x) - period_x)
    wave_y = jnp.abs(2 * (index_y % period_y) - period_y)
    height = NZ // 4 + NZ // 4 * wave_x[:, None] // period_x + NZ // 8 * wave_y[None, :] // period_y + jax.random.randint(key_jitter, (NX, NY), 0, 3)
    thick = jax.random.randint(key_thick, (NX, NY), 1, 3)
    depth = jnp.arange(NZ, dtype=jnp.int32)[None, None, :]
    below = depth < height[:, :, None]
    skin = (depth >= height[:, :, None]) & (depth < (height + thick)[:, :, None])
    drops = jax.random.randint(key_drops, (NX, NY, NZ), 0, 50) == 0
    kinds = jnp.where(below, 2, jnp.where(skin | drops, 1, 0))
    return kinds.astype(jnp.int32)


def draw_flags(key, part):
    return flag_field(key).astype(jnp.int32)


def draw_fill(key, part):
    kinds = flag_field(key)
    key = jax.random.fold_in(key, 11)
    level = jax.random.uniform(key, (NX, NY, NZ), jnp.float32)
    level = 0.02 + 0.96 * level
    return jnp.where(kinds == 2, 1.0, jnp.where(kinds == 0, 0.0, level)).astype(jnp.float32)


def draw_populations(key, part):
    key = jax.random.fold_in(key, 23)
    weights = jnp.array((1.0 / 3.0,) + (1.0 / 18.0,) * 6 + (1.0 / 36.0,) * 12, jnp.float32).reshape(19, 1, 1, 1)
    noise = jax.random.uniform(key, (19, NX, NY, NZ), jnp.float32, 0.6, 1.4)
    return (weights * noise).astype(jnp.float32)


def level_of(own_key, dims, split, low, high):
    loudness = 1.0
    for axis_at, blocks in split:
        steps = jax.random.uniform(jax.random.fold_in(jax.random.fold_in(own_key, 6), axis_at), (blocks,), jnp.float32, low / len(split), high / len(split))
        loudness = loudness * jnp.repeat(jnp.exp(steps), dims[axis_at] // blocks).reshape((-1,) + (1,) * (len(dims) - 1 - axis_at))
    return loudness


def setup_inputs(seed: int = 0) -> dict:
    seeds = jax.random.split(jax.random.key(seed), 5)
    populations = draw_populations(jax.random.fold_in(seeds[4], 71), 0)
    fill = draw_fill(jax.random.fold_in(seeds[4], 71), 0)
    flags = draw_flags(jax.random.fold_in(seeds[4], 71), 0)
    specific_energy_grid = jnp.clip(2.5 * jax.random.uniform(seeds[3], (NX, NY, NZ), jnp.float32) ** level_of(seeds[3], (NX, NY, NZ), ((0, 128),), -0.2, 0.2), 0.0, 2.5)
    return {"populations": populations, "fill": fill, "flags": flags, "specific_energy_grid": specific_energy_grid}


VELOCITIES = ((0, 0, 0), (1, 0, 0), (-1, 0, 0), (0, 1, 0), (0, -1, 0), (0, 0, 1), (0, 0, -1),
              (1, 1, 0), (-1, -1, 0), (1, -1, 0), (-1, 1, 0), (1, 0, 1), (-1, 0, -1),
              (1, 0, -1), (-1, 0, 1), (0, 1, 1), (0, -1, -1), (0, 1, -1), (0, -1, 1))
WEIGHTS = (1.0 / 3.0,) + (1.0 / 18.0,) * 6 + (1.0 / 36.0,) * 12
RELAX_TIME = 0.8
GRAVITY = -0.002
STEP_TIME = 0.2


def opposite(direction):
    if direction == 0:
        return 0
    return direction + 1 if direction % 2 == 1 else direction - 1


def equilibrium(direction, density, vel_x, vel_y, vel_z, squared):
    cx, cy, cz = VELOCITIES[direction]
    along = cx * vel_x + cy * vel_y + cz * vel_z
    return WEIGHTS[direction] * density * (1.0 + 3.0 * along + 4.5 * along * along - 1.5 * squared)


def velocity_of(pops, density):
    table = jnp.array(VELOCITIES, jnp.float32).T
    moment = jnp.einsum("aq,qxyz->axyz", table, pops, precision=lax.Precision.HIGHEST)
    return moment / density[None]


def fluid_update(pops, fill, flags, padded):
    gas = flags == 0
    liquid = flags == 2
    size_x, size_y, size_z = fill.shape
    density_old = jnp.where(gas, 1.0, jnp.sum(pops, axis=0))
    old_vel = velocity_of(pops, density_old)
    old_sq = old_vel[0] ** 2 + old_vel[1] ** 2 + old_vel[2] ** 2
    read = [pops[0]]
    exchange = jnp.zeros_like(fill)
    for direction in range(1, 19):
        cx, cy, cz = VELOCITIES[direction]
        back = opposite(direction)
        window = (slice(1 - cx, 1 - cx + size_x), slice(1 - cy, 1 - cy + size_y), slice(1 - cz, 1 - cz + size_z))
        incoming = padded[direction][window]
        beside = padded[19][window]
        empty = beside == 0.0
        rebuilt = (equilibrium(direction, 1.0, old_vel[0], old_vel[1], old_vel[2], old_sq)
                   + equilibrium(back, 1.0, old_vel[0], old_vel[1], old_vel[2], old_sq) - pops[back])
        read.append(jnp.where(empty, rebuilt, incoming))
        exchange = exchange + jnp.where(empty, 0.0, 0.5 * (fill + beside) * (incoming - pops[back]))
    moved = jnp.stack(read)
    density = jnp.where(gas, 1.0, jnp.sum(moved, axis=0))
    velocity = velocity_of(moved, density)
    forced_z = velocity[2] + RELAX_TIME * GRAVITY
    forced_sq = velocity[0] ** 2 + velocity[1] ** 2 + forced_z ** 2
    target = jnp.stack([equilibrium(d, density, velocity[0], velocity[1], forced_z, forced_sq) for d in range(19)])
    relaxed = moved - (moved - target) / RELAX_TIME
    relaxed = jnp.where(gas[None], 0.0, relaxed)
    mass = fill * density_old + exchange
    fill_new = jnp.where(liquid, 1.0, jnp.where(gas, 0.0, jnp.clip(mass / density, 0.01, 1.0)))
    return relaxed, fill_new, velocity


def site_warmth_level(stored_scalar_item):
    return jnp.minimum(stored_scalar_item, 1.0) + jnp.maximum(stored_scalar_item - 1.5, 0.0)


def heat_update(specific_energy_grid, fill, velocity, padded):
    shape = specific_energy_grid.shape
    thermal_conduction_factor = 0.02 + 0.1 * fill
    own_site_warmth = site_warmth_level(specific_energy_grid)
    spreading_flux_part = jnp.zeros_like(specific_energy_grid)
    advection = jnp.zeros_like(specific_energy_grid)
    for axis in range(3):
        for sign in (-1, 1):
            offset = [1, 1, 1]
            offset[axis] = 1 + sign
            window = tuple(slice(offset[k], offset[k] + shape[k]) for k in range(3))
            neighbor_enthalpy_share = padded[0][window]
            neighbor_liquid_share = padded[1][window]
            spreading_flux_part = spreading_flux_part + 0.5 * (thermal_conduction_factor + 0.02 + 0.1 * neighbor_liquid_share) * (site_warmth_level(neighbor_enthalpy_share) - own_site_warmth)
            if sign < 0:
                advection = advection + jnp.maximum(velocity[axis], 0.0) * (specific_energy_grid - neighbor_enthalpy_share)
            else:
                advection = advection + jnp.minimum(velocity[axis], 0.0) * (neighbor_enthalpy_share - specific_energy_grid)
    return specific_energy_grid + STEP_TIME * (spreading_flux_part - advection)


def reference(populations, fill, flags, specific_energy_grid):
    pops = populations
    for step in range(2):
        stacked = jnp.concatenate([pops, fill[None]], axis=0)
        padded = jnp.pad(stacked, ((0, 0), (1, 1), (1, 1), (1, 1)))
        pops, fill, velocity = fluid_update(pops, fill, flags, padded)
    pair = jnp.stack([specific_energy_grid, fill])
    padded = jnp.pad(pair, ((0, 0), (1, 1), (1, 1), (1, 1)))
    heat = heat_update(specific_energy_grid, fill, velocity, padded)
    return pops, fill, heat
```

```python
import functools

import jax
import jax.numpy as jnp
from jax import lax
from jax.experimental import pallas as pl
from jax.experimental.pallas import tpu as pltpu
from jax.sharding import PartitionSpec as P

MESH = pl.DeviceIdType.MESH
F32 = jnp.float32
VELOCITIES = (
    (0, 0, 0),
    (1, 0, 0),
    (-1, 0, 0),
    (0, 1, 0),
    (0, -1, 0),
    (0, 0, 1),
    (0, 0, -1),
    (1, 1, 0),
    (-1, -1, 0),
    (1, -1, 0),
    (-1, 1, 0),
    (1, 0, 1),
    (-1, 0, -1),
    (1, 0, -1),
    (-1, 0, 1),
    (0, 1, 1),
    (0, -1, -1),
    (0, 1, -1),
    (0, -1, 1),
)
WEIGHTS = (1.0 / 3.0,) + (1.0 / 18.0,) * 6 + (1.0 / 36.0,) * 12
RELAX_TIME = 0.8
GRAVITY = -0.002
STEP_TIME = 0.2

NG, ND, NP, NY, NL = 4, 32, 32, 8, 128
FLAT = (1, 2, 3, 4, 7, 8, 9, 10)
UP = (5, 15, 18, 11, 14)
DOWN = (6, 16, 17, 13, 12)
CROSS = UP + DOWN
EAST = (1, 7, 9, 11, 13)
WEST = (2, 8, 10, 12, 14)
Z_PAIRS = (5, 11, 13, 15, 17)


def opposite(q):
    return q + 1 if q % 2 == 1 else q - 1


def lane_iota():
    return lax.broadcasted_iota(jnp.int32, (NY, NL), 1)


def shift_rows(x, cy):
    return x if cy == 0 else pltpu.roll(x, cy % NY, 0)


def spread(x, lane):
    return jnp.broadcast_to(x[:, lane : lane + 1], (NY, NL))


def moments(d, s):
    out = []
    for axis in range(3):
        total = None
        for q, diff in d.items():
            c = VELOCITIES[q][axis]
            if c == 0:
                continue
            if total is None:
                total = diff if c > 0 else -diff
            else:
                total = total + diff if c > 0 else total - diff
        out.append(total)
    return out, sum(s.values())


def pack_columns(tops, bottoms, fill, p, acc, lane):
    spot = lane & 31
    here = spot == p
    east = lane == ((p + 1) & 31)
    west = lane == 32 + ((p + 31) & 31)
    out = []
    for side, (cols, edge) in enumerate(((tops, NL - 1), (bottoms, 0))):
        a, b = acc[2 * side], acc[2 * side + 1]
        v = spread(cols[0], edge)
        v = jnp.where(lane >= 32, spread(cols[1], edge), v)
        v = jnp.where(lane >= 64, spread(cols[2], edge), v)
        v = jnp.where(lane >= 96, spread(fill, edge), v)
        a = jnp.where(here, v, a)
        b = jnp.where(east, spread(cols[3], edge), b)
        b = jnp.where(west, spread(cols[4], edge), b)
        out += [a, b]
    return tuple(out)


def fluid_kernel(
    pops_in, fill_in, flags_in, energy_in,
    pops_out, fill_out, warm_out,
    f0, f1, fz0, fz1, fz2, roll_z, g_s, part, eqs, flags, vel, heat_pad, heat_d,
    xs, xr, zs, zr, zd, hx, hzs, hzr, msg,
    load_sem, send_sem, recv_sem, hot_sem, hsend_sem, hrecv_sem, aout_sem, out_sem,
):
    g, d = lax.axis_index("grp"), lax.axis_index("dev")
    up, down = lax.rem(d + 1, ND), lax.rem(d + ND - 1, ND)
    east, west = lax.rem(g + 1, NG), lax.rem(g + NG - 1, NG)
    lane = lane_iota()

    loads = [
        pltpu.make_async_copy(pops_in, f0.at[:, pl.ds(1, NP)], load_sem.at[0]),
        pltpu.make_async_copy(fill_in, fz0.at[1, pl.ds(1, NP), pl.ds(8, 8)], load_sem.at[1]),
        pltpu.make_async_copy(flags_in, flags, load_sem.at[2]),
    ]
    for c in loads:
        c.start()

    barrier = pltpu.get_barrier_semaphore()

    def greet(i, c):
        pl.semaphore_signal(barrier, inc=1, device_id=(g, lax.rem(d + i, ND)), device_id_type=MESH)
        return c

    lax.fori_loop(1, ND, greet, 0)
    for gg in (east, west):
        for dd in (d, up, down):
            pl.semaphore_signal(barrier, inc=1, device_id=(gg, dd), device_id_type=MESH)

    zero8 = jnp.zeros((NY, NL), F32)

    def clear(p, c):
        for ref in (fz0, fz1, fz2):
            for k in range(3):
                ref[k, p, 0:8] = zero8
                ref[k, p, 16:24] = zero8
        for k in range(2):
            heat_pad[k, p, 0:8] = zero8
            heat_pad[k, p, 16:24] = zero8
        return c

    lax.fori_loop(0, NP + 2, clear, 0)

    for c in loads:
        c.wait()

    def send(t, src, dst, n, to):
        return pltpu.make_async_remote_copy(
            src_ref=src, dst_ref=dst, send_sem=send_sem.at[t, n], recv_sem=recv_sem.at[t, n],
            device_id=to, device_id_type=MESH,
        )

    def x_sends(t):
        return [
            send(t, xs.at[t, 0], xr.at[t, 0], 0, (east, d)),
            send(t, xs.at[t, 1], xr.at[t, 1], 1, (west, d)),
        ]

    def z_sends(t):
        out = []
        for side, to in ((0, up), (1, down)):
            out.append(send(t, zs.at[t, side], zr.at[t, side], 2 + 3 * side, (g, to)))
            out.append(send(t, zs.at[t, side], zd.at[t, side, 0], 3 + 3 * side, (east, to)))
            out.append(send(t, zs.at[t, side], zd.at[t, side, 1], 4 + 3 * side, (west, to)))
        return out

    def fill_x(t, f, fz):
        for k, q in enumerate(EAST):
            xs[t, 0, k] = f[q, NP]
        xs[t, 0, 5] = fz[1, NP, 8:16]
        for k, q in enumerate(WEST):
            xs[t, 1, k] = f[q, 1]
        xs[t, 1, 5] = fz[1, 1, 8:16]

    def store_z(t, acc):
        for side in range(2):
            zs[t, side, 0:8] = acc[2 * side]
            zs[t, side, 8:16] = acc[2 * side + 1]

    fill_x(0, f0, fz0)

    def pack0(p, acc):
        return pack_columns(
            [f0[q, p + 1] for q in UP], [f0[q, p + 1] for q in DOWN], fz0[1, p + 1, 8:16], p, acc, lane
        )

    acc0 = (zero8,) * 4
    store_z(0, lax.fori_loop(0, NP, pack0, acc0, unroll=4))

    pl.semaphore_wait(barrier, 37)
    pending = z_sends(0) + x_sends(0)
    for c in pending:
        c.start()

    def hot(i, to):
        return pltpu.make_async_remote_copy(
            src_ref=energy_in.at[0, :, pl.ds(pl.multiple_of(to * NL, NL), NL)],
            dst_ref=heat_pad.at[0, d + 1, pl.ds(8, 8)],
            send_sem=hot_sem.at[0], recv_sem=hot_sem.at[1], device_id=(g, to), device_id_type=MESH,
        )

    def hot_start(i, c):
        hot(i, lax.rem(d + i, ND)).start()
        return c

    lax.fori_loop(1, ND, hot_start, 0)
    own = pltpu.make_async_copy(
        energy_in.at[0, :, pl.ds(pl.multiple_of(d * NL, NL), NL)],
        heat_pad.at[0, d + 1, pl.ds(8, 8)], load_sem.at[3],
    )
    own.start()

    def local_part(f, fz):
        def body(p):
            pops = [f[q, p + 1] for q in range(19)]
            kind = flags[p]
            gas = kind == 0
            fill = fz[1, p + 1, 8:16]
            diffs = {q: pops[q] - pops[q + 1] for q in range(1, 19, 2)}
            sums = {q: pops[q] + pops[q + 1] for q in range(1, 19, 2)}
            (mx, my, mz), total = moments(diffs, sums)
            dens = jnp.where(gas, 1.0, total + pops[0])
            inv = 1.0 / dens
            vx, vy, vz = mx * inv, my * inv, mz * inv
            base = 1.0 - 1.5 * (vx * vx + vy * vy + vz * vz)

            def paired(q):
                cx, cy, cz = VELOCITIES[q]
                along = None
                for c, v in ((cx, vx), (cy, vy), (cz, vz)):
                    if c:
                        along = (v if c > 0 else -v) if along is None else (along + v if c > 0 else along - v)
                return (2.0 * WEIGHTS[q]) * (base + 4.5 * along * along)

            for k, q in enumerate(Z_PAIRS):
                eqs[k, p] = paired(q)
            for k, q in enumerate(CROSS):
                roll_z[k, p + 1] = pltpu.roll(pops[q], 1 if q in UP else NL - 1, 1)
            ex = None
            got = {0: pops[0]}
            for q in FLAT:
                cx, cy, _ = VELOCITIES[q]
                incoming = shift_rows(f[q, p + 1 - cx], cy)
                beside = fz[1, p + 1 - cx, 8 - cy : 16 - cy]
                empty = beside == 0.0
                back = pops[opposite(q)]
                got[q] = jnp.where(empty, paired(q if q % 2 else q - 1) - back, incoming)
                term = jnp.where(empty, 0.0, (fill + beside) * (incoming - back))
                ex = term if ex is None else ex + term
                g_s[q, p] = got[q]
            diffs = {q: got[q] - got[q + 1] for q in FLAT if q % 2}
            sums = {q: got[q] + got[q + 1] for q in FLAT if q % 2}
            (mx, my, _), total = moments(diffs, sums)
            part[0, p] = total + got[0]
            part[1, p] = mx
            part[2, p] = my
            part[3, p] = fill * dens + 0.5 * ex

        return body

    def arrive_x(t, f, fz):
        not_first, not_last = g > 0, g < NG - 1
        for k, q in enumerate(EAST):
            f[q, 0] = xr[t, 0, k]
        for k, q in enumerate(WEST):
            f[q, NP + 1] = xr[t, 1, k]
        fz[1, 0, 8:16] = jnp.where(not_first, xr[t, 0, 5], 0.0)
        fz[1, NP + 1, 8:16] = jnp.where(not_last, xr[t, 1, 5], 0.0)
        for q in (11, 13):
            roll_z[CROSS.index(q), 0] = pltpu.roll(f[q, 0], 1 if q in UP else NL - 1, 1)
        for q in (12, 14):
            roll_z[CROSS.index(q), NP + 1] = pltpu.roll(f[q, NP + 1], 1 if q in UP else NL - 1, 1)

    def arrive_z(t, fz):
        for side in range(2):
            inside = d > 0 if side == 0 else d < ND - 1
            main0, main1 = zr[t, side, 0:8], zr[t, side, 8:16]
            b = jnp.where(lane == 0, zd[t, side, 0, 8:16], main1)
            b = jnp.where(lane == 63, zd[t, side, 1, 8:16], b)
            zr[t, side, 8:16] = b
            edge = 0 if side == 0 else NL - 1
            k = 0 if side == 0 else 2
            by = 1 if side == 0 else NL - 1

            def column(p, c):
                old = pltpu.roll(fz[1, p + 1, 8:16], by, 1)
                new = pltpu.roll(main0, lax.rem(NL + edge - 96 - p, NL), 1)
                fz[k, p + 1, 8:16] = jnp.where(lane == edge, jnp.where(inside, new, 0.0), old)
                return c

            lax.fori_loop(0, NP, column, 0, unroll=8)
            for at, src, spot, ok in ((0, 0, 127, g > 0), (NP + 1, 1, 96, g < NG - 1)):
                old = pltpu.roll(fz[1, at, 8:16], by, 1)
                new = spread(zd[t, side, src, 0:8], spot)
                ok = jnp.logical_and(ok, inside)
                fz[k, at, 8:16] = jnp.where(lane == edge, jnp.where(ok, new, 0.0), old)

    def cross_part(t, f, fz, p):
        kind = flags[p]
        gas = kind == 0
        fill = fz[1, p + 1, 8:16]
        got = {}
        ex = None
        for side, dirs in enumerate((UP, DOWN)):
            edge = 0 if side == 0 else NL - 1
            for k, q in enumerate(dirs):
                cx, cy, cz = VELOCITIES[q]
                spot = 32 * k if k < 3 else 32 * (k - 3)
                rows = zr[t, side, 0:8] if k < 3 else zr[t, side, 8:16]
                halo = pltpu.roll(rows, lax.rem(NL + edge - spot - p, NL), 1)
                incoming = jnp.where(lane == edge, halo, roll_z[CROSS.index(q), p + 1 - cx])
                incoming = shift_rows(incoming, cy)
                beside = fz[1 - cz, p + 1 - cx, 8 - cy : 16 - cy]
                empty = beside == 0.0
                back = f[opposite(q), p + 1]
                pair = q if q % 2 else q - 1
                got[q] = jnp.where(empty, eqs[Z_PAIRS.index(pair), p] - back, incoming)
                term = jnp.where(empty, 0.0, (fill + beside) * (incoming - back))
                ex = term if ex is None else ex + term
        diffs = {q: got[q] - got[q + 1] for q in Z_PAIRS}
        sums = {q: got[q] + got[q + 1] for q in Z_PAIRS}
        (mx, my, mz), total = moments(diffs, sums)
        dens = jnp.where(gas, 1.0, total + part[0, p])
        inv = 1.0 / dens
        vx, vy, vz = (mx + part[1, p]) * inv, (my + part[2, p]) * inv, mz * inv
        mass = part[3, p] + 0.5 * ex
        fill_new = jnp.where(kind == 2, 1.0, jnp.where(gas, 0.0, jnp.clip(mass * inv, 0.01, 1.0)))
        return got, dens, (vx, vy, vz), fill_new

    def collide(got, gas, dens, vx, vy, vz):
        wz = vz + RELAX_TIME * GRAVITY
        base = 1.0 - 1.5 * (vx * vx + vy * vy + wz * wz)
        keep = jnp.where(gas, 0.0, 1.0 - 1.0 / RELAX_TIME)
        scale = jnp.where(gas, 0.0, dens * (1.0 / RELAX_TIME))
        new = {0: keep * got[0] + (WEIGHTS[0] * scale) * base}
        by_weight = {w: (w * scale, 3.0 * w * scale) for w in (WEIGHTS[1], WEIGHTS[7])}
        for q in range(1, 19, 2):
            along = None
            for c, v in zip(VELOCITIES[q], (vx, vy, wz)):
                if c:
                    along = (v if c > 0 else -v) if along is None else (along + v if c > 0 else along - v)
            even_w, odd_w = by_weight[WEIGHTS[q]]
            even = even_w * (base + 4.5 * along * along)
            odd = odd_w * along
            new[q] = keep * got[q] + (even + odd)
            new[q + 1] = keep * got[q + 1] + (even - odd)
        return new

    def before_z(t, f, fz, sends):
        body = local_part(f, fz)

        def inner(p, c):
            body(p)
            return c

        lax.fori_loop(1, NP - 1, inner, 0, unroll=2)
        for c in sends[6:]:
            c.wait_recv()
        arrive_x(t, f, fz)

        def outer(i, c):
            body(i * (NP - 1))
            return c

        lax.fori_loop(0, 2, outer, 0, unroll=2)

    before_z(0, f0, fz0, pending)
    for c in pending[:6]:
        c.wait_recv()
    arrive_z(0, fz0)

    def first(p, acc):
        got, dens, (vx, vy, vz), fill_new = cross_part(0, f0, fz0, p)
        got[0] = f0[0, p + 1]
        for q in FLAT:
            got[q] = g_s[q, p]
        new = collide(got, flags[p] == 0, dens, vx, vy, vz)
        for q in range(19):
            f1[q, p + 1] = new[q]
        fz1[1, p + 1, 8:16] = fill_new
        return pack_columns([new[q] for q in UP], [new[q] for q in DOWN], fill_new, p, acc, lane)

    store_z(1, lax.fori_loop(0, NP, first, acc0, unroll=2))
    fill_x(1, f1, fz1)
    again = z_sends(1) + x_sends(1)
    for c in again:
        c.start()

    own.wait()
    pltpu.make_async_copy(heat_pad.at[0, pl.ds(1, ND - 1), pl.ds(8, 8)], heat_pad.at[0, pl.ds(1, ND - 1), pl.ds(8, 8)], hot_sem.at[1]).wait()

    def heat_columns(p, acc):
        h = heat_pad[0, p + 1, 8:16]
        here = lane == p
        return jnp.where(here, spread(h, NL - 1), acc[0]), jnp.where(here, spread(h, 0), acc[1])

    hcols = lax.fori_loop(0, NP, heat_columns, (zero8, zero8), unroll=8)
    hzs[0] = hcols[0]
    hzs[1] = hcols[1]

    def hsend(src, dst, n, to):
        return pltpu.make_async_remote_copy(
            src_ref=src, dst_ref=dst, send_sem=hsend_sem.at[n], recv_sem=hrecv_sem.at[n],
            device_id=to, device_id_type=MESH,
        )

    hs = [
        hsend(hzs.at[0], hzr.at[0], 0, (g, up)),
        hsend(hzs.at[1], hzr.at[1], 1, (g, down)),
        hsend(heat_pad.at[0, NP, pl.ds(8, 8)], hx.at[0], 2, (east, d)),
        hsend(heat_pad.at[0, 1, pl.ds(8, 8)], hx.at[1], 3, (west, d)),
    ]
    for c in hs:
        c.start()

    before_z(1, f1, fz1, again)

    for c in hs:
        c.wait_recv()
    heat_pad[0, 0, 8:16] = jnp.where(g > 0, hx[0], 0.0)
    heat_pad[0, NP + 1, 8:16] = jnp.where(g < NG - 1, hx[1], 0.0)
    hz_low = jnp.where(d > 0, hzr[0], 0.0)
    hz_high = jnp.where(d < ND - 1, hzr[1], 0.0)

    def temp(h):
        return jnp.minimum(h, 1.0) + jnp.maximum(h - 1.5, 0.0)

    def differences(p, c):
        h = heat_pad[0, p + 1, 8:16]
        low = jnp.where(lane == 0, pltpu.roll(hz_low, lax.rem(NL - p, NL), 1), pltpu.roll(h, 1, 1))
        high = jnp.where(lane == NL - 1, pltpu.roll(hz_high, NL - 1 - p, 1), pltpu.roll(h, NL - 1, 1))
        others = (
            heat_pad[0, p, 8:16], heat_pad[0, p + 2, 8:16],
            heat_pad[0, p + 1, 7:15], heat_pad[0, p + 1, 9:17],
            low, high,
        )
        mine = temp(h)
        total = None
        for k, other in enumerate(others):
            dt = temp(other) - mine
            total = dt if total is None else total + dt
            heat_d[k, p] = dt * (0.05 * STEP_TIME)
            heat_d[6 + k, p] = (other - h) * STEP_TIME
        heat_d[12, p] = total * STEP_TIME
        return c

    lax.fori_loop(0, NP, differences, 0, unroll=4)

    for c in again[:6]:
        c.wait_recv()
    arrive_z(1, fz1)

    def second(p, c):
        got, dens, v, fill_new = cross_part(1, f1, fz1, p)
        for q in CROSS:
            g_s[q, p] = got[q]
        vel[0, p] = dens
        for a in range(3):
            vel[1 + a, p] = v[a]
        fz2[1, p + 1, 8:16] = fill_new
        return c

    lax.fori_loop(0, NP, second, 0, unroll=2)

    xs[2, 0, 0] = fz2[1, NP, 8:16]
    xs[2, 1, 0] = fz2[1, 1, 8:16]
    last = [
        send(2, xs.at[2, 0, 0], xr.at[2, 0, 0], 0, (east, d)),
        send(2, xs.at[2, 1, 0], xr.at[2, 1, 0], 1, (west, d)),
    ]
    for c in last:
        c.start()
    fill_copy = pltpu.make_async_copy(fz2.at[1, pl.ds(1, NP), pl.ds(8, 8)], fill_out, out_sem.at[0])
    fill_copy.start()
    for c in last:
        c.wait_recv()
    fz2[1, 0, 8:16] = jnp.where(g > 0, xr[2, 0, 0], 0.0)
    fz2[1, NP + 1, 8:16] = jnp.where(g < NG - 1, xr[2, 1, 0], 0.0)

    def back_copy(p):
        return pltpu.make_async_remote_copy(
            src_ref=msg.at[p], dst_ref=warm_out.at[d],
            send_sem=aout_sem.at[0], recv_sem=aout_sem.at[1], device_id=(g, p), device_id_type=MESH,
        )

    def transport(i, c):
        p = lax.rem(d + i, ND)
        fill = fz2[1, p + 1, 8:16]
        beside = (
            fz2[1, p, 8:16], fz2[1, p + 2, 8:16], fz2[1, p + 1, 7:15], fz2[1, p + 1, 9:17],
            jnp.where(lane == 0, 0.0, pltpu.roll(fill, 1, 1)),
            jnp.where(lane == NL - 1, 0.0, pltpu.roll(fill, NL - 1, 1)),
        )
        out = heat_pad[0, p + 1, 8:16] + (0.02 + 0.05 * fill) * heat_d[12, p]
        for k in range(6):
            out = out + beside[k] * heat_d[k, p]
        for a in range(3):
            v = vel[1 + a, p]
            out = out + jnp.maximum(v, 0.0) * heat_d[6 + 2 * a, p] - jnp.minimum(v, 0.0) * heat_d[7 + 2 * a, p]
        msg[p, 0:8] = out
        msg[p, 8:16] = fill

        @pl.when(i < ND)
        def _():
            back_copy(p).start()

        return c

    lax.fori_loop(1, ND + 1, transport, 0)
    keep = pltpu.make_async_copy(msg.at[d], warm_out.at[d], load_sem.at[3])
    keep.start()

    def collide_again(p, c):
        got = {q: g_s[q, p] for q in FLAT + CROSS}
        got[0] = f1[0, p + 1]
        new = collide(got, flags[p] == 0, vel[0, p], vel[1, p], vel[2, p], vel[3, p])
        for q in range(19):
            f0[q, p + 1] = new[q]
        return c

    lax.fori_loop(0, NP, collide_again, 0, unroll=2)
    pops_copy = pltpu.make_async_copy(f0.at[:, pl.ds(1, NP)], pops_out, out_sem.at[1])
    pops_copy.start()

    for c in pending + again + hs + last:
        c.wait_send()
    pltpu.make_async_copy(heat_pad.at[0, pl.ds(1, ND - 1), pl.ds(8, 8)], heat_pad.at[0, pl.ds(1, ND - 1), pl.ds(8, 8)], hot_sem.at[0]).wait()
    keep.wait()
    fill_copy.wait()
    pops_copy.wait()
    pltpu.make_async_copy(msg.at[pl.ds(0, ND - 1)], msg.at[pl.ds(0, ND - 1)], aout_sem.at[0]).wait()
    pltpu.make_async_copy(msg.at[pl.ds(0, ND - 1)], msg.at[pl.ds(0, ND - 1)], aout_sem.at[1]).wait()


def finish_kernel(pops_mid, fill_mid, warm_mid, energy_in, pops_out, fill_out, energy_out, got, own, done, sem):
    copies = [
        pltpu.make_async_copy(warm_mid, got, sem.at[0]),
        pltpu.make_async_copy(energy_in, own, sem.at[1]),
        pltpu.make_async_copy(fill_mid, fill_out, sem.at[2]),
        pltpu.make_async_copy(pops_mid, pops_out, sem.at[3]),
    ]
    for c in copies:
        c.start()
    copies[0].wait()
    copies[1].wait()
    lane = lane_iota()

    def temp(h):
        return jnp.minimum(h, 1.0) + jnp.maximum(h - 1.5, 0.0)

    for e in range(ND):
        cells = slice(e * NL, (e + 1) * NL)
        out = got[e, 0:8]
        warmth = temp(own[0, :, cells])
        for side, other in ((0, e - 1), (1, e + 1)):
            if other < 0 or other >= ND:
                continue
            by, edge = (1, 0) if side == 0 else (NL - 1, NL - 1)
            beyond = temp(own[0, :, other * NL : (other + 1) * NL])
            term = pltpu.roll(got[other, 8:16], by, 1) * (pltpu.roll(beyond, by, 1) - warmth)
            out = out + jnp.where(lane == edge, (0.05 * STEP_TIME) * term, 0.0)
        done[0, :, cells] = out
    last = pltpu.make_async_copy(done, energy_out, sem.at[0])
    last.start()
    last.wait()
    copies[2].wait()
    copies[3].wait()


def shards(populations, fill, flags, specific_energy_grid):
    plane = (NY, NL)
    any_spec = pl.BlockSpec(memory_space=pl.ANY)
    pops_mid, fill_mid, warm_mid = pl.pallas_call(
        fluid_kernel,
        out_shape=(
            jax.ShapeDtypeStruct((19, NP) + plane, F32),
            jax.ShapeDtypeStruct((NP,) + plane, F32),
            jax.ShapeDtypeStruct((ND, 16, NL), F32),
        ),
        in_specs=[any_spec] * 4,
        out_specs=(any_spec,) * 3,
        scratch_shapes=[
            pltpu.VMEM((19, NP + 2) + plane, F32),
            pltpu.VMEM((19, NP + 2) + plane, F32),
            pltpu.VMEM((3, NP + 2, 24, NL), F32),
            pltpu.VMEM((3, NP + 2, 24, NL), F32),
            pltpu.VMEM((3, NP + 2, 24, NL), F32),
            pltpu.VMEM((10, NP + 2) + plane, F32),
            pltpu.VMEM((19, NP) + plane, F32),
            pltpu.VMEM((4, NP) + plane, F32),
            pltpu.VMEM((5, NP) + plane, F32),
            pltpu.VMEM((NP,) + plane, jnp.int32),
            pltpu.VMEM((4, NP) + plane, F32),
            pltpu.VMEM((2, NP + 2, 24, NL), F32),
            pltpu.VMEM((13, NP) + plane, F32),
            pltpu.VMEM((3, 2, 6) + plane, F32),
            pltpu.VMEM((3, 2, 6) + plane, F32),
            pltpu.VMEM((2, 2, 16, NL), F32),
            pltpu.VMEM((2, 2, 16, NL), F32),
            pltpu.VMEM((2, 2, 2, 16, NL), F32),
            pltpu.VMEM((2,) + plane, F32),
            pltpu.VMEM((2,) + plane, F32),
            pltpu.VMEM((2,) + plane, F32),
            pltpu.VMEM((ND, 16, NL), F32),
            pltpu.SemaphoreType.DMA((4,)),
            pltpu.SemaphoreType.DMA((3, 8)),
            pltpu.SemaphoreType.DMA((3, 8)),
            pltpu.SemaphoreType.DMA((2,)),
            pltpu.SemaphoreType.DMA((4,)),
            pltpu.SemaphoreType.DMA((4,)),
            pltpu.SemaphoreType.DMA((2,)),
            pltpu.SemaphoreType.DMA((2,)),
        ],
        compiler_params=pltpu.CompilerParams(
            collective_id=0, has_side_effects=True, vmem_limit_bytes=40 * 1024 * 1024
        ),
        name="pour",
    )(populations, fill, flags, specific_energy_grid)
    return pl.pallas_call(
        finish_kernel,
        out_shape=(
            jax.ShapeDtypeStruct((19, NP) + plane, F32),
            jax.ShapeDtypeStruct((NP,) + plane, F32),
            jax.ShapeDtypeStruct((1, NY, ND * NL), F32),
        ),
        in_specs=[any_spec] * 4,
        out_specs=(any_spec,) * 3,
        scratch_shapes=[
            pltpu.VMEM((ND, 16, NL), F32),
            pltpu.VMEM((1, NY, ND * NL), F32),
            pltpu.VMEM((1, NY, ND * NL), F32),
            pltpu.SemaphoreType.DMA((4,)),
        ],
        compiler_params=pltpu.CompilerParams(vmem_limit_bytes=8 * 1024 * 1024),
        name="finish",
    )(pops_mid, fill_mid, warm_mid, specific_energy_grid)


def solution(mesh):
    in_specs = (
        P(None, "grp", None, "dev"),
        P("grp", None, "dev"),
        P("grp", None, "dev"),
        P(("grp", "dev"), None, None),
    )
    out_specs = (P(None, "grp", None, "dev"), P("grp", None, "dev"), P(("grp", "dev"), None, None))
    return jax.shard_map(shards, mesh=mesh, in_specs=in_specs, out_specs=out_specs, check_vma=False)
```

```python
import functools

import jax
import jax.numpy as jnp
from jax import lax
from jax.experimental import pallas as pl
from jax.experimental.pallas import tpu as pltpu
from jax.sharding import PartitionSpec as P

MESH = pl.DeviceIdType.MESH
F32 = jnp.float32
VELOCITIES = (
    (0, 0, 0),
    (1, 0, 0),
    (-1, 0, 0),
    (0, 1, 0),
    (0, -1, 0),
    (0, 0, 1),
    (0, 0, -1),
    (1, 1, 0),
    (-1, -1, 0),
    (1, -1, 0),
    (-1, 1, 0),
    (1, 0, 1),
    (-1, 0, -1),
    (1, 0, -1),
    (-1, 0, 1),
    (0, 1, 1),
    (0, -1, -1),
    (0, 1, -1),
    (0, -1, 1),
)
WEIGHTS = (1.0 / 3.0,) + (1.0 / 18.0,) * 6 + (1.0 / 36.0,) * 12
RELAX_TIME = 0.8
GRAVITY = -0.002
STEP_TIME = 0.2

NG, ND, NP, NY, NL = 4, 32, 32, 8, 128
FLAT = (1, 2, 3, 4, 7, 8, 9, 10)
UP = (5, 15, 18, 11, 14)
DOWN = (6, 16, 17, 13, 12)
CROSS = UP + DOWN
EAST = (1, 7, 9, 11, 13)
WEST = (2, 8, 10, 12, 14)
Z_PAIRS = (5, 11, 13, 15, 17)


def opposite(q):
    return q + 1 if q % 2 == 1 else q - 1


def lane_iota():
    return lax.broadcasted_iota(jnp.int32, (NY, NL), 1)


def shift_rows(x, cy):
    return x if cy == 0 else pltpu.roll(x, cy % NY, 0)


def spread(x, lane):
    return jnp.broadcast_to(x[:, lane : lane + 1], (NY, NL))


def moments(d, s):
    out = []
    for axis in range(3):
        total = None
        for q, diff in d.items():
            c = VELOCITIES[q][axis]
            if c == 0:
                continue
            if total is None:
                total = diff if c > 0 else -diff
            else:
                total = total + diff if c > 0 else total - diff
        out.append(total)
    return out, sum(s.values())


def pack_columns(tops, bottoms, fill, p, acc, lane):
    spot = lane & 31
    here = spot == p
    east = lane == ((p + 1) & 31)
    west = lane == 32 + ((p + 31) & 31)
    out = []
    for side, (cols, edge) in enumerate(((tops, NL - 1), (bottoms, 0))):
        a, b = acc[2 * side], acc[2 * side + 1]
        v = spread(cols[0], edge)
        v = jnp.where(lane >= 32, spread(cols[1], edge), v)
        v = jnp.where(lane >= 64, spread(cols[2], edge), v)
        v = jnp.where(lane >= 96, spread(fill, edge), v)
        a = jnp.where(here, v, a)
        b = jnp.where(east, spread(cols[3], edge), b)
        b = jnp.where(west, spread(cols[4], edge), b)
        out += [a, b]
    return tuple(out)


def fluid_kernel(
    pops_in, fill_in, flags_in, energy_in,
    pops_out, fill_out, warm_out,
    f0, f1, fz0, fz1, fz2, roll_z, g_s, part, eqs, flags, vel, heat_pad, heat_d,
    xs, xr, zs, zr, zd, hx, hzs, hzr, msg,
    load_sem, send_sem, recv_sem, hot_sem, hsend_sem, hrecv_sem, aout_sem, out_sem,
):
    g, d = lax.axis_index("grp"), lax.axis_index("dev")
    up, down = lax.rem(d + 1, ND), lax.rem(d + ND - 1, ND)
    east, west = lax.rem(g + 1, NG), lax.rem(g + NG - 1, NG)
    lane = lane_iota()

    loads = [
        pltpu.make_async_copy(pops_in, f0.at[:, pl.ds(1, NP)], load_sem.at[0]),
        pltpu.make_async_copy(fill_in, fz0.at[1, pl.ds(1, NP), pl.ds(8, 8)], load_sem.at[1]),
        pltpu.make_async_copy(flags_in, flags, load_sem.at[2]),
    ]
    for c in loads:
        c.start()

    barrier = pltpu.get_barrier_semaphore()

    def greet(i, c):
        pl.semaphore_signal(barrier, inc=1, device_id=(g, lax.rem(d + i, ND)), device_id_type=MESH)
        return c

    lax.fori_loop(1, ND, greet, 0)
    for gg in (east, west):
        for dd in (d, up, down):
            pl.semaphore_signal(barrier, inc=1, device_id=(gg, dd), device_id_type=MESH)

    zero8 = jnp.zeros((NY, NL), F32)

    def clear(p, c):
        for ref in (fz0, fz1, fz2):
            for k in range(3):
                ref[k, p, 0:8] = zero8
                ref[k, p, 16:24] = zero8
        for k in range(2):
            heat_pad[k, p, 0:8] = zero8
            heat_pad[k, p, 16:24] = zero8
        return c

    lax.fori_loop(0, NP + 2, clear, 0)

    for c in loads:
        c.wait()

    def send(t, src, dst, n, to):
        return pltpu.make_async_remote_copy(
            src_ref=src, dst_ref=dst, send_sem=send_sem.at[t, n], recv_sem=recv_sem.at[t, n],
            device_id=to, device_id_type=MESH,
        )

    def ends_first(body, carry, between):
        def block(base, c):
            for j in range(4):
                c = body(base + j, c)
            return c

        carry = lax.fori_loop(0, 2, lambda i, c: block(i * (NP - 4), c), carry)
        between()
        return lax.fori_loop(1, NP // 4 - 1, lambda i, c: block(i * 4, c), carry)

    def x_sends(t):
        return [
            send(t, xs.at[t, 0], xr.at[t, 0], 0, (east, d)),
            send(t, xs.at[t, 1], xr.at[t, 1], 1, (west, d)),
        ]

    def z_sends(t):
        out = []
        for side, to in ((0, up), (1, down)):
            out.append(send(t, zs.at[t, side], zr.at[t, side], 2 + 3 * side, (g, to)))
            out.append(send(t, zs.at[t, side], zd.at[t, side, 0], 3 + 3 * side, (east, to)))
            out.append(send(t, zs.at[t, side], zd.at[t, side, 1], 4 + 3 * side, (west, to)))
        return out

    def fill_x(t, f, fz):
        for k, q in enumerate(EAST):
            xs[t, 0, k] = f[q, NP]
        xs[t, 0, 5] = fz[1, NP, 8:16]
        for k, q in enumerate(WEST):
            xs[t, 1, k] = f[q, 1]
        xs[t, 1, 5] = fz[1, 1, 8:16]

    def store_z(t, acc):
        for side in range(2):
            zs[t, side, 0:8] = acc[2 * side]
            zs[t, side, 8:16] = acc[2 * side + 1]

    fill_x(0, f0, fz0)

    def pack0(p, acc):
        return pack_columns(
            [f0[q, p + 1] for q in UP], [f0[q, p + 1] for q in DOWN], fz0[1, p + 1, 8:16], p, acc, lane
        )

    acc0 = (zero8,) * 4
    store_z(0, lax.fori_loop(0, NP, pack0, acc0, unroll=8))

    pl.semaphore_wait(barrier, 37)
    pending = z_sends(0) + x_sends(0)
    for c in pending:
        c.start()

    def hot(i, to):
        return pltpu.make_async_remote_copy(
            src_ref=energy_in.at[0, :, pl.ds(pl.multiple_of(to * NL, NL), NL)],
            dst_ref=heat_pad.at[0, d + 1, pl.ds(8, 8)],
            send_sem=hot_sem.at[0], recv_sem=hot_sem.at[1], device_id=(g, to), device_id_type=MESH,
        )

    def hot_start(i, c):
        hot(i, lax.rem(d + i, ND)).start()
        return c

    lax.fori_loop(1, ND, hot_start, 0)
    own = pltpu.make_async_copy(
        energy_in.at[0, :, pl.ds(pl.multiple_of(d * NL, NL), NL)],
        heat_pad.at[0, d + 1, pl.ds(8, 8)], load_sem.at[3],
    )
    own.start()

    def local_part(f, fz):
        def body(p):
            pops = [f[q, p + 1] for q in range(19)]
            kind = flags[p]
            gas = kind == 0
            fill = fz[1, p + 1, 8:16]
            diffs = {q: pops[q] - pops[q + 1] for q in range(1, 19, 2)}
            sums = {q: pops[q] + pops[q + 1] for q in range(1, 19, 2)}
            (mx, my, mz), total = moments(diffs, sums)
            dens = jnp.where(gas, 1.0, total + pops[0])
            inv = 1.0 / dens
            vx, vy, vz = mx * inv, my * inv, mz * inv
            base = 1.0 - 1.5 * (vx * vx + vy * vy + vz * vz)

            def paired(q):
                cx, cy, cz = VELOCITIES[q]
                along = None
                for c, v in ((cx, vx), (cy, vy), (cz, vz)):
                    if c:
                        along = (v if c > 0 else -v) if along is None else (along + v if c > 0 else along - v)
                return (2.0 * WEIGHTS[q]) * (base + 4.5 * along * along)

            for k, q in enumerate(Z_PAIRS):
                eqs[k, p] = paired(q)
            for k, q in enumerate(CROSS):
                roll_z[k, p + 1] = pltpu.roll(pops[q], 1 if q in UP else NL - 1, 1)
            fz[0, p + 1, 8:16] = pltpu.roll(fill, 1, 1)
            fz[2, p + 1, 8:16] = pltpu.roll(fill, NL - 1, 1)
            ex = None
            got = {0: pops[0]}
            for q in FLAT:
                cx, cy, _ = VELOCITIES[q]
                incoming = shift_rows(f[q, p + 1 - cx], cy)
                beside = fz[1, p + 1 - cx, 8 - cy : 16 - cy]
                empty = beside == 0.0
                back = pops[opposite(q)]
                got[q] = jnp.where(empty, paired(q if q % 2 else q - 1) - back, incoming)
                term = jnp.where(empty, 0.0, (fill + beside) * (incoming - back))
                ex = term if ex is None else ex + term
                g_s[q, p] = got[q]
            diffs = {q: got[q] - got[q + 1] for q in FLAT if q % 2}
            sums = {q: got[q] + got[q + 1] for q in FLAT if q % 2}
            (mx, my, _), total = moments(diffs, sums)
            part[0, p] = total + got[0]
            part[1, p] = mx
            part[2, p] = my
            part[3, p] = fill * dens + 0.5 * ex

        return body

    def arrive_x(t, f, fz):
        not_first, not_last = g > 0, g < NG - 1
        for k, q in enumerate(EAST):
            f[q, 0] = xr[t, 0, k]
        for k, q in enumerate(WEST):
            f[q, NP + 1] = xr[t, 1, k]
        fz[1, 0, 8:16] = jnp.where(not_first, xr[t, 0, 5], 0.0)
        fz[1, NP + 1, 8:16] = jnp.where(not_last, xr[t, 1, 5], 0.0)
        for q in (11, 13):
            roll_z[CROSS.index(q), 0] = pltpu.roll(f[q, 0], 1 if q in UP else NL - 1, 1)
        for q in (12, 14):
            roll_z[CROSS.index(q), NP + 1] = pltpu.roll(f[q, NP + 1], 1 if q in UP else NL - 1, 1)

    def arrive_z(t, fz):
        inside = (d > 0, d < ND - 1)
        fills = []
        for side in range(2):
            b = jnp.where(lane == 0, zd[t, side, 0, 8:16], zr[t, side, 8:16])
            b = jnp.where(lane == 63, zd[t, side, 1, 8:16], b)
            zr[t, side, 8:16] = b
            fills.append(jnp.where(inside[side], zr[t, side, 0:8], 0.0))
            edge, k, by = ((0, 0, 1), (NL - 1, 2, NL - 1))[side]
            for at, src, spot, ok in ((0, 0, 127, g > 0), (NP + 1, 1, 96, g < NG - 1)):
                old = pltpu.roll(fz[1, at, 8:16], by, 1)
                new = spread(zd[t, side, src, 0:8], spot)
                ok = jnp.logical_and(ok, inside[side])
                fz[k, at, 8:16] = jnp.where(lane == edge, jnp.where(ok, new, 0.0), old)

        def column(p, c):
            for side, edge, k in ((0, 0, 0), (1, NL - 1, 2)):
                new = pltpu.roll(fills[side], lax.rem(NL + edge - 96 - p, NL), 1)
                fz[k, p + 1, 8:16] = jnp.where(lane == edge, new, fz[k, p + 1, 8:16])
            return c

        lax.fori_loop(0, NP, column, 0, unroll=16)

    def cross_part(t, f, fz, p):
        kind = flags[p]
        gas = kind == 0
        fill = fz[1, p + 1, 8:16]
        got = {}
        ex = None
        for side, dirs in enumerate((UP, DOWN)):
            edge = 0 if side == 0 else NL - 1
            for k, q in enumerate(dirs):
                cx, cy, cz = VELOCITIES[q]
                spot = 32 * k if k < 3 else 32 * (k - 3)
                rows = zr[t, side, 0:8] if k < 3 else zr[t, side, 8:16]
                halo = pltpu.roll(rows, lax.rem(NL + edge - spot - p, NL), 1)
                incoming = jnp.where(lane == edge, halo, roll_z[CROSS.index(q), p + 1 - cx])
                incoming = shift_rows(incoming, cy)
                beside = fz[1 - cz, p + 1 - cx, 8 - cy : 16 - cy]
                empty = beside == 0.0
                back = f[opposite(q), p + 1]
                pair = q if q % 2 else q - 1
                got[q] = jnp.where(empty, eqs[Z_PAIRS.index(pair), p] - back, incoming)
                term = jnp.where(empty, 0.0, (fill + beside) * (incoming - back))
                ex = term if ex is None else ex + term
        diffs = {q: got[q] - got[q + 1] for q in Z_PAIRS}
        sums = {q: got[q] + got[q + 1] for q in Z_PAIRS}
        (mx, my, mz), total = moments(diffs, sums)
        dens = jnp.where(gas, 1.0, total + part[0, p])
        inv = 1.0 / dens
        vx, vy, vz = (mx + part[1, p]) * inv, (my + part[2, p]) * inv, mz * inv
        mass = part[3, p] + 0.5 * ex
        fill_new = jnp.where(kind == 2, 1.0, jnp.where(gas, 0.0, jnp.clip(mass * inv, 0.01, 1.0)))
        return got, dens, (vx, vy, vz), fill_new

    def collide(got, gas, dens, vx, vy, vz):
        wz = vz + RELAX_TIME * GRAVITY
        base = 1.0 - 1.5 * (vx * vx + vy * vy + wz * wz)
        keep = jnp.where(gas, 0.0, 1.0 - 1.0 / RELAX_TIME)
        scale = jnp.where(gas, 0.0, dens * (1.0 / RELAX_TIME))
        new = {0: keep * got[0] + (WEIGHTS[0] * scale) * base}
        by_weight = {w: (w * scale, 3.0 * w * scale) for w in (WEIGHTS[1], WEIGHTS[7])}
        for q in range(1, 19, 2):
            along = None
            for c, v in zip(VELOCITIES[q], (vx, vy, wz)):
                if c:
                    along = (v if c > 0 else -v) if along is None else (along + v if c > 0 else along - v)
            even_w, odd_w = by_weight[WEIGHTS[q]]
            even = even_w * (base + 4.5 * along * along)
            odd = odd_w * along
            new[q] = keep * got[q] + (even + odd)
            new[q + 1] = keep * got[q + 1] + (even - odd)
        return new

    def before_z(t, f, fz, sends):
        body = local_part(f, fz)

        def inner(p, c):
            body(p)
            return c

        lax.fori_loop(1, NP - 1, inner, 0, unroll=5)
        for c in sends[6:]:
            c.wait_recv()
        arrive_x(t, f, fz)

        def outer(i, c):
            body(i * (NP - 1))
            return c

        lax.fori_loop(0, 2, outer, 0, unroll=2)

    before_z(0, f0, fz0, pending)
    for c in pending[:6]:
        c.wait_recv()
    arrive_z(0, fz0)

    def first(p, acc):
        got, dens, (vx, vy, vz), fill_new = cross_part(0, f0, fz0, p)
        got[0] = f0[0, p + 1]
        for q in FLAT:
            got[q] = g_s[q, p]
        new = collide(got, flags[p] == 0, dens, vx, vy, vz)
        for q in range(19):
            f1[q, p + 1] = new[q]
        fz1[1, p + 1, 8:16] = fill_new
        return pack_columns([new[q] for q in UP], [new[q] for q in DOWN], fill_new, p, acc, lane)

    again = z_sends(1) + x_sends(1)

    def first_ends():
        fill_x(1, f1, fz1)
        for c in again[6:]:
            c.start()

    store_z(1, ends_first(first, acc0, first_ends))
    for c in again[:6]:
        c.start()

    own.wait()
    pltpu.make_async_copy(heat_pad.at[0, pl.ds(1, ND - 1), pl.ds(8, 8)], heat_pad.at[0, pl.ds(1, ND - 1), pl.ds(8, 8)], hot_sem.at[1]).wait()

    def heat_columns(p, acc):
        h = heat_pad[0, p + 1, 8:16]
        here = lane == p
        return jnp.where(here, spread(h, NL - 1), acc[0]), jnp.where(here, spread(h, 0), acc[1])

    hcols = lax.fori_loop(0, NP, heat_columns, (zero8, zero8), unroll=8)
    hzs[0] = hcols[0]
    hzs[1] = hcols[1]

    def hsend(src, dst, n, to):
        return pltpu.make_async_remote_copy(
            src_ref=src, dst_ref=dst, send_sem=hsend_sem.at[n], recv_sem=hrecv_sem.at[n],
            device_id=to, device_id_type=MESH,
        )

    hs = [
        hsend(hzs.at[0], hzr.at[0], 0, (g, up)),
        hsend(hzs.at[1], hzr.at[1], 1, (g, down)),
        hsend(heat_pad.at[0, NP, pl.ds(8, 8)], hx.at[0], 2, (east, d)),
        hsend(heat_pad.at[0, 1, pl.ds(8, 8)], hx.at[1], 3, (west, d)),
    ]
    for c in hs:
        c.start()

    before_z(1, f1, fz1, again)

    for c in hs:
        c.wait_recv()
    heat_pad[0, 0, 8:16] = jnp.where(g > 0, hx[0], 0.0)
    heat_pad[0, NP + 1, 8:16] = jnp.where(g < NG - 1, hx[1], 0.0)
    hz_low = jnp.where(d > 0, hzr[0], 0.0)
    hz_high = jnp.where(d < ND - 1, hzr[1], 0.0)

    def temp(h):
        return jnp.minimum(h, 1.0) + jnp.maximum(h - 1.5, 0.0)

    def differences(p, c):
        h = heat_pad[0, p + 1, 8:16]
        low = jnp.where(lane == 0, pltpu.roll(hz_low, lax.rem(NL - p, NL), 1), pltpu.roll(h, 1, 1))
        high = jnp.where(lane == NL - 1, pltpu.roll(hz_high, NL - 1 - p, 1), pltpu.roll(h, NL - 1, 1))
        others = (
            heat_pad[0, p, 8:16], heat_pad[0, p + 2, 8:16],
            heat_pad[0, p + 1, 7:15], heat_pad[0, p + 1, 9:17],
            low, high,
        )
        mine = temp(h)
        total = None
        for k, other in enumerate(others):
            dt = temp(other) - mine
            total = dt if total is None else total + dt
            heat_d[k, p] = dt * (0.05 * STEP_TIME)
            heat_d[6 + k, p] = (other - h) * STEP_TIME
        heat_d[12, p] = total * STEP_TIME
        return c

    lax.fori_loop(0, NP, differences, 0, unroll=8)

    for c in again[:6]:
        c.wait_recv()
    arrive_z(1, fz1)

    def second(p, c):
        got, dens, v, fill_new = cross_part(1, f1, fz1, p)
        for q in CROSS:
            g_s[q, p] = got[q]
        vel[0, p] = dens
        for a in range(3):
            vel[1 + a, p] = v[a]
        fz2[1, p + 1, 8:16] = fill_new
        return c

    last = [
        send(2, xs.at[2, 0, 0], xr.at[2, 0, 0], 0, (east, d)),
        send(2, xs.at[2, 1, 0], xr.at[2, 1, 0], 1, (west, d)),
    ]

    def second_ends():
        xs[2, 0, 0] = fz2[1, NP, 8:16]
        xs[2, 1, 0] = fz2[1, 1, 8:16]
        for c in last:
            c.start()

    ends_first(second, 0, second_ends)
    fill_copy = pltpu.make_async_copy(fz2.at[1, pl.ds(1, NP), pl.ds(8, 8)], fill_out, out_sem.at[0])
    fill_copy.start()
    for c in last:
        c.wait_recv()
    fz2[1, 0, 8:16] = jnp.where(g > 0, xr[2, 0, 0], 0.0)
    fz2[1, NP + 1, 8:16] = jnp.where(g < NG - 1, xr[2, 1, 0], 0.0)

    def back_copy(p):
        return pltpu.make_async_remote_copy(
            src_ref=msg.at[p], dst_ref=warm_out.at[d],
            send_sem=aout_sem.at[0], recv_sem=aout_sem.at[1], device_id=(g, p), device_id_type=MESH,
        )

    def transport(p, c):
        fill = fz2[1, p + 1, 8:16]
        beside = (
            fz2[1, p, 8:16], fz2[1, p + 2, 8:16], fz2[1, p + 1, 7:15], fz2[1, p + 1, 9:17],
            jnp.where(lane == 0, 0.0, pltpu.roll(fill, 1, 1)),
            jnp.where(lane == NL - 1, 0.0, pltpu.roll(fill, NL - 1, 1)),
        )
        out = heat_pad[0, p + 1, 8:16] + (0.02 + 0.05 * fill) * heat_d[12, p]
        for k in range(6):
            out = out + beside[k] * heat_d[k, p]
        for a in range(3):
            v = vel[1 + a, p]
            out = out + jnp.maximum(v, 0.0) * heat_d[6 + 2 * a, p] - jnp.minimum(v, 0.0) * heat_d[7 + 2 * a, p]
        msg[p, 0:8] = out
        msg[p, 8:16] = fill
        return c

    lax.fori_loop(0, NP, transport, 0, unroll=8)

    def back_start(i, c):
        back_copy(lax.rem(d + i, ND)).start()
        return c

    lax.fori_loop(1, ND, back_start, 0)
    keep = pltpu.make_async_copy(msg.at[d], warm_out.at[d], load_sem.at[3])
    keep.start()

    def collide_again(p, c):
        got = {q: g_s[q, p] for q in FLAT + CROSS}
        got[0] = f1[0, p + 1]
        new = collide(got, flags[p] == 0, vel[0, p], vel[1, p], vel[2, p], vel[3, p])
        for q in range(19):
            f0[q, p + 1] = new[q]
        return c

    lax.fori_loop(0, NP, collide_again, 0, unroll=2)
    pops_copy = pltpu.make_async_copy(f0.at[:, pl.ds(1, NP)], pops_out, out_sem.at[1])
    pops_copy.start()

    for c in pending + again + hs + last:
        c.wait_send()
    pltpu.make_async_copy(heat_pad.at[0, pl.ds(1, ND - 1), pl.ds(8, 8)], heat_pad.at[0, pl.ds(1, ND - 1), pl.ds(8, 8)], hot_sem.at[0]).wait()
    keep.wait()
    fill_copy.wait()
    pops_copy.wait()
    pltpu.make_async_copy(msg.at[pl.ds(0, ND - 1)], msg.at[pl.ds(0, ND - 1)], aout_sem.at[0]).wait()
    pltpu.make_async_copy(msg.at[pl.ds(0, ND - 1)], msg.at[pl.ds(0, ND - 1)], aout_sem.at[1]).wait()


def finish_kernel(pops_mid, fill_mid, warm_mid, energy_in, pops_out, fill_out, energy_out, got, own, done, sem):
    copies = [
        pltpu.make_async_copy(warm_mid, got, sem.at[0]),
        pltpu.make_async_copy(energy_in, own, sem.at[1]),
        pltpu.make_async_copy(fill_mid, fill_out, sem.at[2]),
        pltpu.make_async_copy(pops_mid, pops_out, sem.at[3]),
    ]
    for c in copies:
        c.start()
    copies[0].wait()
    copies[1].wait()
    lane = lane_iota()

    def temp(h):
        return jnp.minimum(h, 1.0) + jnp.maximum(h - 1.5, 0.0)

    for e in range(ND):
        cells = slice(e * NL, (e + 1) * NL)
        out = got[e, 0:8]
        warmth = temp(own[0, :, cells])
        for side, other in ((0, e - 1), (1, e + 1)):
            if other < 0 or other >= ND:
                continue
            by, edge = (1, 0) if side == 0 else (NL - 1, NL - 1)
            beyond = temp(own[0, :, other * NL : (other + 1) * NL])
            term = pltpu.roll(got[other, 8:16], by, 1) * (pltpu.roll(beyond, by, 1) - warmth)
            out = out + jnp.where(lane == edge, (0.05 * STEP_TIME) * term, 0.0)
        done[0, :, cells] = out
    last = pltpu.make_async_copy(done, energy_out, sem.at[0])
    last.start()
    last.wait()
    copies[2].wait()
    copies[3].wait()


def shards(populations, fill, flags, specific_energy_grid):
    plane = (NY, NL)
    any_spec = pl.BlockSpec(memory_space=pl.ANY)
    hbm_spec = pl.BlockSpec(memory_space=pltpu.HBM)
    given = [
        pltpu.with_memory_space_constraint(x, pltpu.HBM)
        for x in (populations, fill, flags, specific_energy_grid)
    ]
    pops_mid, fill_mid, warm_mid = pl.pallas_call(
        fluid_kernel,
        out_shape=(
            jax.ShapeDtypeStruct((19, NP) + plane, F32),
            jax.ShapeDtypeStruct((NP,) + plane, F32),
            jax.ShapeDtypeStruct((ND, 16, NL), F32),
        ),
        in_specs=[hbm_spec] * 4,
        out_specs=(any_spec,) * 3,
        scratch_shapes=[
            pltpu.VMEM((19, NP + 2) + plane, F32),
            pltpu.VMEM((19, NP + 2) + plane, F32),
            pltpu.VMEM((3, NP + 2, 24, NL), F32),
            pltpu.VMEM((3, NP + 2, 24, NL), F32),
            pltpu.VMEM((3, NP + 2, 24, NL), F32),
            pltpu.VMEM((10, NP + 2) + plane, F32),
            pltpu.VMEM((19, NP) + plane, F32),
            pltpu.VMEM((4, NP) + plane, F32),
            pltpu.VMEM((5, NP) + plane, F32),
            pltpu.VMEM((NP,) + plane, jnp.int32),
            pltpu.VMEM((4, NP) + plane, F32),
            pltpu.VMEM((2, NP + 2, 24, NL), F32),
            pltpu.VMEM((13, NP) + plane, F32),
            pltpu.VMEM((3, 2, 6) + plane, F32),
            pltpu.VMEM((3, 2, 6) + plane, F32),
            pltpu.VMEM((2, 2, 16, NL), F32),
            pltpu.VMEM((2, 2, 16, NL), F32),
            pltpu.VMEM((2, 2, 2, 16, NL), F32),
            pltpu.VMEM((2,) + plane, F32),
            pltpu.VMEM((2,) + plane, F32),
            pltpu.VMEM((2,) + plane, F32),
            pltpu.VMEM((ND, 16, NL), F32),
            pltpu.SemaphoreType.DMA((4,)),
            pltpu.SemaphoreType.DMA((3, 8)),
            pltpu.SemaphoreType.DMA((3, 8)),
            pltpu.SemaphoreType.DMA((2,)),
            pltpu.SemaphoreType.DMA((4,)),
            pltpu.SemaphoreType.DMA((4,)),
            pltpu.SemaphoreType.DMA((2,)),
            pltpu.SemaphoreType.DMA((2,)),
        ],
        compiler_params=pltpu.CompilerParams(
            collective_id=0, has_side_effects=True, vmem_limit_bytes=40 * 1024 * 1024
        ),
        name="pour",
    )(*given)
    return pl.pallas_call(
        finish_kernel,
        out_shape=(
            jax.ShapeDtypeStruct((19, NP) + plane, F32),
            jax.ShapeDtypeStruct((NP,) + plane, F32),
            jax.ShapeDtypeStruct((1, NY, ND * NL), F32),
        ),
        in_specs=[any_spec] * 4,
        out_specs=(any_spec,) * 3,
        scratch_shapes=[
            pltpu.VMEM((ND, 16, NL), F32),
            pltpu.VMEM((1, NY, ND * NL), F32),
            pltpu.VMEM((1, NY, ND * NL), F32),
            pltpu.SemaphoreType.DMA((4,)),
        ],
        compiler_params=pltpu.CompilerParams(vmem_limit_bytes=8 * 1024 * 1024),
        name="finish",
    )(pops_mid, fill_mid, warm_mid, given[3])


def solution(mesh):
    in_specs = (
        P(None, "grp", None, "dev"),
        P("grp", None, "dev"),
        P("grp", None, "dev"),
        P(("grp", "dev"), None, None),
    )
    out_specs = (P(None, "grp", None, "dev"), P("grp", None, "dev"), P(("grp", "dev"), None, None))
    return jax.shard_map(shards, mesh=mesh, in_specs=in_specs, out_specs=out_specs, check_vma=False)
```

```python
import functools

import jax
import jax.numpy as jnp
from jax import lax
from jax.experimental import pallas as pl
from jax.experimental.pallas import tpu as pltpu
from jax.sharding import PartitionSpec as P

MESH = pl.DeviceIdType.MESH
F32 = jnp.float32
VELOCITIES = (
    (0, 0, 0),
    (1, 0, 0),
    (-1, 0, 0),
    (0, 1, 0),
    (0, -1, 0),
    (0, 0, 1),
    (0, 0, -1),
    (1, 1, 0),
    (-1, -1, 0),
    (1, -1, 0),
    (-1, 1, 0),
    (1, 0, 1),
    (-1, 0, -1),
    (1, 0, -1),
    (-1, 0, 1),
    (0, 1, 1),
    (0, -1, -1),
    (0, 1, -1),
    (0, -1, 1),
)
WEIGHTS = (1.0 / 3.0,) + (1.0 / 18.0,) * 6 + (1.0 / 36.0,) * 12
RELAX_TIME = 0.8
GRAVITY = -0.002
STEP_TIME = 0.2

NG, ND, NP, NY, NL = 4, 32, 32, 8, 128
FLAT = (1, 2, 3, 4, 7, 8, 9, 10)
UP = (5, 15, 18, 11, 14)
DOWN = (6, 16, 17, 13, 12)
CROSS = UP + DOWN
EAST = (1, 7, 9, 11, 13)
WEST = (2, 8, 10, 12, 14)
Z_PAIRS = (5, 11, 13, 15, 17)


FAR_FIRST = sorted(
    ((dz, dy, dc) for dz in range(4) for dy in range(4) for dc in range(2) if dz or dy or dc),
    key=lambda at: -(min(at[0], 4 - at[0]) + min(at[1], 4 - at[1])),
)


def opposite(q):
    return q + 1 if q % 2 == 1 else q - 1


def lane_iota():
    return lax.broadcasted_iota(jnp.int32, (NY, NL), 1)


def shift_rows(x, cy):
    return x if cy == 0 else pltpu.roll(x, cy % NY, 0)


def spread(x, lane):
    return jnp.broadcast_to(x[:, lane : lane + 1], (NY, NL))


def moments(d, s):
    out = []
    for axis in range(3):
        total = None
        for q, diff in d.items():
            c = VELOCITIES[q][axis]
            if c == 0:
                continue
            if total is None:
                total = diff if c > 0 else -diff
            else:
                total = total + diff if c > 0 else total - diff
        out.append(total)
    return out, sum(s.values())


def pack_columns(tops, bottoms, fill, p, acc, lane):
    spot = lane & 31
    here = spot == p
    east = lane == ((p + 1) & 31)
    west = lane == 32 + ((p + 31) & 31)
    out = []
    for side, (cols, edge) in enumerate(((tops, NL - 1), (bottoms, 0))):
        a, b = acc[2 * side], acc[2 * side + 1]
        v = spread(cols[0], edge)
        v = jnp.where(lane >= 32, spread(cols[1], edge), v)
        v = jnp.where(lane >= 64, spread(cols[2], edge), v)
        v = jnp.where(lane >= 96, spread(fill, edge), v)
        a = jnp.where(here, v, a)
        b = jnp.where(east, spread(cols[3], edge), b)
        b = jnp.where(west, spread(cols[4], edge), b)
        out += [a, b]
    return tuple(out)


def fluid_kernel(
    pops_in, fill_in, flags_in, energy_in,
    pops_out, fill_out, warm_out, ends_out,
    f0, f1, fz0, fz1, fz2, roll_z, halo_s, g_s, part, eqs, flags, vel, own_e, hot_msg, hbuf, heat_d,
    xs, xr, zs, zr, zd, msg, end_msg,
    load_sem, send_sem, recv_sem, hot_sem, back_sem, out_sem, group_sem, next_sem,
):
    g, d = lax.axis_index("grp"), lax.axis_index("dev")
    up, down = lax.rem(d + 1, ND), lax.rem(d + ND - 1, ND)
    east, west = lax.rem(g + 1, NG), lax.rem(g + NG - 1, NG)
    lane = lane_iota()
    row = lax.broadcasted_iota(jnp.int32, (NY, NL), 0)
    zero8 = jnp.zeros((NY, NL), F32)

    def load(src, dst, n):
        c = pltpu.make_async_copy(src, dst, load_sem.at[n])
        c.start()
        return c

    def load_pops(q, count, n):
        return load(pops_in.at[pl.ds(q, count)], f0.at[pl.ds(q, count), pl.ds(1, NP)], n)

    fill_load = load(fill_in, fz0.at[1, pl.ds(1, NP), pl.ds(8, 8)], 0)
    cross_loads = [load_pops(11, 8, 1), load_pops(5, 2, 2)]
    more_loads = [load_pops(0, 5, 3), load_pops(7, 4, 4), load(flags_in, flags, 5)]
    energy_load = load(energy_in.at[0], own_e.at[:, pl.ds(NL, ND * NL)], 6)

    z, y, core = lax.div(d, 8), lax.rem(lax.div(d, 2), 4), lax.rem(d, 2)
    barrier = pltpu.get_barrier_semaphore()
    column_peers = [(g, lax.rem(d + 8 * k, ND)) for k in range(1, 4)]
    x_peers = [(east, d), (west, d)]
    near = [(gg, dd) for dd in (up, down, d) for gg in (east, west)] + [(g, up), (g, down)]
    near += column_peers + [(g, 8 * z + lax.rem(d + k, 8)) for k in range(1, 8)]
    for to in near:
        pl.semaphore_signal(barrier, inc=1, device_id=to, device_id_type=MESH)

    def clear(p, c):
        for k in range(3):
            for ref in (fz0, fz1):
                ref[k, p, 0:8] = zero8
                ref[k, p, 16:24] = zero8
        fz2[p, 0:8] = zero8
        fz2[p, 16:24] = zero8
        return c

    lax.fori_loop(0, NP + 2, clear, 0)
    fz2[0, 8:16] = zero8
    fz2[NP + 1, 8:16] = zero8
    own_e[:, 0:NL] = zero8
    own_e[:, (ND + 1) * NL : (ND + 2) * NL] = zero8

    def send(t, src, dst, n, to):
        return pltpu.make_async_remote_copy(
            src_ref=src, dst_ref=dst, send_sem=send_sem.at[t, n], recv_sem=recv_sem.at[t, n],
            device_id=to, device_id_type=MESH,
        )

    def x_sends(t):
        return [
            send(t, xs.at[t, 0], xr.at[t, 0], 0, (east, d)),
            send(t, xs.at[t, 1], xr.at[t, 1], 1, (west, d)),
        ]

    def z_sends(t):
        return [
            send(t, zs.at[t, side], zr.at[t, side], 2 + side, (g, to))
            for side, to in ((0, up), (1, down))
        ]

    def corner_sends(t):
        return [
            send(t, zs.at[t, side], zd.at[t, side, k], 4 + 2 * side + k, (gg, to))
            for side, to in ((0, up), (1, down))
            for k, gg in ((0, east), (1, west))
        ]

    def fill_x(t, f, fz):
        for k, q in enumerate(EAST):
            xs[t, 0, k] = f[q, NP]
        xs[t, 0, 5] = fz[1, NP, 8:16]
        for k, q in enumerate(WEST):
            xs[t, 1, k] = f[q, 1]
        xs[t, 1, 5] = fz[1, 1, 8:16]

    def store_z(t, acc):
        for side in range(2):
            zs[t, side, 0:8] = acc[2 * side]
            zs[t, side, 8:16] = acc[2 * side + 1]

    def started(copies):
        for c in copies:
            c.start()
        return copies

    def arrived(copies):
        for c in copies:
            c.wait_recv()

    fill_load.wait()
    for c in cross_loads:
        c.wait()

    def pack0(p, acc):
        return pack_columns(
            [f0[q, p + 1] for q in UP], [f0[q, p + 1] for q in DOWN], fz0[1, p + 1, 8:16], p, acc, lane
        )

    acc0 = (zero8,) * 4
    store_z(0, lax.fori_loop(0, NP, pack0, acc0, unroll=8))

    pl.semaphore_wait(barrier, len(near))
    for to in column_peers:
        pl.semaphore_signal(group_sem, inc=1, device_id=to, device_id_type=MESH)

    corner0 = started(corner_sends(0))
    z0 = started(z_sends(0))
    for c in more_loads:
        c.wait()
    fill_x(0, f0, fz0)
    x0 = started(x_sends(0))

    def local_part(f, fz):
        def body(p):
            pops = [f[q, p + 1] for q in range(19)]
            kind = flags[p]
            gas = kind == 0
            fill = fz[1, p + 1, 8:16]
            diffs = {q: pops[q] - pops[q + 1] for q in range(1, 19, 2)}
            sums = {q: pops[q] + pops[q + 1] for q in range(1, 19, 2)}
            (mx, my, mz), total = moments(diffs, sums)
            dens = jnp.where(gas, 1.0, total + pops[0])
            inv = 1.0 / dens
            vx, vy, vz = mx * inv, my * inv, mz * inv
            base = 1.0 - 1.5 * (vx * vx + vy * vy + vz * vz)

            def paired(q):
                cx, cy, cz = VELOCITIES[q]
                along = None
                for c, v in ((cx, vx), (cy, vy), (cz, vz)):
                    if c:
                        along = (v if c > 0 else -v) if along is None else (along + v if c > 0 else along - v)
                return (2.0 * WEIGHTS[q]) * (base + 4.5 * along * along)

            for k, q in enumerate(Z_PAIRS):
                eqs[k, p] = paired(q)
            for k, q in enumerate(CROSS):
                roll_z[k, p + 1] = pltpu.roll(pops[q], 1 if q in UP else NL - 1, 1)
            fz[0, p + 1, 8:16] = pltpu.roll(fill, 1, 1)
            fz[2, p + 1, 8:16] = pltpu.roll(fill, NL - 1, 1)
            ex = None
            got = {0: pops[0]}
            for q in FLAT:
                cx, cy, _ = VELOCITIES[q]
                incoming = shift_rows(f[q, p + 1 - cx], cy)
                beside = fz[1, p + 1 - cx, 8 - cy : 16 - cy]
                empty = beside == 0.0
                back = pops[opposite(q)]
                got[q] = jnp.where(empty, paired(q if q % 2 else q - 1) - back, incoming)
                term = jnp.where(empty, 0.0, (fill + beside) * (incoming - back))
                ex = term if ex is None else ex + term
                g_s[q, p] = got[q]
            diffs = {q: got[q] - got[q + 1] for q in FLAT if q % 2}
            sums = {q: got[q] + got[q + 1] for q in FLAT if q % 2}
            (mx, my, _), total = moments(diffs, sums)
            part[0, p] = total + got[0]
            part[1, p] = mx
            part[2, p] = my
            part[3, p] = fill * dens + 0.5 * ex

        return body

    def local_inner(f, fz):
        body = local_part(f, fz)

        def inner(p, c):
            body(p)
            return c

        lax.fori_loop(1, NP - 1, inner, 0, unroll=6)

    def local_outer(t, f, fz):
        for k, q in enumerate(EAST):
            f[q, 0] = xr[t, 0, k]
        for k, q in enumerate(WEST):
            f[q, NP + 1] = xr[t, 1, k]
        fz[1, 0, 8:16] = jnp.where(g > 0, xr[t, 0, 5], 0.0)
        fz[1, NP + 1, 8:16] = jnp.where(g < NG - 1, xr[t, 1, 5], 0.0)
        for q in (11, 13):
            roll_z[CROSS.index(q), 0] = pltpu.roll(f[q, 0], 1 if q in UP else NL - 1, 1)
        for q in (12, 14):
            roll_z[CROSS.index(q), NP + 1] = pltpu.roll(f[q, NP + 1], 1 if q in UP else NL - 1, 1)
        body = local_part(f, fz)

        def outer(i, c):
            body(i * (NP - 1))
            return c

        lax.fori_loop(0, 2, outer, 0, unroll=2)

    def cross_part(f, fz, fill_ref, p):
        kind = flags[p]
        gas = kind == 0
        fill = fz[1, p + 1, 8:16]
        got = {}
        ex = None
        for side, dirs in enumerate((UP, DOWN)):
            edge = 0 if side == 0 else NL - 1
            for q in dirs:
                cx, cy, cz = VELOCITIES[q]
                k = CROSS.index(q)
                incoming = jnp.where(lane == edge, halo_s[k, p], roll_z[k, p + 1 - cx])
                incoming = shift_rows(incoming, cy)
                beside = fz[1 - cz, p + 1 - cx, 8 - cy : 16 - cy]
                empty = beside == 0.0
                back = f[opposite(q), p + 1]
                pair = q if q % 2 else q - 1
                got[q] = jnp.where(empty, eqs[Z_PAIRS.index(pair), p] - back, incoming)
                term = jnp.where(empty, 0.0, (fill + beside) * (incoming - back))
                ex = term if ex is None else ex + term
                g_s[q, p] = got[q]
        diffs = {q: got[q] - got[q + 1] for q in Z_PAIRS}
        sums = {q: got[q] + got[q + 1] for q in Z_PAIRS}
        (mx, my, mz), total = moments(diffs, sums)
        dens = jnp.where(gas, 1.0, total + part[0, p])
        inv = 1.0 / dens
        vel[0, p] = dens
        vel[1, p] = (mx + part[1, p]) * inv
        vel[2, p] = (my + part[2, p]) * inv
        vel[3, p] = mz * inv
        mass = part[3, p] + 0.5 * ex
        fill_ref[p + 1, 8:16] = jnp.where(
            kind == 2, 1.0, jnp.where(gas, 0.0, jnp.clip(mass * inv, 0.01, 1.0))
        )

    def cross(t, f, fz, fill_ref, corner):
        inside = (d > 0, d < ND - 1)
        fills = [jnp.where(inside[side], zr[t, side, 0:8], 0.0) for side in range(2)]

        def halos(p):
            for side, dirs in enumerate((UP, DOWN)):
                edge = 0 if side == 0 else NL - 1
                for k, q in enumerate(dirs):
                    spot = 32 * k if k < 3 else 32 * (k - 3)
                    rows = zr[t, side, 0:8] if k < 3 else zr[t, side, 8:16]
                    halo_s[CROSS.index(q), p] = pltpu.roll(rows, lax.rem(NL + edge - spot - p, NL), 1)

        def fill_columns(p):
            for side, edge, k in ((0, 0, 0), (1, NL - 1, 2)):
                new = pltpu.roll(fills[side], lax.rem(2 * NL + edge - 96 - p, NL), 1)
                fz[k, p + 1, 8:16] = jnp.where(lane == edge, new, fz[k, p + 1, 8:16])

        def prepare(base):
            for j in range(4):
                halos(base + j)
                fill_columns(base + j + 1)

        def work(base):
            for j in range(4):
                cross_part(f, fz, fill_ref, base + j)

        fill_columns(3)
        fill_columns(4)
        prepare(4)

        def mid(i, c):
            for base in (8 * i + 4, 8 * i + 8):
                work(base)
                prepare(base + 4)
            return c

        lax.fori_loop(0, NP // 8 - 1, mid, 0)

        arrived(corner)
        for side in range(2):
            b = jnp.where(lane == 0, zd[t, side, 0, 8:16], zr[t, side, 8:16])
            b = jnp.where(lane == 63, zd[t, side, 1, 8:16], b)
            zr[t, side, 8:16] = b
            edge, k, by = ((0, 0, 1), (NL - 1, 2, NL - 1))[side]
            for at, src, spot, ok in ((0, 0, 127, g > 0), (NP + 1, 1, 96, g < NG - 1)):
                old = pltpu.roll(fz[1, at, 8:16], by, 1)
                new = spread(zd[t, side, src, 0:8], spot)
                ok = jnp.logical_and(ok, inside[side])
                fz[k, at, 8:16] = jnp.where(lane == edge, jnp.where(ok, new, 0.0), old)
        for j in range(4):
            halos(j)
            halos(NP - 4 + j)
        for j in range(3):
            fill_columns(j)

        def last(i, c):
            work(i * (NP - 4))
            return c

        lax.fori_loop(0, 2, last, 0)

    def collide(f, p):
        gas = flags[p] == 0
        vx, vy, wz = vel[1, p], vel[2, p], vel[3, p] + RELAX_TIME * GRAVITY
        base = 1.0 - 1.5 * (vx * vx + vy * vy + wz * wz)
        keep = jnp.where(gas, 0.0, 1.0 - 1.0 / RELAX_TIME)
        scale = jnp.where(gas, 0.0, vel[0, p] * (1.0 / RELAX_TIME))
        new = {0: keep * f[0, p + 1] + (WEIGHTS[0] * scale) * base}
        by_weight = {w: (w * scale, 3.0 * w * scale) for w in (WEIGHTS[1], WEIGHTS[7])}
        for q in range(1, 19, 2):
            along = None
            for c, v in zip(VELOCITIES[q], (vx, vy, wz)):
                if c:
                    along = (v if c > 0 else -v) if along is None else (along + v if c > 0 else along - v)
            even_w, odd_w = by_weight[WEIGHTS[q]]
            even = even_w * (base + 4.5 * along * along)
            odd = odd_w * along
            new[q] = keep * g_s[q, p] + (even + odd)
            new[q + 1] = keep * g_s[q + 1, p] + (even - odd)
        return new

    local_inner(f0, fz0)

    energy_load.wait()

    def block_of(e):
        return own_e[:, pl.ds(pl.multiple_of((e + 1) * NL, NL), NL)]

    def hot_build(e, c):
        hot_msg[e, 0:8] = block_of(e)
        beside = jnp.where(lane == 0, pltpu.roll(block_of(e - 1), 1, 1), pltpu.roll(block_of(e + 1), NL - 1, 1))
        hot_msg[e, 8:16] = beside
        return c

    lax.fori_loop(0, ND, hot_build, 0, unroll=8)

    pl.semaphore_wait(group_sem, len(column_peers))
    for to in x_peers:
        pl.semaphore_signal(next_sem, inc=1, device_id=to, device_id_type=MESH)

    def hot_start(i, c):
        to = lax.rem(d + i, ND)
        pltpu.make_async_remote_copy(
            src_ref=hot_msg.at[to], dst_ref=hbuf.at[d + 1],
            send_sem=hot_sem.at[0], recv_sem=hot_sem.at[1], device_id=(g, to), device_id_type=MESH,
        ).start()
        return c

    lax.fori_loop(1, ND, hot_start, 0)
    own = pltpu.make_async_copy(hot_msg.at[d], hbuf.at[d + 1], load_sem.at[0])
    own.start()

    pl.semaphore_wait(next_sem, len(x_peers))

    def beyond(i, gg, at, sem):
        to = lax.rem(d + i, ND)
        return pltpu.make_async_remote_copy(
            src_ref=hot_msg.at[to, pl.ds(0, 8)], dst_ref=hbuf.at[at, pl.ds(0, 8)],
            send_sem=hot_sem.at[4], recv_sem=hot_sem.at[sem], device_id=(gg, to), device_id_type=MESH,
        )

    def beyond_all(gg, at, sem):
        def one(i, c):
            beyond(i, gg, at, sem).start()
            return c

        lax.fori_loop(0, ND, one, 0)

    @pl.when(d == ND - 1)
    def _():
        beyond_all(east, 0, 2)

    @pl.when(d == 0)
    def _():
        beyond_all(west, NP + 1, 3)

    arrived(x0)
    local_outer(0, f0, fz0)
    arrived(z0)
    cross(0, f0, fz0, fz1.at[1], corner0)

    def first(p, acc):
        new = collide(f0, p)
        for q in range(19):
            f1[q, p + 1] = new[q]
        return pack_columns([new[q] for q in UP], [new[q] for q in DOWN], fz1[1, p + 1, 8:16], p, acc, lane)

    store_z(1, lax.fori_loop(0, NP, first, acc0, unroll=8))
    corner1 = started(corner_sends(1))
    z1 = started(z_sends(1))
    fill_x(1, f1, fz1)
    x1 = started(x_sends(1))

    local_inner(f1, fz1)

    own.wait()
    pltpu.make_async_copy(hot_msg.at[pl.ds(0, ND - 1)], hot_msg.at[pl.ds(0, ND - 1)], hot_sem.at[1]).wait()
    beyond(0, east, 0, 2).wait_recv()
    beyond(0, west, NP + 1, 3).wait_recv()
    hbuf[0, 0:8] = jnp.where(g > 0, hbuf[0, 0:8], 0.0)
    hbuf[NP + 1, 0:8] = jnp.where(g < NG - 1, hbuf[NP + 1, 0:8], 0.0)

    def temp(h):
        return jnp.minimum(h, 1.0) + jnp.maximum(h - 1.5, 0.0)

    def differences(p, c):
        h = hbuf[p + 1, 0:8]
        edges = hbuf[p + 1, 8:16]
        others = (
            hbuf[p, 0:8], hbuf[p + 2, 0:8],
            jnp.where(row == 0, 0.0, pltpu.roll(h, 1, 0)), jnp.where(row == NY - 1, 0.0, pltpu.roll(h, NY - 1, 0)),
            jnp.where(lane == 0, edges, pltpu.roll(h, 1, 1)), jnp.where(lane == NL - 1, edges, pltpu.roll(h, NL - 1, 1)),
        )
        mine = temp(h)
        total = None
        for k, other in enumerate(others):
            dt = temp(other) - mine
            total = dt if total is None else total + dt
            heat_d[k, p] = dt * (0.05 * STEP_TIME)
            heat_d[6 + k, p] = (other - h) * STEP_TIME
        heat_d[12, p] = total * STEP_TIME
        return c

    lax.fori_loop(0, NP, differences, 0, unroll=8)

    arrived(x1)
    local_outer(1, f1, fz1)
    arrived(z1)
    cross(1, f1, fz1, fz2, corner1)

    end_msg[0] = -fz2[NP, 8:16] * heat_d[1, NP - 1]
    end_msg[1] = -fz2[1, 8:16] * heat_d[0, 0]
    end_sends = [
        pltpu.make_async_remote_copy(
            src_ref=end_msg.at[k], dst_ref=ends_out.at[k, d],
            send_sem=back_sem.at[2 + k], recv_sem=back_sem.at[4 + k], device_id=to, device_id_type=MESH,
        )
        for k, to in ((0, (east, 0)), (1, (west, ND - 1)))
    ]
    for c in end_sends:
        c.start()

    def transport(p, c):
        fill = fz2[p + 1, 8:16]
        beside = (
            fz2[p, 8:16], fz2[p + 2, 8:16], fz2[p + 1, 7:15], fz2[p + 1, 9:17],
            jnp.where(lane == 0, 0.0, pltpu.roll(fill, 1, 1)),
            jnp.where(lane == NL - 1, 0.0, pltpu.roll(fill, NL - 1, 1)),
        )
        out = hbuf[p + 1, 0:8] + (0.02 + 0.05 * fill) * heat_d[12, p]
        for k in range(6):
            out = out + beside[k] * heat_d[k, p]
        for a in range(3):
            v = vel[1 + a, p]
            out = out + jnp.maximum(v, 0.0) * heat_d[6 + 2 * a, p] - jnp.minimum(v, 0.0) * heat_d[7 + 2 * a, p]
        msg[p, 0:8] = out
        msg[p, 8:16] = fill
        return c

    lax.fori_loop(0, NP, transport, 0, unroll=8)

    for dz, dy, dc in FAR_FIRST:
        p = lax.rem(z + dz, 4) * 8 + lax.rem(y + dy, 4) * 2 + lax.rem(core + dc, 2)
        pltpu.make_async_remote_copy(
            src_ref=msg.at[p], dst_ref=warm_out.at[d],
            send_sem=back_sem.at[0], recv_sem=back_sem.at[1], device_id=(g, p), device_id_type=MESH,
        ).start()
    keep = pltpu.make_async_copy(msg.at[d], warm_out.at[d], load_sem.at[0])
    keep.start()
    fill_copy = pltpu.make_async_copy(fz2.at[pl.ds(1, NP), pl.ds(8, 8)], fill_out, out_sem.at[0])
    fill_copy.start()

    def second(p, c):
        new = collide(f1, p)
        for q in range(19):
            f0[q, p + 1] = new[q]
        return c

    lax.fori_loop(0, NP, second, 0, unroll=2)
    pops_copy = pltpu.make_async_copy(f0.at[:, pl.ds(1, NP)], pops_out, out_sem.at[1])
    pops_copy.start()

    for c in corner0 + z0 + x0 + corner1 + z1 + x1 + end_sends:
        c.wait_send()

    def all_of(ref, count, sem):
        part_of = ref.at[pl.ds(0, count)]
        pltpu.make_async_copy(part_of, part_of, sem).wait()

    all_of(hot_msg, ND - 1, hot_sem.at[0])

    @pl.when(d == 0)
    def _():
        all_of(hot_msg, ND // 2, hot_sem.at[4])

    @pl.when(d == ND - 1)
    def _():
        all_of(hot_msg, ND // 2, hot_sem.at[4])

    keep.wait()
    fill_copy.wait()
    pops_copy.wait()
    all_of(msg, ND - 1, back_sem.at[0])
    all_of(msg, ND - 1, back_sem.at[1])

    @pl.when(d == 0)
    def _():
        all_of(msg, ND // 2, back_sem.at[4])

    @pl.when(d == ND - 1)
    def _():
        all_of(msg, ND // 2, back_sem.at[5])


def finish_kernel(
    pops_mid, fill_mid, warm_mid, ends_mid, energy_in, pops_out, fill_out, energy_out, got, ends, own, done, sem
):
    g, d = lax.axis_index("grp"), lax.axis_index("dev")
    copies = [
        pltpu.make_async_copy(pops_mid, pops_out, sem.at[0]),
        pltpu.make_async_copy(warm_mid, got, sem.at[1]),
        pltpu.make_async_copy(energy_in, own, sem.at[2]),
        pltpu.make_async_copy(ends_mid, ends, sem.at[3]),
        pltpu.make_async_copy(fill_mid, fill_out, sem.at[4]),
    ]
    for c in copies:
        c.start()
    for c in copies[1:4]:
        c.wait()
    lane = lane_iota()
    low = jnp.logical_and(d == 0, g > 0)
    high = jnp.logical_and(d == ND - 1, g < NG - 1)

    def temp(h):
        return jnp.minimum(h, 1.0) + jnp.maximum(h - 1.5, 0.0)

    for e in range(ND):
        cells = slice(e * NL, (e + 1) * NL)
        out = got[e, 0:8] + jnp.where(low, ends[0, e], 0.0) + jnp.where(high, ends[1, e], 0.0)
        warmth = temp(own[0, :, cells])
        for side, other in ((0, e - 1), (1, e + 1)):
            if other < 0 or other >= ND:
                continue
            by, edge = (1, 0) if side == 0 else (NL - 1, NL - 1)
            beyond = temp(own[0, :, other * NL : (other + 1) * NL])
            term = pltpu.roll(got[other, 8:16], by, 1) * (pltpu.roll(beyond, by, 1) - warmth)
            out = out + jnp.where(lane == edge, (0.05 * STEP_TIME) * term, 0.0)
        done[0, :, cells] = out
    last = pltpu.make_async_copy(done, energy_out, sem.at[1])
    last.start()
    last.wait()
    copies[4].wait()
    copies[0].wait()


def shards(populations, fill, flags, specific_energy_grid):
    plane = (NY, NL)
    any_spec = pl.BlockSpec(memory_space=pl.ANY)
    hbm_spec = pl.BlockSpec(memory_space=pltpu.HBM)
    given = [
        pltpu.with_memory_space_constraint(x, pltpu.HBM)
        for x in (populations, fill, flags, specific_energy_grid)
    ]
    pops_mid, fill_mid, warm_mid, ends_mid = pl.pallas_call(
        fluid_kernel,
        out_shape=(
            jax.ShapeDtypeStruct((19, NP) + plane, F32),
            jax.ShapeDtypeStruct((NP,) + plane, F32),
            jax.ShapeDtypeStruct((ND, 16, NL), F32),
            jax.ShapeDtypeStruct((2, ND) + plane, F32),
        ),
        in_specs=[hbm_spec] * 4,
        out_specs=(any_spec,) * 4,
        scratch_shapes=[
            pltpu.VMEM((19, NP + 2) + plane, F32),
            pltpu.VMEM((19, NP + 2) + plane, F32),
            pltpu.VMEM((3, NP + 2, 24, NL), F32),
            pltpu.VMEM((3, NP + 2, 24, NL), F32),
            pltpu.VMEM((NP + 2, 24, NL), F32),
            pltpu.VMEM((10, NP + 2) + plane, F32),
            pltpu.VMEM((10, NP) + plane, F32),
            pltpu.VMEM((19, NP) + plane, F32),
            pltpu.VMEM((4, NP) + plane, F32),
            pltpu.VMEM((5, NP) + plane, F32),
            pltpu.VMEM((NP,) + plane, jnp.int32),
            pltpu.VMEM((4, NP) + plane, F32),
            pltpu.VMEM((NY, (ND + 2) * NL), F32),
            pltpu.VMEM((ND, 16, NL), F32),
            pltpu.VMEM((NP + 2, 16, NL), F32),
            pltpu.VMEM((13, NP) + plane, F32),
            pltpu.VMEM((2, 2, 6) + plane, F32),
            pltpu.VMEM((2, 2, 6) + plane, F32),
            pltpu.VMEM((2, 2, 16, NL), F32),
            pltpu.VMEM((2, 2, 16, NL), F32),
            pltpu.VMEM((2, 2, 2, 16, NL), F32),
            pltpu.VMEM((ND, 16, NL), F32),
            pltpu.VMEM((2,) + plane, F32),
            pltpu.SemaphoreType.DMA((7,)),
            pltpu.SemaphoreType.DMA((2, 8)),
            pltpu.SemaphoreType.DMA((2, 8)),
            pltpu.SemaphoreType.DMA((5,)),
            pltpu.SemaphoreType.DMA((6,)),
            pltpu.SemaphoreType.DMA((2,)),
            pltpu.SemaphoreType.REGULAR,
            pltpu.SemaphoreType.REGULAR,
        ],
        compiler_params=pltpu.CompilerParams(
            collective_id=0, has_side_effects=True, vmem_limit_bytes=40 * 1024 * 1024
        ),
        name="pour",
    )(*given)
    return pl.pallas_call(
        finish_kernel,
        out_shape=(
            jax.ShapeDtypeStruct((19, NP) + plane, F32),
            jax.ShapeDtypeStruct((NP,) + plane, F32),
            jax.ShapeDtypeStruct((1, NY, ND * NL), F32),
        ),
        in_specs=[any_spec] * 5,
        out_specs=(any_spec,) * 3,
        scratch_shapes=[
            pltpu.VMEM((ND, 16, NL), F32),
            pltpu.VMEM((2, ND) + plane, F32),
            pltpu.VMEM((1, NY, ND * NL), F32),
            pltpu.VMEM((1, NY, ND * NL), F32),
            pltpu.SemaphoreType.DMA((5,)),
        ],
        compiler_params=pltpu.CompilerParams(vmem_limit_bytes=8 * 1024 * 1024),
        name="finish",
    )(pops_mid, fill_mid, warm_mid, ends_mid, given[3])


def solution(mesh):
    in_specs = (
        P(None, "grp", None, "dev"),
        P("grp", None, "dev"),
        P("grp", None, "dev"),
        P(("grp", "dev"), None, None),
    )
    out_specs = (P(None, "grp", None, "dev"), P("grp", None, "dev"), P(("grp", "dev"), None, None))
    return jax.shard_map(shards, mesh=mesh, in_specs=in_specs, out_specs=out_specs, check_vma=False)
```

```python
import functools

import jax
import jax.numpy as jnp
from jax import lax
from jax.experimental import pallas as pl
from jax.experimental.pallas import tpu as pltpu
from jax.sharding import PartitionSpec as P

MESH = pl.DeviceIdType.MESH
F32 = jnp.float32
VELOCITIES = (
    (0, 0, 0),
    (1, 0, 0),
    (-1, 0, 0),
    (0, 1, 0),
    (0, -1, 0),
    (0, 0, 1),
    (0, 0, -1),
    (1, 1, 0),
    (-1, -1, 0),
    (1, -1, 0),
    (-1, 1, 0),
    (1, 0, 1),
    (-1, 0, -1),
    (1, 0, -1),
    (-1, 0, 1),
    (0, 1, 1),
    (0, -1, -1),
    (0, 1, -1),
    (0, -1, 1),
)
WEIGHTS = (1.0 / 3.0,) + (1.0 / 18.0,) * 6 + (1.0 / 36.0,) * 12
RELAX_TIME = 0.8
GRAVITY = -0.002
STEP_TIME = 0.2

NG, ND, NP, NY, NL = 4, 32, 32, 8, 128
FLAT = (1, 2, 3, 4, 7, 8, 9, 10)
UP = (5, 15, 18, 11, 14)
DOWN = (6, 17, 16, 13, 12)
CROSS = UP + DOWN
EAST = (1, 7, 9, 11, 13)
WEST = (2, 8, 10, 12, 14)
Z_PAIRS = (5, 11, 13, 15, 17)


def opposite(q):
    return q + 1 if q % 2 == 1 else q - 1


def lane_iota():
    return lax.broadcasted_iota(jnp.int32, (NY, NL), 1)


def shift_rows(x, cy):
    return x if cy == 0 else pltpu.roll(x, cy % NY, 0)


def spread(x, lane):
    return jnp.broadcast_to(x[:, lane : lane + 1], (NY, NL))


def moments(d, s):
    out = []
    for axis in range(3):
        total = None
        for q, diff in d.items():
            c = VELOCITIES[q][axis]
            if c == 0:
                continue
            if total is None:
                total = diff if c > 0 else -diff
            else:
                total = total + diff if c > 0 else total - diff
        out.append(total)
    return out, sum(s.values())


def pack_columns(ups, downs, fill, p, acc, lane):
    here = (lane >> 1) == p
    there = (lane >> 1) == p + 32

    def both(k):
        return jnp.where(lane == NL - 1, ups[k], downs[k])

    out = []
    for a, first, second in ((acc[0], both(0), both(1)), (acc[1], both(2), fill), (acc[2], both(3), both(4))):
        a = jnp.where(here, pltpu.roll(first, 2 * p + 1, 1), a)
        out.append(jnp.where(there, pltpu.roll(second, 2 * p + 65, 1), a))
    return tuple(out)


def fluid_kernel(
    pops_in, fill_in, flags_in, energy_in,
    pops_out, fill_out, warm_out, ends_out,
    f0, f1, fz0, fz1, fz2, roll_z, halo_s, columns, g_s, part, eqs, flags, vel, own_e, hot_msg, hbuf, heat_d,
    xs, xr, zs, zr, zd, msg, end_msg,
    load_sem, send_sem, recv_sem, hot_sem, back_sem, out_sem, group_sem, next_sem,
):
    g, d = lax.axis_index("grp"), lax.axis_index("dev")
    up, down = lax.rem(d + 1, ND), lax.rem(d + ND - 1, ND)
    east, west = lax.rem(g + 1, NG), lax.rem(g + NG - 1, NG)
    lane = lane_iota()
    row = lax.broadcasted_iota(jnp.int32, (NY, NL), 0)
    zero8 = jnp.zeros((NY, NL), F32)

    z, y, core = lax.div(d, 8), lax.rem(lax.div(d, 2), 4), lax.rem(d, 2)
    barrier = pltpu.get_barrier_semaphore()
    column_peers = [(g, lax.rem(d + 8 * k, ND)) for k in range(1, 4)]
    x_peers = [(east, d), (west, d)]
    near = [(gg, dd) for dd in (up, down, d) for gg in (east, west)] + [(g, up), (g, down)]
    near += column_peers + [(g, 8 * z + lax.rem(d + k, 8)) for k in range(1, 8)]
    for to in near:
        pl.semaphore_signal(barrier, inc=1, device_id=to, device_id_type=MESH)

    def load(src, dst, n):
        c = pltpu.make_async_copy(src, dst, load_sem.at[n])
        c.start()
        return c

    def load_pops(q, count, n):
        return load(pops_in.at[pl.ds(q, count)], f0.at[pl.ds(q, count), pl.ds(1, NP)], n)

    fill_load = load(fill_in, fz0.at[1, pl.ds(1, NP), pl.ds(8, 8)], 0)
    cross_loads = [load_pops(11, 8, 1), load_pops(5, 2, 2)]
    more_loads = [load_pops(0, 5, 3), load_pops(7, 4, 4), load(flags_in, flags, 5)]
    energy_load = load(energy_in.at[0], own_e.at[:, pl.ds(NL, ND * NL)], 6)

    def clear(p, c):
        for k in range(3):
            for ref in (fz0, fz1):
                ref[k, p, 0:8] = zero8
                ref[k, p, 16:24] = zero8
        fz2[p, 0:8] = zero8
        fz2[p, 16:24] = zero8
        return c

    lax.fori_loop(0, NP + 2, clear, 0)
    fz2[0, 8:16] = zero8
    fz2[NP + 1, 8:16] = zero8
    own_e[:, 0:NL] = zero8
    own_e[:, (ND + 1) * NL : (ND + 2) * NL] = zero8

    def send(t, src, dst, n, to):
        return pltpu.make_async_remote_copy(
            src_ref=src, dst_ref=dst, send_sem=send_sem.at[t, n], recv_sem=recv_sem.at[t, n],
            device_id=to, device_id_type=MESH,
        )

    def x_sends(t):
        return [
            send(t, xs.at[t, 0], xr.at[t, 0], 0, (east, d)),
            send(t, xs.at[t, 1], xr.at[t, 1], 1, (west, d)),
        ]

    def z_sends(t):
        return [
            send(t, zs.at[t], zr.at[t, side], 2 + side, (g, to))
            for side, to in ((0, up), (1, down))
        ]

    def corner_sends(t):
        return [
            send(t, zs.at[t], zd.at[t, side, k], 4 + 2 * side + k, (gg, to))
            for side, to in ((0, up), (1, down))
            for k, gg in ((0, east), (1, west))
        ]

    def fill_x(t, f, fz):
        for k, q in enumerate(EAST):
            xs[t, 0, k] = f[q, NP]
        xs[t, 0, 5] = fz[1, NP, 8:16]
        for k, q in enumerate(WEST):
            xs[t, 1, k] = f[q, 1]
        xs[t, 1, 5] = fz[1, 1, 8:16]

    def store_z(t, acc):
        for k in range(3):
            zs[t, 8 * k : 8 * k + 8] = acc[k]

    def started(copies):
        for c in copies:
            c.start()
        return copies

    def arrived(copies):
        for c in copies:
            c.wait_recv()

    fill_load.wait()
    for c in cross_loads:
        c.wait()

    def pack0(p, acc):
        return pack_columns(
            [f0[q, p + 1] for q in UP], [f0[q, p + 1] for q in DOWN], fz0[1, p + 1, 8:16], p, acc, lane
        )

    acc0 = (zero8,) * 3
    store_z(0, lax.fori_loop(0, NP, pack0, acc0, unroll=8))

    pl.semaphore_wait(barrier, len(near))
    for to in column_peers:
        pl.semaphore_signal(group_sem, inc=1, device_id=to, device_id_type=MESH)

    corner0 = started(corner_sends(0))
    z0 = started(z_sends(0))
    for c in more_loads:
        c.wait()
    fill_x(0, f0, fz0)
    x0 = started(x_sends(0))

    def local_part(f, fz):
        def body(p):
            pops = [f[q, p + 1] for q in range(19)]
            kind = flags[p]
            gas = kind == 0
            fill = fz[1, p + 1, 8:16]
            diffs = {q: pops[q] - pops[q + 1] for q in range(1, 19, 2)}
            sums = {q: pops[q] + pops[q + 1] for q in range(1, 19, 2)}
            (mx, my, mz), total = moments(diffs, sums)
            dens = jnp.where(gas, 1.0, total + pops[0])
            inv = 1.0 / dens
            vx, vy, vz = mx * inv, my * inv, mz * inv
            base = 1.0 - 1.5 * (vx * vx + vy * vy + vz * vz)

            def paired(q):
                cx, cy, cz = VELOCITIES[q]
                along = None
                for c, v in ((cx, vx), (cy, vy), (cz, vz)):
                    if c:
                        along = (v if c > 0 else -v) if along is None else (along + v if c > 0 else along - v)
                return (2.0 * WEIGHTS[q]) * (base + 4.5 * along * along)

            for k, q in enumerate(Z_PAIRS):
                eqs[k, p] = paired(q)
            for k, q in enumerate(CROSS):
                roll_z[k, p + 1] = pltpu.roll(pops[q], 1 if q in UP else NL - 1, 1)
            fz[0, p + 1, 8:16] = pltpu.roll(fill, 1, 1)
            fz[2, p + 1, 8:16] = pltpu.roll(fill, NL - 1, 1)
            ex = None
            got = {0: pops[0]}
            for q in FLAT:
                cx, cy, _ = VELOCITIES[q]
                incoming = shift_rows(f[q, p + 1 - cx], cy)
                beside = fz[1, p + 1 - cx, 8 - cy : 16 - cy]
                empty = beside == 0.0
                back = pops[opposite(q)]
                got[q] = jnp.where(empty, paired(q if q % 2 else q - 1) - back, incoming)
                term = jnp.where(empty, 0.0, (fill + beside) * (incoming - back))
                ex = term if ex is None else ex + term
                g_s[q, p] = got[q]
            diffs = {q: got[q] - got[q + 1] for q in FLAT if q % 2}
            sums = {q: got[q] + got[q + 1] for q in FLAT if q % 2}
            (mx, my, _), total = moments(diffs, sums)
            part[0, p] = total + got[0]
            part[1, p] = mx
            part[2, p] = my
            part[3, p] = fill * dens + 0.5 * ex

        return body

    def local_inner(f, fz):
        body = local_part(f, fz)

        def inner(p, c):
            body(p)
            return c

        lax.fori_loop(1, NP - 1, inner, 0, unroll=6)

    def local_outer(t, f, fz):
        for k, q in enumerate(EAST):
            f[q, 0] = xr[t, 0, k]
        for k, q in enumerate(WEST):
            f[q, NP + 1] = xr[t, 1, k]
        fz[1, 0, 8:16] = jnp.where(g > 0, xr[t, 0, 5], 0.0)
        fz[1, NP + 1, 8:16] = jnp.where(g < NG - 1, xr[t, 1, 5], 0.0)
        for q in (11, 13):
            roll_z[CROSS.index(q), 0] = pltpu.roll(f[q, 0], 1 if q in UP else NL - 1, 1)
        for q in (12, 14):
            roll_z[CROSS.index(q), NP + 1] = pltpu.roll(f[q, NP + 1], 1 if q in UP else NL - 1, 1)
        body = local_part(f, fz)

        def outer(i, c):
            body(i * (NP - 1))
            return c

        lax.fori_loop(0, 2, outer, 0, unroll=2)

    def cross_part(f, fz, fill_ref, p):
        kind = flags[p]
        gas = kind == 0
        fill = fz[1, p + 1, 8:16]
        got = {}
        ex = None
        for side, dirs in enumerate((UP, DOWN)):
            edge = 0 if side == 0 else NL - 1
            for q in dirs:
                cx, cy, cz = VELOCITIES[q]
                k = CROSS.index(q)
                incoming = jnp.where(lane == edge, halo_s[k % 5, p], roll_z[k, p + 1 - cx])
                incoming = shift_rows(incoming, cy)
                beside = fz[1 - cz, p + 1 - cx, 8 - cy : 16 - cy]
                empty = beside == 0.0
                back = f[opposite(q), p + 1]
                pair = q if q % 2 else q - 1
                got[q] = jnp.where(empty, eqs[Z_PAIRS.index(pair), p] - back, incoming)
                term = jnp.where(empty, 0.0, (fill + beside) * (incoming - back))
                ex = term if ex is None else ex + term
                g_s[q, p] = got[q]
        diffs = {q: got[q] - got[q + 1] for q in Z_PAIRS}
        sums = {q: got[q] + got[q + 1] for q in Z_PAIRS}
        (mx, my, mz), total = moments(diffs, sums)
        dens = jnp.where(gas, 1.0, total + part[0, p])
        inv = 1.0 / dens
        vel[0, p] = dens
        vel[1, p] = (mx + part[1, p]) * inv
        vel[2, p] = (my + part[2, p]) * inv
        vel[3, p] = mz * inv
        mass = part[3, p] + 0.5 * ex
        fill_ref[p + 1, 8:16] = jnp.where(
            kind == 2, 1.0, jnp.where(gas, 0.0, jnp.clip(mass * inv, 0.01, 1.0))
        )

    def cross(t, f, fz, fill_ref, corner):
        odd = (lane & 1) == 1
        inside = jnp.logical_or(jnp.logical_and(odd, d > 0), jnp.logical_and(jnp.logical_not(odd), d < ND - 1))

        def turned(low, high, k):
            rows = slice(8 * (k // 2), 8 * (k // 2) + 8)
            by = 64 * (k % 2)
            return jnp.where(odd, pltpu.roll(low[rows], by + 1, 1), pltpu.roll(high[rows], (by + NL - 1) % NL, 1))

        main = (zr.at[t, 0], zr.at[t, 1])
        for k, half in enumerate((0, 1, 2, 4, 5)):
            columns[k] = turned(*main, half)
        columns[5] = jnp.where(inside, turned(*main, 3), 0.0)

        def to_edges(k, p):
            return pltpu.roll(columns[k], lax.rem(2 * NL - 1 - 2 * p, NL), 1)

        def halos(p):
            for k in range(5):
                halo_s[k, p] = to_edges(k, p - VELOCITIES[UP[k]][0])

        def fill_columns(p):
            new = to_edges(5, p)
            for edge, k in ((0, 0), (NL - 1, 2)):
                fz[k, p + 1, 8:16] = jnp.where(lane == edge, new, fz[k, p + 1, 8:16])

        def prepare(base):
            for j in range(4):
                halos(base + j)
                fill_columns(base + j + 1)

        def work(base):
            for j in range(4):
                cross_part(f, fz, fill_ref, base + j)

        fill_columns(3)
        fill_columns(4)
        prepare(4)

        def mid(i, c):
            for base in (8 * i + 4, 8 * i + 8):
                work(base)
                prepare(base + 4)
            return c

        lax.fori_loop(0, NP // 8 - 1, mid, 0)

        arrived(corner)
        west_lanes, east_lanes = lane >= NL - 2, (lane >> 1) == 32
        last_of = (zd.at[t, 0, 0], zd.at[t, 1, 0])
        first_of = (zd.at[t, 0, 1], zd.at[t, 1, 1])
        columns[3] = jnp.where(west_lanes, pltpu.roll(turned(*last_of, 4), 64, 1), columns[3])
        columns[4] = jnp.where(east_lanes, pltpu.roll(turned(*first_of, 5), 64, 1), columns[4])
        fills = columns[5]
        ghost = jnp.where(jnp.logical_and(inside, g > 0), pltpu.roll(turned(*last_of, 3), 64, 1), 0.0)
        fills = jnp.where(west_lanes, ghost, fills)
        ghost = jnp.where(jnp.logical_and(inside, g < NG - 1), pltpu.roll(turned(*first_of, 3), 64, 1), 0.0)
        columns[5] = jnp.where(east_lanes, ghost, fills)
        for at in (0, NP + 1):
            fz[0, at, 8:16] = pltpu.roll(fz[1, at, 8:16], 1, 1)
            fz[2, at, 8:16] = pltpu.roll(fz[1, at, 8:16], NL - 1, 1)
        fill_columns(-1)
        fill_columns(NP)
        for j in range(4):
            halos(j)
            halos(NP - 4 + j)
        for j in range(3):
            fill_columns(j)

        def last(i, c):
            work(i * (NP - 4))
            return c

        lax.fori_loop(0, 2, last, 0)

    def collide(f, p):
        gas = flags[p] == 0
        vx, vy, wz = vel[1, p], vel[2, p], vel[3, p] + RELAX_TIME * GRAVITY
        base = 1.0 - 1.5 * (vx * vx + vy * vy + wz * wz)
        keep = jnp.where(gas, 0.0, 1.0 - 1.0 / RELAX_TIME)
        scale = jnp.where(gas, 0.0, vel[0, p] * (1.0 / RELAX_TIME))
        new = {0: keep * f[0, p + 1] + (WEIGHTS[0] * scale) * base}
        by_weight = {w: (w * scale, 3.0 * w * scale) for w in (WEIGHTS[1], WEIGHTS[7])}
        for q in range(1, 19, 2):
            along = None
            for c, v in zip(VELOCITIES[q], (vx, vy, wz)):
                if c:
                    along = (v if c > 0 else -v) if along is None else (along + v if c > 0 else along - v)
            even_w, odd_w = by_weight[WEIGHTS[q]]
            even = even_w * (base + 4.5 * along * along)
            odd = odd_w * along
            new[q] = keep * g_s[q, p] + (even + odd)
            new[q + 1] = keep * g_s[q + 1, p] + (even - odd)
        return new

    local_inner(f0, fz0)

    energy_load.wait()

    def block_of(e):
        return own_e[:, pl.ds(pl.multiple_of((e + 1) * NL, NL), NL)]

    def hot_build(e, c):
        hot_msg[e, 0:8] = block_of(e)
        beside = jnp.where(lane == 0, pltpu.roll(block_of(e - 1), 1, 1), pltpu.roll(block_of(e + 1), NL - 1, 1))
        hot_msg[e, 8:16] = beside
        return c

    lax.fori_loop(0, ND, hot_build, 0, unroll=8)

    pl.semaphore_wait(group_sem, len(column_peers))
    for to in x_peers:
        pl.semaphore_signal(next_sem, inc=1, device_id=to, device_id_type=MESH)

    def hot_start(i, c):
        to = lax.rem(d + i, ND)
        pltpu.make_async_remote_copy(
            src_ref=hot_msg.at[to], dst_ref=hbuf.at[d + 1],
            send_sem=hot_sem.at[0], recv_sem=hot_sem.at[1], device_id=(g, to), device_id_type=MESH,
        ).start()
        return c

    lax.fori_loop(1, ND, hot_start, 0)
    own = pltpu.make_async_copy(hot_msg.at[d], hbuf.at[d + 1], load_sem.at[0])
    own.start()

    pl.semaphore_wait(next_sem, len(x_peers))

    def beyond(i, gg, at, sem):
        to = lax.rem(d + i, ND)
        return pltpu.make_async_remote_copy(
            src_ref=hot_msg.at[to, pl.ds(0, 8)], dst_ref=hbuf.at[at, pl.ds(0, 8)],
            send_sem=hot_sem.at[4], recv_sem=hot_sem.at[sem], device_id=(gg, to), device_id_type=MESH,
        )

    def beyond_all(gg, at, sem):
        def one(i, c):
            beyond(i, gg, at, sem).start()
            return c

        lax.fori_loop(0, ND, one, 0)

    @pl.when(d == ND - 1)
    def _():
        beyond_all(east, 0, 2)

    @pl.when(d == 0)
    def _():
        beyond_all(west, NP + 1, 3)

    arrived(x0)
    local_outer(0, f0, fz0)
    arrived(z0)
    cross(0, f0, fz0, fz1.at[1], corner0)

    def first(p, acc):
        new = collide(f0, p)
        for q in range(19):
            f1[q, p + 1] = new[q]
        return pack_columns([new[q] for q in UP], [new[q] for q in DOWN], fz1[1, p + 1, 8:16], p, acc, lane)

    store_z(1, lax.fori_loop(0, NP, first, acc0, unroll=8))
    corner1 = started(corner_sends(1))
    z1 = started(z_sends(1))
    fill_x(1, f1, fz1)
    x1 = started(x_sends(1))

    local_inner(f1, fz1)

    own.wait()
    pltpu.make_async_copy(hot_msg.at[pl.ds(0, ND - 1)], hot_msg.at[pl.ds(0, ND - 1)], hot_sem.at[1]).wait()
    beyond(0, east, 0, 2).wait_recv()
    beyond(0, west, NP + 1, 3).wait_recv()
    hbuf[0, 0:8] = jnp.where(g > 0, hbuf[0, 0:8], 0.0)
    hbuf[NP + 1, 0:8] = jnp.where(g < NG - 1, hbuf[NP + 1, 0:8], 0.0)

    def temp(h):
        return jnp.minimum(h, 1.0) + jnp.maximum(h - 1.5, 0.0)

    def differences(p, c):
        h = hbuf[p + 1, 0:8]
        edges = hbuf[p + 1, 8:16]
        others = (
            hbuf[p, 0:8], hbuf[p + 2, 0:8],
            jnp.where(row == 0, 0.0, pltpu.roll(h, 1, 0)), jnp.where(row == NY - 1, 0.0, pltpu.roll(h, NY - 1, 0)),
            jnp.where(lane == 0, edges, pltpu.roll(h, 1, 1)), jnp.where(lane == NL - 1, edges, pltpu.roll(h, NL - 1, 1)),
        )
        mine = temp(h)
        total = None
        for k, other in enumerate(others):
            dt = temp(other) - mine
            total = dt if total is None else total + dt
            heat_d[k, p] = dt * (0.05 * STEP_TIME)
            heat_d[6 + k, p] = (other - h) * STEP_TIME
        heat_d[12, p] = total * STEP_TIME
        return c

    lax.fori_loop(0, NP, differences, 0, unroll=8)

    arrived(x1)
    local_outer(1, f1, fz1)
    arrived(z1)
    cross(1, f1, fz1, fz2, corner1)

    end_msg[0] = -fz2[NP, 8:16] * heat_d[1, NP - 1]
    end_msg[1] = -fz2[1, 8:16] * heat_d[0, 0]
    end_sends = [
        pltpu.make_async_remote_copy(
            src_ref=end_msg.at[k], dst_ref=ends_out.at[k, d],
            send_sem=back_sem.at[2 + k], recv_sem=back_sem.at[4 + k], device_id=to, device_id_type=MESH,
        )
        for k, to in ((0, (east, 0)), (1, (west, ND - 1)))
    ]
    for c in end_sends:
        c.start()

    def transport(p, c):
        fill = fz2[p + 1, 8:16]
        beside = (
            fz2[p, 8:16], fz2[p + 2, 8:16], fz2[p + 1, 7:15], fz2[p + 1, 9:17],
            jnp.where(lane == 0, 0.0, pltpu.roll(fill, 1, 1)),
            jnp.where(lane == NL - 1, 0.0, pltpu.roll(fill, NL - 1, 1)),
        )
        out = hbuf[p + 1, 0:8] + (0.02 + 0.05 * fill) * heat_d[12, p]
        for k in range(6):
            out = out + beside[k] * heat_d[k, p]
        for a in range(3):
            v = vel[1 + a, p]
            out = out + jnp.maximum(v, 0.0) * heat_d[6 + 2 * a, p] - jnp.minimum(v, 0.0) * heat_d[7 + 2 * a, p]
        msg[p, 0:8] = out
        msg[p, 8:16] = fill
        return c

    for dz in (2, 1, 3, 0):
        z_to = lax.rem(z + dz, 4)
        for j in range(8):
            transport(8 * z_to + j, 0)
        for dy, dc in ((2, 0), (2, 1), (1, 0), (1, 1), (3, 0), (3, 1), (0, 1), (0, 0)):
            if dz or dy or dc:
                p = 8 * z_to + lax.rem(y + dy, 4) * 2 + lax.rem(core + dc, 2)
                pltpu.make_async_remote_copy(
                    src_ref=msg.at[p], dst_ref=warm_out.at[d],
                    send_sem=back_sem.at[0], recv_sem=back_sem.at[1], device_id=(g, p), device_id_type=MESH,
                ).start()
    keep = pltpu.make_async_copy(msg.at[d], warm_out.at[d], load_sem.at[0])
    keep.start()
    fill_copy = pltpu.make_async_copy(fz2.at[pl.ds(1, NP), pl.ds(8, 8)], fill_out, out_sem.at[0])
    fill_copy.start()

    def second(p, c):
        new = collide(f1, p)
        for q in range(19):
            f0[q, p + 1] = new[q]
        return c

    pops_copies = []
    for base in range(0, NP, 8):
        lax.fori_loop(base, base + 8, second, 0, unroll=4)
        pops_copies.append(
            pltpu.make_async_copy(
                f0.at[:, pl.ds(1 + base, 8)], pops_out.at[:, pl.ds(base, 8)], out_sem.at[1 + base // 8]
            )
        )
        pops_copies[-1].start()

    for c in corner0 + z0 + x0 + corner1 + z1 + x1 + end_sends:
        c.wait_send()

    def all_of(ref, count, sem):
        part_of = ref.at[pl.ds(0, count)]
        pltpu.make_async_copy(part_of, part_of, sem).wait()

    all_of(hot_msg, ND - 1, hot_sem.at[0])

    @pl.when(d == 0)
    def _():
        all_of(hot_msg, ND // 2, hot_sem.at[4])

    @pl.when(d == ND - 1)
    def _():
        all_of(hot_msg, ND // 2, hot_sem.at[4])

    keep.wait()
    fill_copy.wait()
    for c in pops_copies:
        c.wait()
    all_of(msg, ND - 1, back_sem.at[0])
    all_of(msg, ND - 1, back_sem.at[1])

    @pl.when(d == 0)
    def _():
        all_of(msg, ND // 2, back_sem.at[4])

    @pl.when(d == ND - 1)
    def _():
        all_of(msg, ND // 2, back_sem.at[5])


def finish_kernel(
    pops_mid, fill_mid, warm_mid, ends_mid, energy_in, pops_out, fill_out, energy_out, got, ends, own, done, sem
):
    g, d = lax.axis_index("grp"), lax.axis_index("dev")
    copies = [
        pltpu.make_async_copy(pops_mid, pops_out, sem.at[0]),
        pltpu.make_async_copy(warm_mid, got, sem.at[1]),
        pltpu.make_async_copy(energy_in, own, sem.at[2]),
        pltpu.make_async_copy(ends_mid, ends, sem.at[3]),
        pltpu.make_async_copy(fill_mid, fill_out, sem.at[4]),
    ]
    for c in copies:
        c.start()
    for c in copies[1:4]:
        c.wait()
    lane = lane_iota()
    low = jnp.logical_and(d == 0, g > 0)
    high = jnp.logical_and(d == ND - 1, g < NG - 1)

    def temp(h):
        return jnp.minimum(h, 1.0) + jnp.maximum(h - 1.5, 0.0)

    halves = []
    for e in range(ND):
        cells = slice(e * NL, (e + 1) * NL)
        out = got[e, 0:8] + jnp.where(low, ends[0, e], 0.0) + jnp.where(high, ends[1, e], 0.0)
        warmth = temp(own[0, :, cells])
        for side, other in ((0, e - 1), (1, e + 1)):
            if other < 0 or other >= ND:
                continue
            by, edge = (1, 0) if side == 0 else (NL - 1, NL - 1)
            beyond = temp(own[0, :, other * NL : (other + 1) * NL])
            term = pltpu.roll(got[other, 8:16], by, 1) * (pltpu.roll(beyond, by, 1) - warmth)
            out = out + jnp.where(lane == edge, (0.05 * STEP_TIME) * term, 0.0)
        done[0, :, cells] = out
        if e % (ND // 2) == ND // 2 - 1:
            half = pl.ds((e // (ND // 2)) * (ND // 2) * NL, ND // 2 * NL)
            halves.append(
                pltpu.make_async_copy(done.at[:, :, half], energy_out.at[:, :, half], sem.at[1 + len(halves)])
            )
            halves[-1].start()
    for c in halves:
        c.wait()
    copies[4].wait()
    copies[0].wait()


def shards(populations, fill, flags, specific_energy_grid):
    plane = (NY, NL)
    any_spec = pl.BlockSpec(memory_space=pl.ANY)
    hbm_spec = pl.BlockSpec(memory_space=pltpu.HBM)
    given = [
        pltpu.with_memory_space_constraint(x, pltpu.HBM)
        for x in (populations, fill, flags, specific_energy_grid)
    ]
    pops_mid, fill_mid, warm_mid, ends_mid = pl.pallas_call(
        fluid_kernel,
        out_shape=(
            jax.ShapeDtypeStruct((19, NP) + plane, F32),
            jax.ShapeDtypeStruct((NP,) + plane, F32),
            jax.ShapeDtypeStruct((ND, 16, NL), F32),
            jax.ShapeDtypeStruct((2, ND) + plane, F32),
        ),
        in_specs=[hbm_spec] * 4,
        out_specs=(any_spec,) * 4,
        scratch_shapes=[
            pltpu.VMEM((19, NP + 2) + plane, F32),
            pltpu.VMEM((19, NP + 2) + plane, F32),
            pltpu.VMEM((3, NP + 2, 24, NL), F32),
            pltpu.VMEM((3, NP + 2, 24, NL), F32),
            pltpu.VMEM((NP + 2, 24, NL), F32),
            pltpu.VMEM((10, NP + 2) + plane, F32),
            pltpu.VMEM((5, NP) + plane, F32),
            pltpu.VMEM((6,) + plane, F32),
            pltpu.VMEM((19, NP) + plane, F32),
            pltpu.VMEM((4, NP) + plane, F32),
            pltpu.VMEM((5, NP) + plane, F32),
            pltpu.VMEM((NP,) + plane, jnp.int32),
            pltpu.VMEM((4, NP) + plane, F32),
            pltpu.VMEM((NY, (ND + 2) * NL), F32),
            pltpu.VMEM((ND, 16, NL), F32),
            pltpu.VMEM((NP + 2, 16, NL), F32),
            pltpu.VMEM((13, NP) + plane, F32),
            pltpu.VMEM((2, 2, 6) + plane, F32),
            pltpu.VMEM((2, 2, 6) + plane, F32),
            pltpu.VMEM((2, 24, NL), F32),
            pltpu.VMEM((2, 2, 24, NL), F32),
            pltpu.VMEM((2, 2, 2, 24, NL), F32),
            pltpu.VMEM((ND, 16, NL), F32),
            pltpu.VMEM((2,) + plane, F32),
            pltpu.SemaphoreType.DMA((7,)),
            pltpu.SemaphoreType.DMA((2, 8)),
            pltpu.SemaphoreType.DMA((2, 8)),
            pltpu.SemaphoreType.DMA((5,)),
            pltpu.SemaphoreType.DMA((6,)),
            pltpu.SemaphoreType.DMA((5,)),
            pltpu.SemaphoreType.REGULAR,
            pltpu.SemaphoreType.REGULAR,
        ],
        compiler_params=pltpu.CompilerParams(
            collective_id=0, has_side_effects=True, vmem_limit_bytes=40 * 1024 * 1024
        ),
        name="pour",
    )(*given)
    return pl.pallas_call(
        finish_kernel,
        out_shape=(
            jax.ShapeDtypeStruct((19, NP) + plane, F32),
            jax.ShapeDtypeStruct((NP,) + plane, F32),
            jax.ShapeDtypeStruct((1, NY, ND * NL), F32),
        ),
        in_specs=[any_spec] * 5,
        out_specs=(any_spec,) * 3,
        scratch_shapes=[
            pltpu.VMEM((ND, 16, NL), F32),
            pltpu.VMEM((2, ND) + plane, F32),
            pltpu.VMEM((1, NY, ND * NL), F32),
            pltpu.VMEM((1, NY, ND * NL), F32),
            pltpu.SemaphoreType.DMA((5,)),
        ],
        compiler_params=pltpu.CompilerParams(vmem_limit_bytes=8 * 1024 * 1024),
        name="finish",
    )(pops_mid, fill_mid, warm_mid, ends_mid, given[3])


def solution(mesh):
    in_specs = (
        P(None, "grp", None, "dev"),
        P("grp", None, "dev"),
        P("grp", None, "dev"),
        P(("grp", "dev"), None, None),
    )
    out_specs = (P(None, "grp", None, "dev"), P("grp", None, "dev"), P(("grp", "dev"), None, None))
    return jax.shard_map(shards, mesh=mesh, in_specs=in_specs, out_specs=out_specs, check_vma=False)
```

```python
import functools

import jax
import jax.numpy as jnp
from jax import lax
from jax.experimental import pallas as pl
from jax.experimental.pallas import tpu as pltpu
from jax.sharding import PartitionSpec as P

MESH = pl.DeviceIdType.MESH
F32 = jnp.float32
VELOCITIES = (
    (0, 0, 0),
    (1, 0, 0),
    (-1, 0, 0),
    (0, 1, 0),
    (0, -1, 0),
    (0, 0, 1),
    (0, 0, -1),
    (1, 1, 0),
    (-1, -1, 0),
    (1, -1, 0),
    (-1, 1, 0),
    (1, 0, 1),
    (-1, 0, -1),
    (1, 0, -1),
    (-1, 0, 1),
    (0, 1, 1),
    (0, -1, -1),
    (0, 1, -1),
    (0, -1, 1),
)
WEIGHTS = (1.0 / 3.0,) + (1.0 / 18.0,) * 6 + (1.0 / 36.0,) * 12
RELAX_TIME = 0.8
GRAVITY = -0.002
STEP_TIME = 0.2

NG, ND, NP, NY, NL = 4, 32, 32, 8, 128
FLAT = (1, 2, 3, 4, 7, 8, 9, 10)
UP = (5, 15, 18, 11, 14)
DOWN = (6, 17, 16, 13, 12)
CROSS = UP + DOWN
EAST = (1, 7, 9, 11, 13)
WEST = (2, 8, 10, 12, 14)
Z_PAIRS = (5, 11, 13, 15, 17)


FAR_FIRST = sorted(
    ((dz, dy) for dz in range(4) for dy in range(4)),
    key=lambda at: -(min(at[0], 4 - at[0]) + min(at[1], 4 - at[1])),
)


def opposite(q):
    return q + 1 if q % 2 == 1 else q - 1


def lane_iota():
    return lax.broadcasted_iota(jnp.int32, (NY, NL), 1)


def shift_rows(x, cy):
    return x if cy == 0 else pltpu.roll(x, cy % NY, 0)


def spread(x, lane):
    return jnp.broadcast_to(x[:, lane : lane + 1], (NY, NL))


def moments(d, s):
    out = []
    for axis in range(3):
        total = None
        for q, diff in d.items():
            c = VELOCITIES[q][axis]
            if c == 0:
                continue
            if total is None:
                total = diff if c > 0 else -diff
            else:
                total = total + diff if c > 0 else total - diff
        out.append(total)
    return out, sum(s.values())


def pack_columns(ups, downs, fill, p, acc, lane):
    here = (lane >> 1) == p
    there = (lane >> 1) == p + 32

    def both(k):
        return jnp.where(lane == NL - 1, ups[k], downs[k])

    out = []
    for a, first, second in ((acc[0], both(0), both(1)), (acc[1], both(2), fill), (acc[2], both(3), both(4))):
        a = jnp.where(here, pltpu.roll(first, 2 * p + 1, 1), a)
        out.append(jnp.where(there, pltpu.roll(second, 2 * p + 65, 1), a))
    return tuple(out)


def fluid_kernel(
    pops_in, fill_in, flags_in, energy_in,
    pops_out, fill_out, warm_out, ends_out,
    f0, f1, fz0, fz1, fz2, roll_z, halo_s, columns, g_s, part, eqs, flags, vel, own_e, hot_msg, hbuf, heat_d,
    xs, xr, zs, zr, zd, msg, end_msg,
    load_sem, send_sem, recv_sem, hot_sem, back_sem, out_sem, next_sem,
):
    g, d = lax.axis_index("grp"), lax.axis_index("dev")
    up, down = lax.rem(d + 1, ND), lax.rem(d + ND - 1, ND)
    east, west = lax.rem(g + 1, NG), lax.rem(g + NG - 1, NG)
    lane = lane_iota()
    row = lax.broadcasted_iota(jnp.int32, (NY, NL), 0)
    zero8 = jnp.zeros((NY, NL), F32)

    z, y, core = lax.div(d, 8), lax.rem(lax.div(d, 2), 4), lax.rem(d, 2)
    barrier = pltpu.get_barrier_semaphore()
    x_peers = [(east, d), (west, d)]
    near = [(gg, dd) for dd in (up, down) for gg in (east, west)]
    for dz, dy in FAR_FIRST:
        for dc in range(2):
            if dz or dy or dc:
                to = lax.rem(z + dz, 4) * 8 + lax.rem(y + dy, 4) * 2 + lax.rem(core + dc, 2)
                near.append((g, to))
    near += x_peers
    for to in near:
        pl.semaphore_signal(barrier, inc=1, device_id=to, device_id_type=MESH)

    def load(src, dst, n):
        c = pltpu.make_async_copy(src, dst, load_sem.at[n])
        c.start()
        return c

    def load_pops(q, count, n):
        return load(pops_in.at[pl.ds(q, count)], f0.at[pl.ds(q, count), pl.ds(1, NP)], n)

    fill_load = load(fill_in, fz0.at[1, pl.ds(1, NP), pl.ds(8, 8)], 0)
    cross_loads = [load_pops(11, 8, 1), load_pops(5, 2, 2)]
    more_loads = [load_pops(0, 5, 3), load_pops(7, 4, 4), load(flags_in, flags, 5)]
    energy_load = load(energy_in.at[0], own_e.at[:, pl.ds(NL, ND * NL)], 6)

    def clear(p, c):
        for k in range(3):
            for ref in (fz0, fz1):
                ref[k, p, 0:8] = zero8
                ref[k, p, 16:24] = zero8
        fz2[p, 0:8] = zero8
        fz2[p, 16:24] = zero8
        return c

    lax.fori_loop(0, NP + 2, clear, 0)
    fz2[0, 8:16] = zero8
    fz2[NP + 1, 8:16] = zero8
    own_e[:, 0:NL] = zero8
    own_e[:, (ND + 1) * NL : (ND + 2) * NL] = zero8

    def send(t, src, dst, n, to):
        return pltpu.make_async_remote_copy(
            src_ref=src, dst_ref=dst, send_sem=send_sem.at[t, n], recv_sem=recv_sem.at[t, n],
            device_id=to, device_id_type=MESH,
        )

    def x_sends(t):
        return [
            send(t, xs.at[t, 0], xr.at[t, 0], 0, (east, d)),
            send(t, xs.at[t, 1], xr.at[t, 1], 1, (west, d)),
        ]

    def z_sends(t):
        return [
            send(t, zs.at[t], zr.at[t, side], 2 + side, (g, to))
            for side, to in ((0, up), (1, down))
        ]

    def corner_sends(t):
        return [
            send(t, zs.at[t], zd.at[t, side, k], 4 + 2 * side + k, (gg, to))
            for side, to in ((0, up), (1, down))
            for k, gg in ((0, east), (1, west))
        ]

    def fill_x(t, f, fz):
        for k, q in enumerate(EAST):
            xs[t, 0, k] = f[q, NP]
        xs[t, 0, 5] = fz[1, NP, 8:16]
        for k, q in enumerate(WEST):
            xs[t, 1, k] = f[q, 1]
        xs[t, 1, 5] = fz[1, 1, 8:16]

    def store_z(t, acc):
        for k in range(3):
            zs[t, 8 * k : 8 * k + 8] = acc[k]

    def started(copies):
        for c in copies:
            c.start()
        return copies

    def arrived(copies):
        for c in copies:
            c.wait_recv()

    fill_load.wait()
    for c in cross_loads:
        c.wait()

    def pack0(p, acc):
        return pack_columns(
            [f0[q, p + 1] for q in UP], [f0[q, p + 1] for q in DOWN], fz0[1, p + 1, 8:16], p, acc, lane
        )

    acc0 = (zero8,) * 3
    store_z(0, lax.fori_loop(0, NP, pack0, acc0, unroll=8))

    energy_load.wait()

    def block_of(e):
        return own_e[:, pl.ds(pl.multiple_of((e + 1) * NL, NL), NL)]

    def hot_build(e, c):
        hot_msg[e, 0:8] = block_of(e)
        beside = jnp.where(lane == 0, pltpu.roll(block_of(e - 1), 1, 1), pltpu.roll(block_of(e + 1), NL - 1, 1))
        hot_msg[e, 8:16] = beside
        return c

    lax.fori_loop(0, ND, hot_build, 0, unroll=8)

    pl.semaphore_wait(barrier, len(near))
    for to in x_peers:
        pl.semaphore_signal(next_sem, inc=1, device_id=to, device_id_type=MESH)

    corner0 = started(corner_sends(0))
    z0 = started(z_sends(0))
    for c in more_loads:
        c.wait()
    fill_x(0, f0, fz0)
    x0 = started(x_sends(0))

    def hot_start(i, c):
        to = lax.rem(d + i, ND)
        pltpu.make_async_remote_copy(
            src_ref=hot_msg.at[to], dst_ref=hbuf.at[d + 1],
            send_sem=hot_sem.at[0], recv_sem=hot_sem.at[1], device_id=(g, to), device_id_type=MESH,
        ).start()
        return c

    lax.fori_loop(1, ND, hot_start, 0)
    own = pltpu.make_async_copy(hot_msg.at[d], hbuf.at[d + 1], load_sem.at[0])
    own.start()


    def local_part(f, fz):
        def body(p):
            pops = [f[q, p + 1] for q in range(19)]
            kind = flags[p]
            gas = kind == 0
            fill = fz[1, p + 1, 8:16]
            diffs = {q: pops[q] - pops[q + 1] for q in range(1, 19, 2)}
            sums = {q: pops[q] + pops[q + 1] for q in range(1, 19, 2)}
            (mx, my, mz), total = moments(diffs, sums)
            dens = jnp.where(gas, 1.0, total + pops[0])
            inv = 1.0 / dens
            vx, vy, vz = mx * inv, my * inv, mz * inv
            base = 1.0 - 1.5 * (vx * vx + vy * vy + vz * vz)

            def paired(q):
                cx, cy, cz = VELOCITIES[q]
                along = None
                for c, v in ((cx, vx), (cy, vy), (cz, vz)):
                    if c:
                        along = (v if c > 0 else -v) if along is None else (along + v if c > 0 else along - v)
                return (2.0 * WEIGHTS[q]) * (base + 4.5 * along * along)

            for k, q in enumerate(Z_PAIRS):
                eqs[k, p] = paired(q)
            for k, q in enumerate(CROSS):
                roll_z[k, p + 1] = pltpu.roll(pops[q], 1 if q in UP else NL - 1, 1)
            fz[0, p + 1, 8:16] = pltpu.roll(fill, 1, 1)
            fz[2, p + 1, 8:16] = pltpu.roll(fill, NL - 1, 1)
            ex = None
            got = {0: pops[0]}
            for q in FLAT:
                cx, cy, _ = VELOCITIES[q]
                incoming = shift_rows(f[q, p + 1 - cx], cy)
                beside = fz[1, p + 1 - cx, 8 - cy : 16 - cy]
                empty = beside == 0.0
                back = pops[opposite(q)]
                got[q] = jnp.where(empty, paired(q if q % 2 else q - 1) - back, incoming)
                term = jnp.where(empty, 0.0, (fill + beside) * (incoming - back))
                ex = term if ex is None else ex + term
                g_s[q, p] = got[q]
            diffs = {q: got[q] - got[q + 1] for q in FLAT if q % 2}
            sums = {q: got[q] + got[q + 1] for q in FLAT if q % 2}
            (mx, my, _), total = moments(diffs, sums)
            part[0, p] = total + got[0]
            part[1, p] = mx
            part[2, p] = my
            part[3, p] = fill * dens + 0.5 * ex

        return body

    def local_inner(f, fz):
        body = local_part(f, fz)

        def inner(p, c):
            body(p)
            return c

        lax.fori_loop(1, NP - 1, inner, 0, unroll=6)

    def local_outer(t, f, fz):
        for k, q in enumerate(EAST):
            f[q, 0] = xr[t, 0, k]
        for k, q in enumerate(WEST):
            f[q, NP + 1] = xr[t, 1, k]
        fz[1, 0, 8:16] = jnp.where(g > 0, xr[t, 0, 5], 0.0)
        fz[1, NP + 1, 8:16] = jnp.where(g < NG - 1, xr[t, 1, 5], 0.0)
        for q in (11, 13):
            roll_z[CROSS.index(q), 0] = pltpu.roll(f[q, 0], 1 if q in UP else NL - 1, 1)
        for q in (12, 14):
            roll_z[CROSS.index(q), NP + 1] = pltpu.roll(f[q, NP + 1], 1 if q in UP else NL - 1, 1)
        body = local_part(f, fz)

        def outer(i, c):
            body(i * (NP - 1))
            return c

        lax.fori_loop(0, 2, outer, 0, unroll=2)

    def cross_part(f, fz, fill_ref, p):
        kind = flags[p]
        gas = kind == 0
        fill = fz[1, p + 1, 8:16]
        got = {}
        ex = None
        for side, dirs in enumerate((UP, DOWN)):
            edge = 0 if side == 0 else NL - 1
            for q in dirs:
                cx, cy, cz = VELOCITIES[q]
                k = CROSS.index(q)
                incoming = jnp.where(lane == edge, halo_s[k % 5, p], roll_z[k, p + 1 - cx])
                incoming = shift_rows(incoming, cy)
                beside = fz[1 - cz, p + 1 - cx, 8 - cy : 16 - cy]
                empty = beside == 0.0
                back = f[opposite(q), p + 1]
                pair = q if q % 2 else q - 1
                got[q] = jnp.where(empty, eqs[Z_PAIRS.index(pair), p] - back, incoming)
                term = jnp.where(empty, 0.0, (fill + beside) * (incoming - back))
                ex = term if ex is None else ex + term
                g_s[q, p] = got[q]
        diffs = {q: got[q] - got[q + 1] for q in Z_PAIRS}
        sums = {q: got[q] + got[q + 1] for q in Z_PAIRS}
        (mx, my, mz), total = moments(diffs, sums)
        dens = jnp.where(gas, 1.0, total + part[0, p])
        inv = 1.0 / dens
        vel[0, p] = dens
        vel[1, p] = (mx + part[1, p]) * inv
        vel[2, p] = (my + part[2, p]) * inv
        vel[3, p] = mz * inv
        mass = part[3, p] + 0.5 * ex
        fill_ref[p + 1, 8:16] = jnp.where(
            kind == 2, 1.0, jnp.where(gas, 0.0, jnp.clip(mass * inv, 0.01, 1.0))
        )

    def cross(t, f, fz, fill_ref, corner):
        odd = (lane & 1) == 1
        inside = jnp.logical_or(jnp.logical_and(odd, d > 0), jnp.logical_and(jnp.logical_not(odd), d < ND - 1))

        def turned(low, high, k):
            rows = slice(8 * (k // 2), 8 * (k // 2) + 8)
            by = 64 * (k % 2)
            return jnp.where(odd, pltpu.roll(low[rows], by + 1, 1), pltpu.roll(high[rows], (by + NL - 1) % NL, 1))

        main = (zr.at[t, 0], zr.at[t, 1])
        for k, half in enumerate((0, 1, 2, 4, 5)):
            columns[k] = turned(*main, half)
        columns[5] = jnp.where(inside, turned(*main, 3), 0.0)

        def to_edges(k, p):
            return pltpu.roll(columns[k], lax.rem(2 * NL - 1 - 2 * p, NL), 1)

        def halos(p):
            for k in range(5):
                halo_s[k, p] = to_edges(k, p - VELOCITIES[UP[k]][0])

        def fill_columns(p):
            new = to_edges(5, p)
            for edge, k in ((0, 0), (NL - 1, 2)):
                fz[k, p + 1, 8:16] = jnp.where(lane == edge, new, fz[k, p + 1, 8:16])

        def prepare(base):
            for j in range(4):
                halos(base + j)
                fill_columns(base + j + 1)

        def work(base):
            for j in range(4):
                cross_part(f, fz, fill_ref, base + j)

        fill_columns(3)
        fill_columns(4)
        prepare(4)

        def mid(i, c):
            for base in (8 * i + 4, 8 * i + 8):
                work(base)
                prepare(base + 4)
            return c

        lax.fori_loop(0, NP // 8 - 1, mid, 0)

        arrived(corner)
        west_lanes, east_lanes = lane >= NL - 2, (lane >> 1) == 32
        last_of = (zd.at[t, 0, 0], zd.at[t, 1, 0])
        first_of = (zd.at[t, 0, 1], zd.at[t, 1, 1])
        columns[3] = jnp.where(west_lanes, pltpu.roll(turned(*last_of, 4), 64, 1), columns[3])
        columns[4] = jnp.where(east_lanes, pltpu.roll(turned(*first_of, 5), 64, 1), columns[4])
        fills = columns[5]
        ghost = jnp.where(jnp.logical_and(inside, g > 0), pltpu.roll(turned(*last_of, 3), 64, 1), 0.0)
        fills = jnp.where(west_lanes, ghost, fills)
        ghost = jnp.where(jnp.logical_and(inside, g < NG - 1), pltpu.roll(turned(*first_of, 3), 64, 1), 0.0)
        columns[5] = jnp.where(east_lanes, ghost, fills)
        for at in (0, NP + 1):
            fz[0, at, 8:16] = pltpu.roll(fz[1, at, 8:16], 1, 1)
            fz[2, at, 8:16] = pltpu.roll(fz[1, at, 8:16], NL - 1, 1)
        fill_columns(-1)
        fill_columns(NP)
        for j in range(4):
            halos(j)
            halos(NP - 4 + j)
        for j in range(3):
            fill_columns(j)

        def last(i, c):
            work(i * (NP - 4))
            return c

        lax.fori_loop(0, 2, last, 0)

    def collide(f, p):
        gas = flags[p] == 0
        vx, vy, wz = vel[1, p], vel[2, p], vel[3, p] + RELAX_TIME * GRAVITY
        base = 1.0 - 1.5 * (vx * vx + vy * vy + wz * wz)
        keep = jnp.where(gas, 0.0, 1.0 - 1.0 / RELAX_TIME)
        scale = jnp.where(gas, 0.0, vel[0, p] * (1.0 / RELAX_TIME))
        new = {0: keep * f[0, p + 1] + (WEIGHTS[0] * scale) * base}
        by_weight = {w: (w * scale, 3.0 * w * scale) for w in (WEIGHTS[1], WEIGHTS[7])}
        for q in range(1, 19, 2):
            along = None
            for c, v in zip(VELOCITIES[q], (vx, vy, wz)):
                if c:
                    along = (v if c > 0 else -v) if along is None else (along + v if c > 0 else along - v)
            even_w, odd_w = by_weight[WEIGHTS[q]]
            even = even_w * (base + 4.5 * along * along)
            odd = odd_w * along
            new[q] = keep * g_s[q, p] + (even + odd)
            new[q + 1] = keep * g_s[q + 1, p] + (even - odd)
        return new

    local_inner(f0, fz0)

    pl.semaphore_wait(next_sem, len(x_peers))

    def beyond(i, gg, at, sem):
        to = lax.rem(d + i, ND)
        return pltpu.make_async_remote_copy(
            src_ref=hot_msg.at[to, pl.ds(0, 8)], dst_ref=hbuf.at[at, pl.ds(0, 8)],
            send_sem=hot_sem.at[4], recv_sem=hot_sem.at[sem], device_id=(gg, to), device_id_type=MESH,
        )

    def beyond_all(gg, at, sem):
        def one(i, c):
            beyond(i, gg, at, sem).start()
            return c

        lax.fori_loop(0, ND, one, 0)

    @pl.when(d == ND - 1)
    def _():
        beyond_all(east, 0, 2)

    @pl.when(d == 0)
    def _():
        beyond_all(west, NP + 1, 3)

    arrived(x0)
    local_outer(0, f0, fz0)
    arrived(z0)
    cross(0, f0, fz0, fz1.at[1], corner0)

    def first(p, acc):
        new = collide(f0, p)
        for q in range(19):
            f1[q, p + 1] = new[q]
        return pack_columns([new[q] for q in UP], [new[q] for q in DOWN], fz1[1, p + 1, 8:16], p, acc, lane)

    store_z(1, lax.fori_loop(0, NP, first, acc0, unroll=8))
    corner1 = started(corner_sends(1))
    z1 = started(z_sends(1))
    fill_x(1, f1, fz1)
    x1 = started(x_sends(1))

    local_inner(f1, fz1)

    own.wait()
    pltpu.make_async_copy(hot_msg.at[pl.ds(0, ND - 1)], hot_msg.at[pl.ds(0, ND - 1)], hot_sem.at[1]).wait()
    beyond(0, east, 0, 2).wait_recv()
    beyond(0, west, NP + 1, 3).wait_recv()
    hbuf[0, 0:8] = jnp.where(g > 0, hbuf[0, 0:8], 0.0)
    hbuf[NP + 1, 0:8] = jnp.where(g < NG - 1, hbuf[NP + 1, 0:8], 0.0)

    def temp(h):
        return jnp.minimum(h, 1.0) + jnp.maximum(h - 1.5, 0.0)

    def differences(p, c):
        h = hbuf[p + 1, 0:8]
        edges = hbuf[p + 1, 8:16]
        others = (
            hbuf[p, 0:8], hbuf[p + 2, 0:8],
            jnp.where(row == 0, 0.0, pltpu.roll(h, 1, 0)), jnp.where(row == NY - 1, 0.0, pltpu.roll(h, NY - 1, 0)),
            jnp.where(lane == 0, edges, pltpu.roll(h, 1, 1)), jnp.where(lane == NL - 1, edges, pltpu.roll(h, NL - 1, 1)),
        )
        mine = temp(h)
        total = None
        for k, other in enumerate(others):
            dt = temp(other) - mine
            total = dt if total is None else total + dt
            heat_d[k, p] = dt * (0.05 * STEP_TIME)
            heat_d[6 + k, p] = (other - h) * STEP_TIME
        heat_d[12, p] = total * STEP_TIME
        return c

    lax.fori_loop(0, NP, differences, 0, unroll=8)

    arrived(x1)
    local_outer(1, f1, fz1)
    arrived(z1)
    cross(1, f1, fz1, fz2, corner1)

    end_msg[0] = -fz2[NP, 8:16] * heat_d[1, NP - 1]
    end_msg[1] = -fz2[1, 8:16] * heat_d[0, 0]
    end_sends = [
        pltpu.make_async_remote_copy(
            src_ref=end_msg.at[k], dst_ref=ends_out.at[k, d],
            send_sem=back_sem.at[2 + k], recv_sem=back_sem.at[4 + k], device_id=to, device_id_type=MESH,
        )
        for k, to in ((0, (east, 0)), (1, (west, ND - 1)))
    ]
    for c in end_sends:
        c.start()

    def transport(p, c):
        fill = fz2[p + 1, 8:16]
        beside = (
            fz2[p, 8:16], fz2[p + 2, 8:16], fz2[p + 1, 7:15], fz2[p + 1, 9:17],
            jnp.where(lane == 0, 0.0, pltpu.roll(fill, 1, 1)),
            jnp.where(lane == NL - 1, 0.0, pltpu.roll(fill, NL - 1, 1)),
        )
        out = hbuf[p + 1, 0:8] + (0.02 + 0.05 * fill) * heat_d[12, p]
        for k in range(6):
            out = out + beside[k] * heat_d[k, p]
        for a in range(3):
            v = vel[1 + a, p]
            out = out + jnp.maximum(v, 0.0) * heat_d[6 + 2 * a, p] - jnp.minimum(v, 0.0) * heat_d[7 + 2 * a, p]
        msg[p, 0:8] = out
        msg[p, 8:16] = fill
        return c

    for dz in (2, 1, 3, 0):
        z_to = lax.rem(z + dz, 4)
        for j in range(8):
            transport(8 * z_to + j, 0)
        for dy, dc in ((2, 0), (2, 1), (1, 0), (1, 1), (3, 0), (3, 1), (0, 1), (0, 0)):
            if dz or dy or dc:
                p = 8 * z_to + lax.rem(y + dy, 4) * 2 + lax.rem(core + dc, 2)
                pltpu.make_async_remote_copy(
                    src_ref=msg.at[p], dst_ref=warm_out.at[d],
                    send_sem=back_sem.at[0], recv_sem=back_sem.at[1], device_id=(g, p), device_id_type=MESH,
                ).start()
    keep = pltpu.make_async_copy(msg.at[d], warm_out.at[d], load_sem.at[0])
    keep.start()
    fill_copy = pltpu.make_async_copy(fz2.at[pl.ds(1, NP), pl.ds(8, 8)], fill_out, out_sem.at[0])
    fill_copy.start()

    def second(p, c):
        new = collide(f1, p)
        for q in range(19):
            f0[q, p + 1] = new[q]
        return c

    pops_copies = []
    for base in range(0, NP, 8):
        lax.fori_loop(base, base + 8, second, 0, unroll=4)
        pops_copies.append(
            pltpu.make_async_copy(
                f0.at[:, pl.ds(1 + base, 8)], pops_out.at[:, pl.ds(base, 8)], out_sem.at[1 + base // 8]
            )
        )
        pops_copies[-1].start()

    for c in corner0 + z0 + x0 + corner1 + z1 + x1 + end_sends:
        c.wait_send()

    def all_of(ref, count, sem):
        part_of = ref.at[pl.ds(0, count)]
        pltpu.make_async_copy(part_of, part_of, sem).wait()

    all_of(hot_msg, ND - 1, hot_sem.at[0])

    @pl.when(d == 0)
    def _():
        all_of(hot_msg, ND // 2, hot_sem.at[4])

    @pl.when(d == ND - 1)
    def _():
        all_of(hot_msg, ND // 2, hot_sem.at[4])

    keep.wait()
    fill_copy.wait()
    for c in pops_copies:
        c.wait()
    all_of(msg, ND - 1, back_sem.at[0])
    all_of(msg, ND - 1, back_sem.at[1])

    @pl.when(d == 0)
    def _():
        all_of(msg, ND // 2, back_sem.at[4])

    @pl.when(d == ND - 1)
    def _():
        all_of(msg, ND // 2, back_sem.at[5])


def finish_kernel(
    pops_mid, fill_mid, warm_mid, ends_mid, energy_in, pops_out, fill_out, energy_out, got, ends, own, done, sem
):
    g, d = lax.axis_index("grp"), lax.axis_index("dev")
    copies = [
        pltpu.make_async_copy(pops_mid, pops_out, sem.at[0]),
        pltpu.make_async_copy(warm_mid, got, sem.at[1]),
        pltpu.make_async_copy(energy_in, own, sem.at[2]),
        pltpu.make_async_copy(ends_mid, ends, sem.at[3]),
        pltpu.make_async_copy(fill_mid, fill_out, sem.at[4]),
    ]
    for c in copies:
        c.start()
    for c in copies[1:4]:
        c.wait()
    lane = lane_iota()
    low = jnp.logical_and(d == 0, g > 0)
    high = jnp.logical_and(d == ND - 1, g < NG - 1)

    def temp(h):
        return jnp.minimum(h, 1.0) + jnp.maximum(h - 1.5, 0.0)

    halves = []
    for e in range(ND):
        cells = slice(e * NL, (e + 1) * NL)
        out = got[e, 0:8] + jnp.where(low, ends[0, e], 0.0) + jnp.where(high, ends[1, e], 0.0)
        warmth = temp(own[0, :, cells])
        for side, other in ((0, e - 1), (1, e + 1)):
            if other < 0 or other >= ND:
                continue
            by, edge = (1, 0) if side == 0 else (NL - 1, NL - 1)
            beyond = temp(own[0, :, other * NL : (other + 1) * NL])
            term = pltpu.roll(got[other, 8:16], by, 1) * (pltpu.roll(beyond, by, 1) - warmth)
            out = out + jnp.where(lane == edge, (0.05 * STEP_TIME) * term, 0.0)
        done[0, :, cells] = out
        if e % (ND // 2) == ND // 2 - 1:
            half = pl.ds((e // (ND // 2)) * (ND // 2) * NL, ND // 2 * NL)
            halves.append(
                pltpu.make_async_copy(done.at[:, :, half], energy_out.at[:, :, half], sem.at[1 + len(halves)])
            )
            halves[-1].start()
    for c in halves:
        c.wait()
    copies[4].wait()
    copies[0].wait()


def shards(populations, fill, flags, specific_energy_grid):
    plane = (NY, NL)
    any_spec = pl.BlockSpec(memory_space=pl.ANY)
    hbm_spec = pl.BlockSpec(memory_space=pltpu.HBM)
    given = [
        pltpu.with_memory_space_constraint(x, pltpu.HBM)
        for x in (populations, fill, flags, specific_energy_grid)
    ]
    pops_mid, fill_mid, warm_mid, ends_mid = pl.pallas_call(
        fluid_kernel,
        out_shape=(
            jax.ShapeDtypeStruct((19, NP) + plane, F32),
            jax.ShapeDtypeStruct((NP,) + plane, F32),
            jax.ShapeDtypeStruct((ND, 16, NL), F32),
            jax.ShapeDtypeStruct((2, ND) + plane, F32),
        ),
        in_specs=[hbm_spec] * 4,
        out_specs=(any_spec,) * 4,
        scratch_shapes=[
            pltpu.VMEM((19, NP + 2) + plane, F32),
            pltpu.VMEM((19, NP + 2) + plane, F32),
            pltpu.VMEM((3, NP + 2, 24, NL), F32),
            pltpu.VMEM((3, NP + 2, 24, NL), F32),
            pltpu.VMEM((NP + 2, 24, NL), F32),
            pltpu.VMEM((10, NP + 2) + plane, F32),
            pltpu.VMEM((5, NP) + plane, F32),
            pltpu.VMEM((6,) + plane, F32),
            pltpu.VMEM((19, NP) + plane, F32),
            pltpu.VMEM((4, NP) + plane, F32),
            pltpu.VMEM((5, NP) + plane, F32),
            pltpu.VMEM((NP,) + plane, jnp.int32),
            pltpu.VMEM((4, NP) + plane, F32),
            pltpu.VMEM((NY, (ND + 2) * NL), F32),
            pltpu.VMEM((ND, 16, NL), F32),
            pltpu.VMEM((NP + 2, 16, NL), F32),
            pltpu.VMEM((13, NP) + plane, F32),
            pltpu.VMEM((2, 2, 6) + plane, F32),
            pltpu.VMEM((2, 2, 6) + plane, F32),
            pltpu.VMEM((2, 24, NL), F32),
            pltpu.VMEM((2, 2, 24, NL), F32),
            pltpu.VMEM((2, 2, 2, 24, NL), F32),
            pltpu.VMEM((ND, 16, NL), F32),
            pltpu.VMEM((2,) + plane, F32),
            pltpu.SemaphoreType.DMA((7,)),
            pltpu.SemaphoreType.DMA((2, 8)),
            pltpu.SemaphoreType.DMA((2, 8)),
            pltpu.SemaphoreType.DMA((5,)),
            pltpu.SemaphoreType.DMA((6,)),
            pltpu.SemaphoreType.DMA((5,)),
            pltpu.SemaphoreType.REGULAR,
        ],
        compiler_params=pltpu.CompilerParams(
            collective_id=0, has_side_effects=True, vmem_limit_bytes=40 * 1024 * 1024
        ),
        name="pour",
    )(*given)
    return pl.pallas_call(
        finish_kernel,
        out_shape=(
            jax.ShapeDtypeStruct((19, NP) + plane, F32),
            jax.ShapeDtypeStruct((NP,) + plane, F32),
            jax.ShapeDtypeStruct((1, NY, ND * NL), F32),
        ),
        in_specs=[any_spec] * 5,
        out_specs=(any_spec,) * 3,
        scratch_shapes=[
            pltpu.VMEM((ND, 16, NL), F32),
            pltpu.VMEM((2, ND) + plane, F32),
            pltpu.VMEM((1, NY, ND * NL), F32),
            pltpu.VMEM((1, NY, ND * NL), F32),
            pltpu.SemaphoreType.DMA((5,)),
        ],
        compiler_params=pltpu.CompilerParams(vmem_limit_bytes=8 * 1024 * 1024),
        name="finish",
    )(pops_mid, fill_mid, warm_mid, ends_mid, given[3])


def solution(mesh):
    in_specs = (
        P(None, "grp", None, "dev"),
        P("grp", None, "dev"),
        P("grp", None, "dev"),
        P(("grp", "dev"), None, None),
    )
    out_specs = (P(None, "grp", None, "dev"), P("grp", None, "dev"), P(("grp", "dev"), None, None))
    return jax.shard_map(shards, mesh=mesh, in_specs=in_specs, out_specs=out_specs, check_vma=False)
```

```python
import functools

import jax
import jax.numpy as jnp
from jax import lax
from jax.experimental import pallas as pl
from jax.experimental.pallas import tpu as pltpu
from jax.sharding import PartitionSpec as P

MESH = pl.DeviceIdType.MESH
F32 = jnp.float32
VELOCITIES = (
    (0, 0, 0),
    (1, 0, 0),
    (-1, 0, 0),
    (0, 1, 0),
    (0, -1, 0),
    (0, 0, 1),
    (0, 0, -1),
    (1, 1, 0),
    (-1, -1, 0),
    (1, -1, 0),
    (-1, 1, 0),
    (1, 0, 1),
    (-1, 0, -1),
    (1, 0, -1),
    (-1, 0, 1),
    (0, 1, 1),
    (0, -1, -1),
    (0, 1, -1),
    (0, -1, 1),
)
WEIGHTS = (1.0 / 3.0,) + (1.0 / 18.0,) * 6 + (1.0 / 36.0,) * 12
RELAX_TIME = 0.8
GRAVITY = -0.002
STEP_TIME = 0.2

NG, ND, NP, NY, NL = 4, 32, 32, 8, 128
FLAT = (1, 2, 3, 4, 7, 8, 9, 10)
UP = (5, 15, 18, 11, 14)
DOWN = (6, 17, 16, 13, 12)
CROSS = UP + DOWN
EAST = (1, 7, 9, 11, 13)
WEST = (2, 8, 10, 12, 14)
Z_PAIRS = (5, 11, 13, 15, 17)


FAR_FIRST = sorted(
    ((dz, dy) for dz in range(4) for dy in range(4)),
    key=lambda at: -(min(at[0], 4 - at[0]) + min(at[1], 4 - at[1])),
)


def opposite(q):
    return q + 1 if q % 2 == 1 else q - 1


def lane_iota():
    return lax.broadcasted_iota(jnp.int32, (NY, NL), 1)


def shift_rows(x, cy):
    return x if cy == 0 else pltpu.roll(x, cy % NY, 0)


def spread(x, lane):
    return jnp.broadcast_to(x[:, lane : lane + 1], (NY, NL))


def moments(d, s):
    out = []
    for axis in range(3):
        total = None
        for q, diff in d.items():
            c = VELOCITIES[q][axis]
            if c == 0:
                continue
            if total is None:
                total = diff if c > 0 else -diff
            else:
                total = total + diff if c > 0 else total - diff
        out.append(total)
    return out, sum(s.values())


def pack_columns(ups, downs, fill, p, acc, lane):
    here = (lane >> 1) == p
    there = (lane >> 1) == p + 32

    def both(k):
        return jnp.where(lane == NL - 1, ups[k], downs[k])

    out = []
    for a, first, second in ((acc[0], both(0), both(1)), (acc[1], both(2), fill), (acc[2], both(3), both(4))):
        a = jnp.where(here, pltpu.roll(first, 2 * p + 1, 1), a)
        out.append(jnp.where(there, pltpu.roll(second, 2 * p + 65, 1), a))
    return tuple(out)


def fluid_kernel(
    pops_in, fill_in, flags_in, energy_in,
    pops_out, fill_out, warm_out, ends_out,
    f0, f1, fz0, fz1, fz2, roll_z, halo_s, columns, g_s, part, eqs, flags, vel, own_e, hot_msg, hbuf, heat_d,
    xs, xr, zs, zr, zd, msg, turned, end_msg,
    load_sem, send_sem, recv_sem, hot_sem, back_sem, out_sem, next_sem,
):
    g, d = lax.axis_index("grp"), lax.axis_index("dev")
    up, down = lax.rem(d + 1, ND), lax.rem(d + ND - 1, ND)
    east, west = lax.rem(g + 1, NG), lax.rem(g + NG - 1, NG)
    lane = lane_iota()
    row = lax.broadcasted_iota(jnp.int32, (NY, NL), 0)
    zero8 = jnp.zeros((NY, NL), F32)

    z, y, core = lax.div(d, 8), lax.rem(lax.div(d, 2), 4), lax.rem(d, 2)
    barrier = pltpu.get_barrier_semaphore()
    x_peers = [(east, d), (west, d)]
    near = [(gg, dd) for dd in (up, down) for gg in (east, west)]
    for dz, dy in FAR_FIRST:
        for dc in range(2):
            if dz or dy or dc:
                to = lax.rem(z + dz, 4) * 8 + lax.rem(y + dy, 4) * 2 + lax.rem(core + dc, 2)
                near.append((g, to))
    near += x_peers
    for to in near:
        pl.semaphore_signal(barrier, inc=1, device_id=to, device_id_type=MESH)

    def load(src, dst, n):
        c = pltpu.make_async_copy(src, dst, load_sem.at[n])
        c.start()
        return c

    def load_pops(q, count, n):
        return load(pops_in.at[pl.ds(q, count)], f0.at[pl.ds(q, count), pl.ds(1, NP)], n)

    fill_load = load(fill_in, fz0.at[1, pl.ds(1, NP), pl.ds(8, 8)], 0)
    cross_loads = [load_pops(11, 8, 1), load_pops(5, 2, 2)]
    more_loads = [load_pops(0, 5, 3), load_pops(7, 4, 4), load(flags_in, flags, 5)]
    energy_load = load(energy_in.at[0], own_e.at[:, pl.ds(NL, ND * NL)], 6)

    def clear(p, c):
        for k in range(3):
            for ref in (fz0, fz1):
                ref[k, p, 0:8] = zero8
                ref[k, p, 16:24] = zero8
        fz2[p, 0:8] = zero8
        fz2[p, 16:24] = zero8
        return c

    lax.fori_loop(0, NP + 2, clear, 0)
    fz2[0, 8:16] = zero8
    fz2[NP + 1, 8:16] = zero8
    own_e[:, 0:NL] = zero8
    own_e[:, (ND + 1) * NL : (ND + 2) * NL] = zero8

    def send(t, src, dst, n, to):
        return pltpu.make_async_remote_copy(
            src_ref=src, dst_ref=dst, send_sem=send_sem.at[t, n], recv_sem=recv_sem.at[t, n],
            device_id=to, device_id_type=MESH,
        )

    def x_sends(t):
        return [
            send(t, xs.at[t, 0], xr.at[t, 0], 0, (east, d)),
            send(t, xs.at[t, 1], xr.at[t, 1], 1, (west, d)),
        ]

    def z_sends(t):
        return [
            send(t, zs.at[t], zr.at[t, side], 2 + side, (g, to))
            for side, to in ((0, up), (1, down))
        ]

    def corner_sends(t):
        return [
            send(t, zs.at[t], zd.at[t, side, k], 4 + 2 * side + k, (gg, to))
            for side, to in ((0, up), (1, down))
            for k, gg in ((0, east), (1, west))
        ]

    def fill_x(t, f, fz):
        for k, q in enumerate(EAST):
            xs[t, 0, k] = f[q, NP]
        xs[t, 0, 5] = fz[1, NP, 8:16]
        for k, q in enumerate(WEST):
            xs[t, 1, k] = f[q, 1]
        xs[t, 1, 5] = fz[1, 1, 8:16]

    def store_z(t, acc):
        for k in range(3):
            zs[t, 8 * k : 8 * k + 8] = acc[k]

    def started(copies):
        for c in copies:
            c.start()
        return copies

    def arrived(copies):
        for c in copies:
            c.wait_recv()

    fill_load.wait()
    for c in cross_loads:
        c.wait()

    def pack0(p, acc):
        return pack_columns(
            [f0[q, p + 1] for q in UP], [f0[q, p + 1] for q in DOWN], fz0[1, p + 1, 8:16], p, acc, lane
        )

    acc0 = (zero8,) * 3
    store_z(0, lax.fori_loop(0, NP, pack0, acc0, unroll=8))

    energy_load.wait()

    def block_of(e):
        return own_e[:, pl.ds(pl.multiple_of((e + 1) * NL, NL), NL)]

    def hot_build(e, c):
        hot_msg[e, 0:8] = block_of(e)
        beside = jnp.where(lane == 0, pltpu.roll(block_of(e - 1), 1, 1), pltpu.roll(block_of(e + 1), NL - 1, 1))
        hot_msg[e, 8:16] = beside
        return c

    lax.fori_loop(0, ND, hot_build, 0, unroll=8)

    pl.semaphore_wait(barrier, len(near))
    for to in x_peers:
        pl.semaphore_signal(next_sem, inc=1, device_id=to, device_id_type=MESH)

    corner0 = started(corner_sends(0))
    z0 = started(z_sends(0))
    for c in more_loads:
        c.wait()
    fill_x(0, f0, fz0)
    x0 = started(x_sends(0))

    def hot_start(i, c):
        to = lax.rem(d + i, ND)
        pltpu.make_async_remote_copy(
            src_ref=hot_msg.at[to], dst_ref=hbuf.at[d + 1],
            send_sem=hot_sem.at[0], recv_sem=hot_sem.at[1], device_id=(g, to), device_id_type=MESH,
        ).start()
        return c

    lax.fori_loop(1, ND, hot_start, 0)
    own = pltpu.make_async_copy(hot_msg.at[d], hbuf.at[d + 1], load_sem.at[0])
    own.start()


    def local_part(f, fz):
        def body(p):
            pops = [f[q, p + 1] for q in range(19)]
            kind = flags[p]
            gas = kind == 0
            fill = fz[1, p + 1, 8:16]
            diffs = {q: pops[q] - pops[q + 1] for q in range(1, 19, 2)}
            sums = {q: pops[q] + pops[q + 1] for q in range(1, 19, 2)}
            (mx, my, mz), total = moments(diffs, sums)
            dens = jnp.where(gas, 1.0, total + pops[0])
            inv = 1.0 / dens
            vx, vy, vz = mx * inv, my * inv, mz * inv
            base = 1.0 - 1.5 * (vx * vx + vy * vy + vz * vz)

            def paired(q):
                cx, cy, cz = VELOCITIES[q]
                along = None
                for c, v in ((cx, vx), (cy, vy), (cz, vz)):
                    if c:
                        along = (v if c > 0 else -v) if along is None else (along + v if c > 0 else along - v)
                return (2.0 * WEIGHTS[q]) * (base + 4.5 * along * along)

            for k, q in enumerate(Z_PAIRS):
                eqs[k, p] = paired(q)
            for k, q in enumerate(CROSS):
                roll_z[k, p + 1] = pltpu.roll(pops[q], 1 if q in UP else NL - 1, 1)
            fz[0, p + 1, 8:16] = pltpu.roll(fill, 1, 1)
            fz[2, p + 1, 8:16] = pltpu.roll(fill, NL - 1, 1)
            ex = None
            got = {0: pops[0]}
            for q in FLAT:
                cx, cy, _ = VELOCITIES[q]
                incoming = shift_rows(f[q, p + 1 - cx], cy)
                beside = fz[1, p + 1 - cx, 8 - cy : 16 - cy]
                empty = beside == 0.0
                back = pops[opposite(q)]
                got[q] = jnp.where(empty, paired(q if q % 2 else q - 1) - back, incoming)
                term = jnp.where(empty, 0.0, (fill + beside) * (incoming - back))
                ex = term if ex is None else ex + term
                g_s[q, p] = got[q]
            diffs = {q: got[q] - got[q + 1] for q in FLAT if q % 2}
            sums = {q: got[q] + got[q + 1] for q in FLAT if q % 2}
            (mx, my, _), total = moments(diffs, sums)
            part[0, p] = total + got[0]
            part[1, p] = mx
            part[2, p] = my
            part[3, p] = fill * dens + 0.5 * ex

        return body

    def local_inner(f, fz):
        body = local_part(f, fz)

        def inner(p, c):
            body(p)
            return c

        lax.fori_loop(1, NP - 1, inner, 0, unroll=6)

    def local_outer(t, f, fz):
        for k, q in enumerate(EAST):
            f[q, 0] = xr[t, 0, k]
        for k, q in enumerate(WEST):
            f[q, NP + 1] = xr[t, 1, k]
        fz[1, 0, 8:16] = jnp.where(g > 0, xr[t, 0, 5], 0.0)
        fz[1, NP + 1, 8:16] = jnp.where(g < NG - 1, xr[t, 1, 5], 0.0)
        for q in (11, 13):
            roll_z[CROSS.index(q), 0] = pltpu.roll(f[q, 0], 1 if q in UP else NL - 1, 1)
        for q in (12, 14):
            roll_z[CROSS.index(q), NP + 1] = pltpu.roll(f[q, NP + 1], 1 if q in UP else NL - 1, 1)
        body = local_part(f, fz)

        def outer(i, c):
            body(i * (NP - 1))
            return c

        lax.fori_loop(0, 2, outer, 0, unroll=2)

    def cross_part(f, fz, fill_ref, p):
        kind = flags[p]
        gas = kind == 0
        fill = fz[1, p + 1, 8:16]
        got = {}
        ex = None
        for side, dirs in enumerate((UP, DOWN)):
            edge = 0 if side == 0 else NL - 1
            for q in dirs:
                cx, cy, cz = VELOCITIES[q]
                k = CROSS.index(q)
                incoming = jnp.where(lane == edge, halo_s[k % 5, p], roll_z[k, p + 1 - cx])
                incoming = shift_rows(incoming, cy)
                beside = fz[1 - cz, p + 1 - cx, 8 - cy : 16 - cy]
                empty = beside == 0.0
                back = f[opposite(q), p + 1]
                pair = q if q % 2 else q - 1
                got[q] = jnp.where(empty, eqs[Z_PAIRS.index(pair), p] - back, incoming)
                term = jnp.where(empty, 0.0, (fill + beside) * (incoming - back))
                ex = term if ex is None else ex + term
                g_s[q, p] = got[q]
        diffs = {q: got[q] - got[q + 1] for q in Z_PAIRS}
        sums = {q: got[q] + got[q + 1] for q in Z_PAIRS}
        (mx, my, mz), total = moments(diffs, sums)
        dens = jnp.where(gas, 1.0, total + part[0, p])
        inv = 1.0 / dens
        vel[0, p] = dens
        vel[1, p] = (mx + part[1, p]) * inv
        vel[2, p] = (my + part[2, p]) * inv
        vel[3, p] = mz * inv
        mass = part[3, p] + 0.5 * ex
        fill_ref[p + 1, 8:16] = jnp.where(
            kind == 2, 1.0, jnp.where(gas, 0.0, jnp.clip(mass * inv, 0.01, 1.0))
        )

    def cross(t, f, fz, fill_ref, corner):
        odd = (lane & 1) == 1
        inside = jnp.logical_or(jnp.logical_and(odd, d > 0), jnp.logical_and(jnp.logical_not(odd), d < ND - 1))

        def turned(low, high, k):
            rows = slice(8 * (k // 2), 8 * (k // 2) + 8)
            by = 64 * (k % 2)
            return jnp.where(odd, pltpu.roll(low[rows], by + 1, 1), pltpu.roll(high[rows], (by + NL - 1) % NL, 1))

        main = (zr.at[t, 0], zr.at[t, 1])
        for k, half in enumerate((0, 1, 2, 4, 5)):
            columns[k] = turned(*main, half)
        columns[5] = jnp.where(inside, turned(*main, 3), 0.0)

        def to_edges(k, p):
            return pltpu.roll(columns[k], lax.rem(2 * NL - 1 - 2 * p, NL), 1)

        def halos(p):
            for k in range(5):
                halo_s[k, p] = to_edges(k, p - VELOCITIES[UP[k]][0])

        def fill_columns(p):
            new = to_edges(5, p)
            for edge, k in ((0, 0), (NL - 1, 2)):
                fz[k, p + 1, 8:16] = jnp.where(lane == edge, new, fz[k, p + 1, 8:16])

        def prepare(base):
            for j in range(4):
                halos(base + j)
                fill_columns(base + j + 1)

        def work(base):
            for j in range(4):
                cross_part(f, fz, fill_ref, base + j)

        fill_columns(3)
        fill_columns(4)
        prepare(4)

        def mid(i, c):
            for base in (8 * i + 4, 8 * i + 8):
                work(base)
                prepare(base + 4)
            return c

        lax.fori_loop(0, NP // 8 - 1, mid, 0)

        arrived(corner)
        west_lanes, east_lanes = lane >= NL - 2, (lane >> 1) == 32
        last_of = (zd.at[t, 0, 0], zd.at[t, 1, 0])
        first_of = (zd.at[t, 0, 1], zd.at[t, 1, 1])
        columns[3] = jnp.where(west_lanes, pltpu.roll(turned(*last_of, 4), 64, 1), columns[3])
        columns[4] = jnp.where(east_lanes, pltpu.roll(turned(*first_of, 5), 64, 1), columns[4])
        fills = columns[5]
        ghost = jnp.where(jnp.logical_and(inside, g > 0), pltpu.roll(turned(*last_of, 3), 64, 1), 0.0)
        fills = jnp.where(west_lanes, ghost, fills)
        ghost = jnp.where(jnp.logical_and(inside, g < NG - 1), pltpu.roll(turned(*first_of, 3), 64, 1), 0.0)
        columns[5] = jnp.where(east_lanes, ghost, fills)
        for at in (0, NP + 1):
            fz[0, at, 8:16] = pltpu.roll(fz[1, at, 8:16], 1, 1)
            fz[2, at, 8:16] = pltpu.roll(fz[1, at, 8:16], NL - 1, 1)
        fill_columns(-1)
        fill_columns(NP)
        for j in range(4):
            halos(j)
            halos(NP - 4 + j)
        for j in range(3):
            fill_columns(j)

        def last(i, c):
            work(i * (NP - 4))
            return c

        lax.fori_loop(0, 2, last, 0)

    def collide(f, p):
        gas = flags[p] == 0
        vx, vy, wz = vel[1, p], vel[2, p], vel[3, p] + RELAX_TIME * GRAVITY
        base = 1.0 - 1.5 * (vx * vx + vy * vy + wz * wz)
        keep = jnp.where(gas, 0.0, 1.0 - 1.0 / RELAX_TIME)
        scale = jnp.where(gas, 0.0, vel[0, p] * (1.0 / RELAX_TIME))
        new = {0: keep * f[0, p + 1] + (WEIGHTS[0] * scale) * base}
        by_weight = {w: (w * scale, 3.0 * w * scale) for w in (WEIGHTS[1], WEIGHTS[7])}
        for q in range(1, 19, 2):
            along = None
            for c, v in zip(VELOCITIES[q], (vx, vy, wz)):
                if c:
                    along = (v if c > 0 else -v) if along is None else (along + v if c > 0 else along - v)
            even_w, odd_w = by_weight[WEIGHTS[q]]
            even = even_w * (base + 4.5 * along * along)
            odd = odd_w * along
            new[q] = keep * g_s[q, p] + (even + odd)
            new[q + 1] = keep * g_s[q + 1, p] + (even - odd)
        return new

    local_inner(f0, fz0)

    pl.semaphore_wait(next_sem, len(x_peers))

    def beyond(i, gg, at, sem):
        to = lax.rem(d + i, ND)
        return pltpu.make_async_remote_copy(
            src_ref=hot_msg.at[to, pl.ds(0, 8)], dst_ref=hbuf.at[at, pl.ds(0, 8)],
            send_sem=hot_sem.at[4], recv_sem=hot_sem.at[sem], device_id=(gg, to), device_id_type=MESH,
        )

    def beyond_all(gg, at, sem):
        def one(i, c):
            beyond(i, gg, at, sem).start()
            return c

        lax.fori_loop(0, ND, one, 0)

    @pl.when(d == ND - 1)
    def _():
        beyond_all(east, 0, 2)

    @pl.when(d == 0)
    def _():
        beyond_all(west, NP + 1, 3)

    arrived(x0)
    local_outer(0, f0, fz0)
    arrived(z0)
    cross(0, f0, fz0, fz1.at[1], corner0)

    def first(p, acc):
        new = collide(f0, p)
        for q in range(19):
            f1[q, p + 1] = new[q]
        return pack_columns([new[q] for q in UP], [new[q] for q in DOWN], fz1[1, p + 1, 8:16], p, acc, lane)

    store_z(1, lax.fori_loop(0, NP, first, acc0, unroll=8))
    corner1 = started(corner_sends(1))
    z1 = started(z_sends(1))
    fill_x(1, f1, fz1)
    x1 = started(x_sends(1))

    local_inner(f1, fz1)

    own.wait()
    pltpu.make_async_copy(hot_msg.at[pl.ds(0, ND - 1)], hot_msg.at[pl.ds(0, ND - 1)], hot_sem.at[1]).wait()
    beyond(0, east, 0, 2).wait_recv()
    beyond(0, west, NP + 1, 3).wait_recv()
    hbuf[0, 0:8] = jnp.where(g > 0, hbuf[0, 0:8], 0.0)
    hbuf[NP + 1, 0:8] = jnp.where(g < NG - 1, hbuf[NP + 1, 0:8], 0.0)

    def temp(h):
        return jnp.minimum(h, 1.0) + jnp.maximum(h - 1.5, 0.0)

    def differences(p, c):
        h = hbuf[p + 1, 0:8]
        edges = hbuf[p + 1, 8:16]
        others = (
            hbuf[p, 0:8], hbuf[p + 2, 0:8],
            jnp.where(row == 0, 0.0, pltpu.roll(h, 1, 0)), jnp.where(row == NY - 1, 0.0, pltpu.roll(h, NY - 1, 0)),
            jnp.where(lane == 0, edges, pltpu.roll(h, 1, 1)), jnp.where(lane == NL - 1, edges, pltpu.roll(h, NL - 1, 1)),
        )
        mine = temp(h)
        total = None
        for k, other in enumerate(others):
            dt = temp(other) - mine
            total = dt if total is None else total + dt
            heat_d[k, p] = dt * (0.05 * STEP_TIME)
            heat_d[6 + k, p] = (other - h) * STEP_TIME
        heat_d[12, p] = total * STEP_TIME
        return c

    lax.fori_loop(0, NP, differences, 0, unroll=8)

    arrived(x1)
    local_outer(1, f1, fz1)
    arrived(z1)
    cross(1, f1, fz1, fz2, corner1)

    end_msg[0] = -fz2[NP, 8:16] * heat_d[1, NP - 1]
    end_msg[1] = -fz2[1, 8:16] * heat_d[0, 0]
    end_sends = [
        pltpu.make_async_remote_copy(
            src_ref=end_msg.at[k], dst_ref=ends_out.at[k, d],
            send_sem=back_sem.at[2 + k], recv_sem=back_sem.at[4 + k], device_id=to, device_id_type=MESH,
        )
        for k, to in ((0, (east, 0)), (1, (west, ND - 1)))
    ]
    for c in end_sends:
        c.start()

    def edge_fill(p, acc):
        return jnp.where((lane >> 1) == p, pltpu.roll(fz2[p + 1, 8:16], 2 * p + 1, 1), acc)

    edges = lax.fori_loop(0, NP, edge_fill, zero8, unroll=16)
    turned[...] = jnp.concatenate([edges] * (NL // NY), axis=0).T

    def transport(p, c):
        fill = fz2[p + 1, 8:16]
        beside = (
            fz2[p, 8:16], fz2[p + 2, 8:16], fz2[p + 1, 7:15], fz2[p + 1, 9:17],
            jnp.where(lane == 0, 0.0, pltpu.roll(fill, 1, 1)),
            jnp.where(lane == NL - 1, 0.0, pltpu.roll(fill, NL - 1, 1)),
        )
        out = hbuf[p + 1, 0:8] + (0.02 + 0.05 * fill) * heat_d[12, p]
        for k in range(6):
            out = out + beside[k] * heat_d[k, p]
        for a in range(3):
            v = vel[1 + a, p]
            out = out + jnp.maximum(v, 0.0) * heat_d[6 + 2 * a, p] - jnp.minimum(v, 0.0) * heat_d[7 + 2 * a, p]
        msg[p, 0:8] = out
        msg[p, 8:10] = turned[pl.ds(2 * p, 2)]
        return c

    for dz in (2, 1, 3, 0):
        z_to = lax.rem(z + dz, 4)
        for j in range(8):
            transport(8 * z_to + j, 0)
        for dy, dc in ((2, 0), (2, 1), (1, 0), (1, 1), (3, 0), (3, 1), (0, 1), (0, 0)):
            if dz or dy or dc:
                p = 8 * z_to + lax.rem(y + dy, 4) * 2 + lax.rem(core + dc, 2)
                pltpu.make_async_remote_copy(
                    src_ref=msg.at[p, pl.ds(0, 10)], dst_ref=warm_out.at[d, pl.ds(0, 10)],
                    send_sem=back_sem.at[0], recv_sem=back_sem.at[1], device_id=(g, p), device_id_type=MESH,
                ).start()
    keep = pltpu.make_async_copy(msg.at[d, pl.ds(0, 10)], warm_out.at[d, pl.ds(0, 10)], load_sem.at[0])
    keep.start()
    fill_copy = pltpu.make_async_copy(fz2.at[pl.ds(1, NP), pl.ds(8, 8)], fill_out, out_sem.at[0])
    fill_copy.start()

    def second(p, c):
        new = collide(f1, p)
        for q in range(19):
            f0[q, p + 1] = new[q]
        return c

    pops_copies = []
    for base in range(0, NP, 8):
        lax.fori_loop(base, base + 8, second, 0, unroll=4)
        pops_copies.append(
            pltpu.make_async_copy(
                f0.at[:, pl.ds(1 + base, 8)], pops_out.at[:, pl.ds(base, 8)], out_sem.at[1 + base // 8]
            )
        )
        pops_copies[-1].start()

    for c in corner0 + z0 + x0 + corner1 + z1 + x1 + end_sends:
        c.wait_send()

    def all_of(ref, count, sem):
        part_of = ref.at[pl.ds(0, count)]
        pltpu.make_async_copy(part_of, part_of, sem).wait()

    all_of(hot_msg, ND - 1, hot_sem.at[0])

    @pl.when(d == 0)
    def _():
        all_of(hot_msg, ND // 2, hot_sem.at[4])

    @pl.when(d == ND - 1)
    def _():
        all_of(hot_msg, ND // 2, hot_sem.at[4])

    keep.wait()
    fill_copy.wait()
    for c in pops_copies:
        c.wait()
    sent = msg.at[pl.ds(0, ND - 1), pl.ds(0, 10)]
    for n in range(2):
        pltpu.make_async_copy(sent, sent, back_sem.at[n]).wait()

    @pl.when(d == 0)
    def _():
        all_of(msg, ND // 2, back_sem.at[4])

    @pl.when(d == ND - 1)
    def _():
        all_of(msg, ND // 2, back_sem.at[5])


def finish_kernel(
    pops_mid, fill_mid, warm_mid, ends_mid, energy_in, pops_out, fill_out, energy_out, got, ends, own, done, rows, sem
):
    g, d = lax.axis_index("grp"), lax.axis_index("dev")
    copies = [
        pltpu.make_async_copy(pops_mid, pops_out, sem.at[0]),
        pltpu.make_async_copy(warm_mid, got, sem.at[1]),
        pltpu.make_async_copy(energy_in, own, sem.at[2]),
        pltpu.make_async_copy(ends_mid, ends, sem.at[3]),
        pltpu.make_async_copy(fill_mid, fill_out, sem.at[4]),
    ]
    for c in copies:
        c.start()
    for c in copies[1:4]:
        c.wait()
    lane = lane_iota()
    low = jnp.logical_and(d == 0, g > 0)
    high = jnp.logical_and(d == ND - 1, g < NG - 1)

    def temp(h):
        return jnp.minimum(h, 1.0) + jnp.maximum(h - 1.5, 0.0)

    rows[...] = jnp.zeros((NL, NL), F32)
    for e in range(ND):
        rows[2 * e : 2 * e + 2] = got[e, 8:10]
    edges = rows[...].T[0:NY]
    halves = []
    for e in range(ND):
        cells = slice(e * NL, (e + 1) * NL)
        out = got[e, 0:8] + jnp.where(low, ends[0, e], 0.0) + jnp.where(high, ends[1, e], 0.0)
        warmth = temp(own[0, :, cells])
        for side, other in ((0, e - 1), (1, e + 1)):
            if other < 0 or other >= ND:
                continue
            by, edge = (1, 0) if side == 0 else (NL - 1, NL - 1)
            beyond = temp(own[0, :, other * NL : (other + 1) * NL])
            at = 2 * other + side
            term = pltpu.roll(edges, (edge - at) % NL, 1) * (pltpu.roll(beyond, by, 1) - warmth)
            out = out + jnp.where(lane == edge, (0.05 * STEP_TIME) * term, 0.0)
        done[0, :, cells] = out
        if e % (ND // 2) == ND // 2 - 1:
            half = pl.ds((e // (ND // 2)) * (ND // 2) * NL, ND // 2 * NL)
            halves.append(
                pltpu.make_async_copy(done.at[:, :, half], energy_out.at[:, :, half], sem.at[1 + len(halves)])
            )
            halves[-1].start()
    for c in halves:
        c.wait()
    copies[4].wait()
    copies[0].wait()


def shards(populations, fill, flags, specific_energy_grid):
    plane = (NY, NL)
    any_spec = pl.BlockSpec(memory_space=pl.ANY)
    hbm_spec = pl.BlockSpec(memory_space=pltpu.HBM)
    given = [
        pltpu.with_memory_space_constraint(x, pltpu.HBM)
        for x in (populations, fill, flags, specific_energy_grid)
    ]
    pops_mid, fill_mid, warm_mid, ends_mid = pl.pallas_call(
        fluid_kernel,
        out_shape=(
            jax.ShapeDtypeStruct((19, NP) + plane, F32),
            jax.ShapeDtypeStruct((NP,) + plane, F32),
            jax.ShapeDtypeStruct((ND, 16, NL), F32),
            jax.ShapeDtypeStruct((2, ND) + plane, F32),
        ),
        in_specs=[hbm_spec] * 4,
        out_specs=(any_spec,) * 4,
        scratch_shapes=[
            pltpu.VMEM((19, NP + 2) + plane, F32),
            pltpu.VMEM((19, NP + 2) + plane, F32),
            pltpu.VMEM((3, NP + 2, 24, NL), F32),
            pltpu.VMEM((3, NP + 2, 24, NL), F32),
            pltpu.VMEM((NP + 2, 24, NL), F32),
            pltpu.VMEM((10, NP + 2) + plane, F32),
            pltpu.VMEM((5, NP) + plane, F32),
            pltpu.VMEM((6,) + plane, F32),
            pltpu.VMEM((19, NP) + plane, F32),
            pltpu.VMEM((4, NP) + plane, F32),
            pltpu.VMEM((5, NP) + plane, F32),
            pltpu.VMEM((NP,) + plane, jnp.int32),
            pltpu.VMEM((4, NP) + plane, F32),
            pltpu.VMEM((NY, (ND + 2) * NL), F32),
            pltpu.VMEM((ND, 16, NL), F32),
            pltpu.VMEM((NP + 2, 16, NL), F32),
            pltpu.VMEM((13, NP) + plane, F32),
            pltpu.VMEM((2, 2, 6) + plane, F32),
            pltpu.VMEM((2, 2, 6) + plane, F32),
            pltpu.VMEM((2, 24, NL), F32),
            pltpu.VMEM((2, 2, 24, NL), F32),
            pltpu.VMEM((2, 2, 2, 24, NL), F32),
            pltpu.VMEM((ND, 16, NL), F32),
            pltpu.VMEM((NL, NL), F32),
            pltpu.VMEM((2,) + plane, F32),
            pltpu.SemaphoreType.DMA((7,)),
            pltpu.SemaphoreType.DMA((2, 8)),
            pltpu.SemaphoreType.DMA((2, 8)),
            pltpu.SemaphoreType.DMA((5,)),
            pltpu.SemaphoreType.DMA((6,)),
            pltpu.SemaphoreType.DMA((5,)),
            pltpu.SemaphoreType.REGULAR,
        ],
        compiler_params=pltpu.CompilerParams(
            collective_id=0, has_side_effects=True, vmem_limit_bytes=40 * 1024 * 1024
        ),
        name="pour",
    )(*given)
    return pl.pallas_call(
        finish_kernel,
        out_shape=(
            jax.ShapeDtypeStruct((19, NP) + plane, F32),
            jax.ShapeDtypeStruct((NP,) + plane, F32),
            jax.ShapeDtypeStruct((1, NY, ND * NL), F32),
        ),
        in_specs=[any_spec] * 5,
        out_specs=(any_spec,) * 3,
        scratch_shapes=[
            pltpu.VMEM((ND, 16, NL), F32),
            pltpu.VMEM((2, ND) + plane, F32),
            pltpu.VMEM((1, NY, ND * NL), F32),
            pltpu.VMEM((1, NY, ND * NL), F32),
            pltpu.VMEM((NL, NL), F32),
            pltpu.SemaphoreType.DMA((5,)),
        ],
        compiler_params=pltpu.CompilerParams(vmem_limit_bytes=8 * 1024 * 1024),
        name="finish",
    )(pops_mid, fill_mid, warm_mid, ends_mid, given[3])


def solution(mesh):
    in_specs = (
        P(None, "grp", None, "dev"),
        P("grp", None, "dev"),
        P("grp", None, "dev"),
        P(("grp", "dev"), None, None),
    )
    out_specs = (P(None, "grp", None, "dev"), P("grp", None, "dev"), P(("grp", "dev"), None, None))
    return jax.shard_map(shards, mesh=mesh, in_specs=in_specs, out_specs=out_specs, check_vma=False)
```

```python
import functools

import jax
import jax.numpy as jnp
from jax import lax
from jax.experimental import pallas as pl
from jax.experimental.pallas import tpu as pltpu
from jax.sharding import PartitionSpec as P

MESH = pl.DeviceIdType.MESH
F32 = jnp.float32
VELOCITIES = (
    (0, 0, 0),
    (1, 0, 0),
    (-1, 0, 0),
    (0, 1, 0),
    (0, -1, 0),
    (0, 0, 1),
    (0, 0, -1),
    (1, 1, 0),
    (-1, -1, 0),
    (1, -1, 0),
    (-1, 1, 0),
    (1, 0, 1),
    (-1, 0, -1),
    (1, 0, -1),
    (-1, 0, 1),
    (0, 1, 1),
    (0, -1, -1),
    (0, 1, -1),
    (0, -1, 1),
)
WEIGHTS = (1.0 / 3.0,) + (1.0 / 18.0,) * 6 + (1.0 / 36.0,) * 12
RELAX_TIME = 0.8
GRAVITY = -0.002
STEP_TIME = 0.2

NG, ND, NP, NY, NL = 4, 32, 32, 8, 128
FLAT = (1, 2, 3, 4, 7, 8, 9, 10)
UP = (5, 15, 18, 11, 14)
DOWN = (6, 17, 16, 13, 12)
CROSS = UP + DOWN
EAST = (1, 7, 9, 11, 13)
WEST = (2, 8, 10, 12, 14)
Z_PAIRS = (5, 11, 13, 15, 17)


FAR_FIRST = sorted(
    ((dz, dy) for dz in range(4) for dy in range(4)),
    key=lambda at: -(min(at[0], 4 - at[0]) + min(at[1], 4 - at[1])),
)


def opposite(q):
    return q + 1 if q % 2 == 1 else q - 1


def lane_iota():
    return lax.broadcasted_iota(jnp.int32, (NY, NL), 1)


def shift_rows(x, cy):
    return x if cy == 0 else pltpu.roll(x, cy % NY, 0)


def spread(x, lane):
    return jnp.broadcast_to(x[:, lane : lane + 1], (NY, NL))


def moments(d, s):
    out = []
    for axis in range(3):
        total = None
        for q, diff in d.items():
            c = VELOCITIES[q][axis]
            if c == 0:
                continue
            if total is None:
                total = diff if c > 0 else -diff
            else:
                total = total + diff if c > 0 else total - diff
        out.append(total)
    return out, sum(s.values())


def pack_columns(ups, downs, fill, p, acc, lane):
    here = (lane >> 1) == p
    there = (lane >> 1) == p + 32

    def both(k):
        return jnp.where(lane == NL - 1, ups[k], downs[k])

    out = []
    for a, first, second in ((acc[0], both(0), both(1)), (acc[1], both(2), fill), (acc[2], both(3), both(4))):
        a = jnp.where(here, pltpu.roll(first, 2 * p + 1, 1), a)
        out.append(jnp.where(there, pltpu.roll(second, 2 * p + 65, 1), a))
    return tuple(out)


def fluid_kernel(
    pops_in, fill_in, flags_in, energy_in,
    pops_out, fill_out, warm_out, ends_out,
    f0, f1, fz0, fz1, fz2, roll_z, halo_s, columns, g_s, part, eqs, flags, vel, own_e, hot_msg, hbuf, heat_d,
    xs, xr, zs, zr, zd, msg, turned, end_msg,
    load_sem, send_sem, recv_sem, hot_sem, back_sem, out_sem, next_sem,
):
    g, d = lax.axis_index("grp"), lax.axis_index("dev")
    up, down = lax.rem(d + 1, ND), lax.rem(d + ND - 1, ND)
    east, west = lax.rem(g + 1, NG), lax.rem(g + NG - 1, NG)
    lane = lane_iota()
    row = lax.broadcasted_iota(jnp.int32, (NY, NL), 0)
    zero8 = jnp.zeros((NY, NL), F32)

    z, y, core = lax.div(d, 8), lax.rem(lax.div(d, 2), 4), lax.rem(d, 2)
    barrier = pltpu.get_barrier_semaphore()
    x_peers = [(east, d), (west, d)]
    near = [(gg, dd) for dd in (up, down) for gg in (east, west)]
    for dz, dy in FAR_FIRST:
        for dc in range(2):
            if dz or dy or dc:
                to = lax.rem(z + dz, 4) * 8 + lax.rem(y + dy, 4) * 2 + lax.rem(core + dc, 2)
                near.append((g, to))
    near += x_peers
    for to in near:
        pl.semaphore_signal(barrier, inc=1, device_id=to, device_id_type=MESH)

    def load(src, dst, n):
        c = pltpu.make_async_copy(src, dst, load_sem.at[n])
        c.start()
        return c

    def load_pops(q, count, n):
        return load(pops_in.at[pl.ds(q, count)], f0.at[pl.ds(q, count), pl.ds(1, NP)], n)

    fill_load = load(fill_in, fz0.at[1, pl.ds(1, NP), pl.ds(8, 8)], 0)
    cross_loads = [load_pops(11, 8, 1), load_pops(5, 2, 2)]
    more_loads = [load_pops(0, 5, 3), load_pops(7, 4, 4), load(flags_in, flags, 5)]
    energy_load = load(energy_in.at[0], own_e.at[:, pl.ds(NL, ND * NL)], 6)

    def clear(p, c):
        for k in range(3):
            for ref in (fz0, fz1):
                ref[k, p, 0:8] = zero8
                ref[k, p, 16:24] = zero8
        fz2[p, 0:8] = zero8
        fz2[p, 16:24] = zero8
        return c

    lax.fori_loop(0, NP + 2, clear, 0)
    fz2[0, 8:16] = zero8
    fz2[NP + 1, 8:16] = zero8
    own_e[:, 0:NL] = zero8
    own_e[:, (ND + 1) * NL : (ND + 2) * NL] = zero8

    def send(t, src, dst, n, to):
        return pltpu.make_async_remote_copy(
            src_ref=src, dst_ref=dst, send_sem=send_sem.at[t, n], recv_sem=recv_sem.at[t, n],
            device_id=to, device_id_type=MESH,
        )

    def x_sends(t):
        return [
            send(t, xs.at[t, 0], xr.at[t, 0], 0, (east, d)),
            send(t, xs.at[t, 1], xr.at[t, 1], 1, (west, d)),
        ]

    def z_sends(t):
        return [
            send(t, zs.at[t], zr.at[t, side], 2 + side, (g, to))
            for side, to in ((0, up), (1, down))
        ]

    def corner_sends(t):
        return [
            send(t, zs.at[t], zd.at[t, side, k], 4 + 2 * side + k, (gg, to))
            for side, to in ((0, up), (1, down))
            for k, gg in ((0, east), (1, west))
        ]

    def fill_x(t, f, fz):
        for k, q in enumerate(EAST):
            xs[t, 0, k] = f[q, NP]
        xs[t, 0, 5] = fz[1, NP, 8:16]
        for k, q in enumerate(WEST):
            xs[t, 1, k] = f[q, 1]
        xs[t, 1, 5] = fz[1, 1, 8:16]

    def store_z(t, acc):
        for k in range(3):
            zs[t, 8 * k : 8 * k + 8] = acc[k]

    def started(copies):
        for c in copies:
            c.start()
        return copies

    def arrived(copies):
        for c in copies:
            c.wait_recv()

    fill_load.wait()
    for c in cross_loads:
        c.wait()

    def pack0(p, acc):
        return pack_columns(
            [f0[q, p + 1] for q in UP], [f0[q, p + 1] for q in DOWN], fz0[1, p + 1, 8:16], p, acc, lane
        )

    acc0 = (zero8,) * 3
    store_z(0, lax.fori_loop(0, NP, pack0, acc0, unroll=8))

    energy_load.wait()

    def block_of(e):
        return own_e[:, pl.ds(pl.multiple_of((e + 1) * NL, NL), NL)]

    def hot_build(e, c):
        hot_msg[e, 0:8] = block_of(e)
        beside = jnp.where(lane == 0, pltpu.roll(block_of(e - 1), 1, 1), pltpu.roll(block_of(e + 1), NL - 1, 1))
        hot_msg[e, 8:16] = beside
        return c

    lax.fori_loop(0, ND, hot_build, 0, unroll=8)

    pl.semaphore_wait(barrier, len(near))
    for to in x_peers:
        pl.semaphore_signal(next_sem, inc=1, device_id=to, device_id_type=MESH)

    corner0 = started(corner_sends(0))
    z0 = started(z_sends(0))
    for c in more_loads:
        c.wait()
    fill_x(0, f0, fz0)
    x0 = started(x_sends(0))

    def hot_start(i, c):
        to = lax.rem(d + i, ND)
        pltpu.make_async_remote_copy(
            src_ref=hot_msg.at[to], dst_ref=hbuf.at[d + 1],
            send_sem=hot_sem.at[0], recv_sem=hot_sem.at[1], device_id=(g, to), device_id_type=MESH,
        ).start()
        return c

    lax.fori_loop(1, ND, hot_start, 0)
    own = pltpu.make_async_copy(hot_msg.at[d], hbuf.at[d + 1], load_sem.at[0])
    own.start()


    def local_part(f, fz):
        def body(p):
            pops = [f[q, p + 1] for q in range(19)]
            kind = flags[p]
            gas = kind == 0
            fill = fz[1, p + 1, 8:16]
            diffs = {q: pops[q] - pops[q + 1] for q in range(1, 19, 2)}
            sums = {q: pops[q] + pops[q + 1] for q in range(1, 19, 2)}
            (mx, my, mz), total = moments(diffs, sums)
            dens = jnp.where(gas, 1.0, total + pops[0])
            inv = 1.0 / dens
            vx, vy, vz = mx * inv, my * inv, mz * inv
            base = 1.0 - 1.5 * (vx * vx + vy * vy + vz * vz)

            def paired(q):
                cx, cy, cz = VELOCITIES[q]
                along = None
                for c, v in ((cx, vx), (cy, vy), (cz, vz)):
                    if c:
                        along = (v if c > 0 else -v) if along is None else (along + v if c > 0 else along - v)
                return (2.0 * WEIGHTS[q]) * (base + 4.5 * along * along)

            for k, q in enumerate(Z_PAIRS):
                eqs[k, p] = paired(q)
            for k, q in enumerate(CROSS):
                roll_z[k, p + 1] = pltpu.roll(pops[q], 1 if q in UP else NL - 1, 1)
            fz[0, p + 1, 8:16] = pltpu.roll(fill, 1, 1)
            fz[2, p + 1, 8:16] = pltpu.roll(fill, NL - 1, 1)
            ex = None
            got = {0: pops[0]}
            for q in FLAT:
                cx, cy, _ = VELOCITIES[q]
                incoming = shift_rows(f[q, p + 1 - cx], cy)
                beside = fz[1, p + 1 - cx, 8 - cy : 16 - cy]
                empty = beside == 0.0
                back = pops[opposite(q)]
                got[q] = jnp.where(empty, paired(q if q % 2 else q - 1) - back, incoming)
                term = jnp.where(empty, 0.0, (fill + beside) * (incoming - back))
                ex = term if ex is None else ex + term
                g_s[q, p] = got[q]
            diffs = {q: got[q] - got[q + 1] for q in FLAT if q % 2}
            sums = {q: got[q] + got[q + 1] for q in FLAT if q % 2}
            (mx, my, _), total = moments(diffs, sums)
            part[0, p] = total + got[0]
            part[1, p] = mx
            part[2, p] = my
            part[3, p] = fill * dens + 0.5 * ex

        return body

    def local_inner(f, fz):
        body = local_part(f, fz)

        def inner(p, c):
            body(p)
            return c

        lax.fori_loop(1, NP - 1, inner, 0, unroll=6)

    def local_outer(t, f, fz):
        for k, q in enumerate(EAST):
            f[q, 0] = xr[t, 0, k]
        for k, q in enumerate(WEST):
            f[q, NP + 1] = xr[t, 1, k]
        fz[1, 0, 8:16] = jnp.where(g > 0, xr[t, 0, 5], 0.0)
        fz[1, NP + 1, 8:16] = jnp.where(g < NG - 1, xr[t, 1, 5], 0.0)
        for q in (11, 13):
            roll_z[CROSS.index(q), 0] = pltpu.roll(f[q, 0], 1 if q in UP else NL - 1, 1)
        for q in (12, 14):
            roll_z[CROSS.index(q), NP + 1] = pltpu.roll(f[q, NP + 1], 1 if q in UP else NL - 1, 1)
        body = local_part(f, fz)

        def outer(i, c):
            body(i * (NP - 1))
            return c

        lax.fori_loop(0, 2, outer, 0, unroll=2)

    def cross_part(f, fz, fill_ref, p):
        kind = flags[p]
        gas = kind == 0
        fill = fz[1, p + 1, 8:16]
        got = {}
        ex = None
        for side, dirs in enumerate((UP, DOWN)):
            edge = 0 if side == 0 else NL - 1
            for q in dirs:
                cx, cy, cz = VELOCITIES[q]
                k = CROSS.index(q)
                incoming = jnp.where(lane == edge, halo_s[k % 5, p], roll_z[k, p + 1 - cx])
                incoming = shift_rows(incoming, cy)
                beside = fz[1 - cz, p + 1 - cx, 8 - cy : 16 - cy]
                empty = beside == 0.0
                back = f[opposite(q), p + 1]
                pair = q if q % 2 else q - 1
                got[q] = jnp.where(empty, eqs[Z_PAIRS.index(pair), p] - back, incoming)
                term = jnp.where(empty, 0.0, (fill + beside) * (incoming - back))
                ex = term if ex is None else ex + term
                g_s[q, p] = got[q]
        diffs = {q: got[q] - got[q + 1] for q in Z_PAIRS}
        sums = {q: got[q] + got[q + 1] for q in Z_PAIRS}
        (mx, my, mz), total = moments(diffs, sums)
        dens = jnp.where(gas, 1.0, total + part[0, p])
        inv = 1.0 / dens
        vel[0, p] = dens
        vel[1, p] = (mx + part[1, p]) * inv
        vel[2, p] = (my + part[2, p]) * inv
        vel[3, p] = mz * inv
        mass = part[3, p] + 0.5 * ex
        fill_ref[p + 1, 8:16] = jnp.where(
            kind == 2, 1.0, jnp.where(gas, 0.0, jnp.clip(mass * inv, 0.01, 1.0))
        )

    def cross(t, f, fz, fill_ref, corner):
        odd = (lane & 1) == 1
        inside = jnp.logical_or(jnp.logical_and(odd, d > 0), jnp.logical_and(jnp.logical_not(odd), d < ND - 1))

        def turned(low, high, k):
            rows = slice(8 * (k // 2), 8 * (k // 2) + 8)
            by = 64 * (k % 2)
            return jnp.where(odd, pltpu.roll(low[rows], by + 1, 1), pltpu.roll(high[rows], (by + NL - 1) % NL, 1))

        main = (zr.at[t, 0], zr.at[t, 1])
        for k, half in enumerate((0, 1, 2, 4, 5)):
            columns[k] = turned(*main, half)
        columns[5] = jnp.where(inside, turned(*main, 3), 0.0)

        def to_edges(k, p):
            return pltpu.roll(columns[k], lax.rem(2 * NL - 1 - 2 * p, NL), 1)

        def halos(p):
            for k in range(5):
                halo_s[k, p] = to_edges(k, p - VELOCITIES[UP[k]][0])

        def fill_columns(p):
            new = to_edges(5, p)
            for edge, k in ((0, 0), (NL - 1, 2)):
                fz[k, p + 1, 8:16] = jnp.where(lane == edge, new, fz[k, p + 1, 8:16])

        def prepare(base):
            for j in range(4):
                halos(base + j)
                fill_columns(base + j + 1)

        def work(base):
            for j in range(4):
                cross_part(f, fz, fill_ref, base + j)

        fill_columns(3)
        fill_columns(4)
        prepare(4)

        def mid(i, c):
            for base in (8 * i + 4, 8 * i + 8):
                work(base)
                prepare(base + 4)
            return c

        lax.fori_loop(0, NP // 8 - 1, mid, 0)

        arrived(corner)
        west_lanes, east_lanes = lane >= NL - 2, (lane >> 1) == 32
        last_of = (zd.at[t, 0, 0], zd.at[t, 1, 0])
        first_of = (zd.at[t, 0, 1], zd.at[t, 1, 1])
        columns[3] = jnp.where(west_lanes, pltpu.roll(turned(*last_of, 4), 64, 1), columns[3])
        columns[4] = jnp.where(east_lanes, pltpu.roll(turned(*first_of, 5), 64, 1), columns[4])
        fills = columns[5]
        ghost = jnp.where(jnp.logical_and(inside, g > 0), pltpu.roll(turned(*last_of, 3), 64, 1), 0.0)
        fills = jnp.where(west_lanes, ghost, fills)
        ghost = jnp.where(jnp.logical_and(inside, g < NG - 1), pltpu.roll(turned(*first_of, 3), 64, 1), 0.0)
        columns[5] = jnp.where(east_lanes, ghost, fills)
        for at in (0, NP + 1):
            fz[0, at, 8:16] = pltpu.roll(fz[1, at, 8:16], 1, 1)
            fz[2, at, 8:16] = pltpu.roll(fz[1, at, 8:16], NL - 1, 1)
        fill_columns(-1)
        fill_columns(NP)
        for j in range(4):
            halos(j)
            halos(NP - 4 + j)
        for j in range(3):
            fill_columns(j)

        def last(i, c):
            work(i * (NP - 4))
            return c

        lax.fori_loop(0, 2, last, 0)

    def collide(f, p, pairs=range(1, 19, 2), rest=True):
        gas = flags[p] == 0
        vx, vy, wz = vel[1, p], vel[2, p], vel[3, p] + RELAX_TIME * GRAVITY
        base = 1.0 - 1.5 * (vx * vx + vy * vy + wz * wz)
        keep = jnp.where(gas, 0.0, 1.0 - 1.0 / RELAX_TIME)
        scale = jnp.where(gas, 0.0, vel[0, p] * (1.0 / RELAX_TIME))
        new = {0: keep * f[0, p + 1] + (WEIGHTS[0] * scale) * base} if rest else {}
        by_weight = {w: (w * scale, 3.0 * w * scale) for w in (WEIGHTS[1], WEIGHTS[7])}
        for q in pairs:
            along = None
            for c, v in zip(VELOCITIES[q], (vx, vy, wz)):
                if c:
                    along = (v if c > 0 else -v) if along is None else (along + v if c > 0 else along - v)
            even_w, odd_w = by_weight[WEIGHTS[q]]
            even = even_w * (base + 4.5 * along * along)
            odd = odd_w * along
            new[q] = keep * g_s[q, p] + (even + odd)
            new[q + 1] = keep * g_s[q + 1, p] + (even - odd)
        return new

    local_inner(f0, fz0)

    pl.semaphore_wait(next_sem, len(x_peers))

    def beyond(i, gg, at, sem):
        to = lax.rem(d + i, ND)
        return pltpu.make_async_remote_copy(
            src_ref=hot_msg.at[to, pl.ds(0, 8)], dst_ref=hbuf.at[at, pl.ds(0, 8)],
            send_sem=hot_sem.at[4], recv_sem=hot_sem.at[sem], device_id=(gg, to), device_id_type=MESH,
        )

    def beyond_all(gg, at, sem):
        def one(i, c):
            beyond(i, gg, at, sem).start()
            return c

        lax.fori_loop(0, ND, one, 0)

    @pl.when(d == ND - 1)
    def _():
        beyond_all(east, 0, 2)

    @pl.when(d == 0)
    def _():
        beyond_all(west, NP + 1, 3)

    arrived(x0)
    local_outer(0, f0, fz0)
    arrived(z0)
    cross(0, f0, fz0, fz1.at[1], corner0)

    def first(p, acc):
        new = collide(f0, p, Z_PAIRS, False)
        for q in new:
            f1[q, p + 1] = new[q]
        return pack_columns([new[q] for q in UP], [new[q] for q in DOWN], fz1[1, p + 1, 8:16], p, acc, lane)

    def first_flat(p, c):
        new = collide(f0, p, (1, 3, 7, 9))
        for q in new:
            f1[q, p + 1] = new[q]
        return c

    store_z(1, lax.fori_loop(0, NP, first, acc0, unroll=8))
    corner1 = started(corner_sends(1))
    z1 = started(z_sends(1))
    lax.fori_loop(0, NP, first_flat, 0, unroll=4)
    fill_x(1, f1, fz1)
    x1 = started(x_sends(1))

    local_inner(f1, fz1)

    own.wait()
    pltpu.make_async_copy(hot_msg.at[pl.ds(0, ND - 1)], hot_msg.at[pl.ds(0, ND - 1)], hot_sem.at[1]).wait()
    beyond(0, east, 0, 2).wait_recv()
    beyond(0, west, NP + 1, 3).wait_recv()
    hbuf[0, 0:8] = jnp.where(g > 0, hbuf[0, 0:8], 0.0)
    hbuf[NP + 1, 0:8] = jnp.where(g < NG - 1, hbuf[NP + 1, 0:8], 0.0)

    def temp(h):
        return jnp.minimum(h, 1.0) + jnp.maximum(h - 1.5, 0.0)

    def differences(p, c):
        h = hbuf[p + 1, 0:8]
        edges = hbuf[p + 1, 8:16]
        others = (
            hbuf[p, 0:8], hbuf[p + 2, 0:8],
            jnp.where(row == 0, 0.0, pltpu.roll(h, 1, 0)), jnp.where(row == NY - 1, 0.0, pltpu.roll(h, NY - 1, 0)),
            jnp.where(lane == 0, edges, pltpu.roll(h, 1, 1)), jnp.where(lane == NL - 1, edges, pltpu.roll(h, NL - 1, 1)),
        )
        mine = temp(h)
        total = None
        for k, other in enumerate(others):
            dt = temp(other) - mine
            total = dt if total is None else total + dt
            heat_d[k, p] = dt * (0.05 * STEP_TIME)
            heat_d[6 + k, p] = (other - h) * STEP_TIME
        heat_d[12, p] = total * STEP_TIME
        return c

    lax.fori_loop(0, NP, differences, 0, unroll=8)

    arrived(x1)
    local_outer(1, f1, fz1)
    arrived(z1)
    cross(1, f1, fz1, fz2, corner1)

    end_msg[0] = -fz2[NP, 8:16] * heat_d[1, NP - 1]
    end_msg[1] = -fz2[1, 8:16] * heat_d[0, 0]
    end_sends = [
        pltpu.make_async_remote_copy(
            src_ref=end_msg.at[k], dst_ref=ends_out.at[k, d],
            send_sem=back_sem.at[2 + k], recv_sem=back_sem.at[4 + k], device_id=to, device_id_type=MESH,
        )
        for k, to in ((0, (east, 0)), (1, (west, ND - 1)))
    ]
    for c in end_sends:
        c.start()

    def edge_fill(p, acc):
        return jnp.where((lane >> 1) == p, pltpu.roll(fz2[p + 1, 8:16], 2 * p + 1, 1), acc)

    edges = lax.fori_loop(0, NP, edge_fill, zero8, unroll=16)
    turned[...] = jnp.concatenate([edges] * (NL // NY), axis=0).T

    def transport(p, c):
        fill = fz2[p + 1, 8:16]
        beside = (
            fz2[p, 8:16], fz2[p + 2, 8:16], fz2[p + 1, 7:15], fz2[p + 1, 9:17],
            jnp.where(lane == 0, 0.0, pltpu.roll(fill, 1, 1)),
            jnp.where(lane == NL - 1, 0.0, pltpu.roll(fill, NL - 1, 1)),
        )
        out = hbuf[p + 1, 0:8] + (0.02 + 0.05 * fill) * heat_d[12, p]
        for k in range(6):
            out = out + beside[k] * heat_d[k, p]
        for a in range(3):
            v = vel[1 + a, p]
            out = out + jnp.maximum(v, 0.0) * heat_d[6 + 2 * a, p] - jnp.minimum(v, 0.0) * heat_d[7 + 2 * a, p]
        msg[p, 0:8] = out
        msg[p, 8:10] = turned[pl.ds(2 * p, 2)]
        return c

    for dz in (2, 1, 3, 0):
        z_to = lax.rem(z + dz, 4)
        for j in range(8):
            transport(8 * z_to + j, 0)
        for dy, dc in ((2, 0), (2, 1), (1, 0), (1, 1), (3, 0), (3, 1), (0, 1), (0, 0)):
            if dz or dy or dc:
                p = 8 * z_to + lax.rem(y + dy, 4) * 2 + lax.rem(core + dc, 2)
                pltpu.make_async_remote_copy(
                    src_ref=msg.at[p, pl.ds(0, 10)], dst_ref=warm_out.at[d, pl.ds(0, 10)],
                    send_sem=back_sem.at[0], recv_sem=back_sem.at[1], device_id=(g, p), device_id_type=MESH,
                ).start()
    keep = pltpu.make_async_copy(msg.at[d, pl.ds(0, 10)], warm_out.at[d, pl.ds(0, 10)], load_sem.at[0])
    keep.start()
    fill_copy = pltpu.make_async_copy(fz2.at[pl.ds(1, NP), pl.ds(8, 8)], fill_out, out_sem.at[0])
    fill_copy.start()

    def second(p, c):
        new = collide(f1, p)
        for q in range(19):
            f0[q, p + 1] = new[q]
        return c

    pops_copies = []
    for base in range(0, NP, 8):
        lax.fori_loop(base, base + 8, second, 0, unroll=4)
        pops_copies.append(
            pltpu.make_async_copy(
                f0.at[:, pl.ds(1 + base, 8)], pops_out.at[:, pl.ds(base, 8)], out_sem.at[1 + base // 8]
            )
        )
        pops_copies[-1].start()

    for c in corner0 + z0 + x0 + corner1 + z1 + x1 + end_sends:
        c.wait_send()

    def all_of(ref, count, sem):
        part_of = ref.at[pl.ds(0, count)]
        pltpu.make_async_copy(part_of, part_of, sem).wait()

    all_of(hot_msg, ND - 1, hot_sem.at[0])

    @pl.when(d == 0)
    def _():
        all_of(hot_msg, ND // 2, hot_sem.at[4])

    @pl.when(d == ND - 1)
    def _():
        all_of(hot_msg, ND // 2, hot_sem.at[4])

    keep.wait()
    fill_copy.wait()
    for c in pops_copies:
        c.wait()
    sent = msg.at[pl.ds(0, ND - 1), pl.ds(0, 10)]
    for n in range(2):
        pltpu.make_async_copy(sent, sent, back_sem.at[n]).wait()

    @pl.when(d == 0)
    def _():
        all_of(msg, ND // 2, back_sem.at[4])

    @pl.when(d == ND - 1)
    def _():
        all_of(msg, ND // 2, back_sem.at[5])


def finish_kernel(
    pops_mid, fill_mid, warm_mid, ends_mid, energy_in, pops_out, fill_out, energy_out, got, ends, own, done, rows, sem
):
    g, d = lax.axis_index("grp"), lax.axis_index("dev")
    copies = [
        pltpu.make_async_copy(pops_mid, pops_out, sem.at[0]),
        pltpu.make_async_copy(warm_mid, got, sem.at[1]),
        pltpu.make_async_copy(energy_in, own, sem.at[2]),
        pltpu.make_async_copy(ends_mid, ends, sem.at[3]),
        pltpu.make_async_copy(fill_mid, fill_out, sem.at[4]),
    ]
    for c in copies:
        c.start()
    for c in copies[1:4]:
        c.wait()
    lane = lane_iota()
    low = jnp.logical_and(d == 0, g > 0)
    high = jnp.logical_and(d == ND - 1, g < NG - 1)

    def temp(h):
        return jnp.minimum(h, 1.0) + jnp.maximum(h - 1.5, 0.0)

    rows[...] = jnp.zeros((NL, NL), F32)
    for e in range(ND):
        rows[2 * e : 2 * e + 2] = got[e, 8:10]
    edges = rows[...].T[0:NY]
    halves = []
    for e in range(ND):
        cells = slice(e * NL, (e + 1) * NL)
        out = got[e, 0:8] + jnp.where(low, ends[0, e], 0.0) + jnp.where(high, ends[1, e], 0.0)
        warmth = temp(own[0, :, cells])
        for side, other in ((0, e - 1), (1, e + 1)):
            if other < 0 or other >= ND:
                continue
            by, edge = (1, 0) if side == 0 else (NL - 1, NL - 1)
            beyond = temp(own[0, :, other * NL : (other + 1) * NL])
            at = 2 * other + side
            term = pltpu.roll(edges, (edge - at) % NL, 1) * (pltpu.roll(beyond, by, 1) - warmth)
            out = out + jnp.where(lane == edge, (0.05 * STEP_TIME) * term, 0.0)
        done[0, :, cells] = out
        if e % (ND // 2) == ND // 2 - 1:
            half = pl.ds((e // (ND // 2)) * (ND // 2) * NL, ND // 2 * NL)
            halves.append(
                pltpu.make_async_copy(done.at[:, :, half], energy_out.at[:, :, half], sem.at[1 + len(halves)])
            )
            halves[-1].start()
    for c in halves:
        c.wait()
    copies[4].wait()
    copies[0].wait()


def shards(populations, fill, flags, specific_energy_grid):
    plane = (NY, NL)
    any_spec = pl.BlockSpec(memory_space=pl.ANY)
    hbm_spec = pl.BlockSpec(memory_space=pltpu.HBM)
    given = [
        pltpu.with_memory_space_constraint(x, pltpu.HBM)
        for x in (populations, fill, flags, specific_energy_grid)
    ]
    pops_mid, fill_mid, warm_mid, ends_mid = pl.pallas_call(
        fluid_kernel,
        out_shape=(
            jax.ShapeDtypeStruct((19, NP) + plane, F32),
            jax.ShapeDtypeStruct((NP,) + plane, F32),
            jax.ShapeDtypeStruct((ND, 16, NL), F32),
            jax.ShapeDtypeStruct((2, ND) + plane, F32),
        ),
        in_specs=[hbm_spec] * 4,
        out_specs=(any_spec,) * 4,
        scratch_shapes=[
            pltpu.VMEM((19, NP + 2) + plane, F32),
            pltpu.VMEM((19, NP + 2) + plane, F32),
            pltpu.VMEM((3, NP + 2, 24, NL), F32),
            pltpu.VMEM((3, NP + 2, 24, NL), F32),
            pltpu.VMEM((NP + 2, 24, NL), F32),
            pltpu.VMEM((10, NP + 2) + plane, F32),
            pltpu.VMEM((5, NP) + plane, F32),
            pltpu.VMEM((6,) + plane, F32),
            pltpu.VMEM((19, NP) + plane, F32),
            pltpu.VMEM((4, NP) + plane, F32),
            pltpu.VMEM((5, NP) + plane, F32),
            pltpu.VMEM((NP,) + plane, jnp.int32),
            pltpu.VMEM((4, NP) + plane, F32),
            pltpu.VMEM((NY, (ND + 2) * NL), F32),
            pltpu.VMEM((ND, 16, NL), F32),
            pltpu.VMEM((NP + 2, 16, NL), F32),
            pltpu.VMEM((13, NP) + plane, F32),
            pltpu.VMEM((2, 2, 6) + plane, F32),
            pltpu.VMEM((2, 2, 6) + plane, F32),
            pltpu.VMEM((2, 24, NL), F32),
            pltpu.VMEM((2, 2, 24, NL), F32),
            pltpu.VMEM((2, 2, 2, 24, NL), F32),
            pltpu.VMEM((ND, 16, NL), F32),
            pltpu.VMEM((NL, NL), F32),
            pltpu.VMEM((2,) + plane, F32),
            pltpu.SemaphoreType.DMA((7,)),
            pltpu.SemaphoreType.DMA((2, 8)),
            pltpu.SemaphoreType.DMA((2, 8)),
            pltpu.SemaphoreType.DMA((5,)),
            pltpu.SemaphoreType.DMA((6,)),
            pltpu.SemaphoreType.DMA((5,)),
            pltpu.SemaphoreType.REGULAR,
        ],
        compiler_params=pltpu.CompilerParams(
            collective_id=0, has_side_effects=True, vmem_limit_bytes=40 * 1024 * 1024
        ),
        name="pour",
    )(*given)
    return pl.pallas_call(
        finish_kernel,
        out_shape=(
            jax.ShapeDtypeStruct((19, NP) + plane, F32),
            jax.ShapeDtypeStruct((NP,) + plane, F32),
            jax.ShapeDtypeStruct((1, NY, ND * NL), F32),
        ),
        in_specs=[any_spec] * 5,
        out_specs=(any_spec,) * 3,
        scratch_shapes=[
            pltpu.VMEM((ND, 16, NL), F32),
            pltpu.VMEM((2, ND) + plane, F32),
            pltpu.VMEM((1, NY, ND * NL), F32),
            pltpu.VMEM((1, NY, ND * NL), F32),
            pltpu.VMEM((NL, NL), F32),
            pltpu.SemaphoreType.DMA((5,)),
        ],
        compiler_params=pltpu.CompilerParams(vmem_limit_bytes=8 * 1024 * 1024),
        name="finish",
    )(pops_mid, fill_mid, warm_mid, ends_mid, given[3])


def solution(mesh):
    in_specs = (
        P(None, "grp", None, "dev"),
        P("grp", None, "dev"),
        P("grp", None, "dev"),
        P(("grp", "dev"), None, None),
    )
    out_specs = (P(None, "grp", None, "dev"), P("grp", None, "dev"), P(("grp", "dev"), None, None))
    return jax.shard_map(shards, mesh=mesh, in_specs=in_specs, out_specs=out_specs, check_vma=False)
```
